128 devices in a mesh: queue: 64 (over z_hi, x, y, core), head: 2 (over z_lo).
Axes of the slice: x: 4, y: 4, z: 4 (z_hi: 2, z_lo: 2; z = z_hi * 2 + z_lo), core: 2. Of those that a mesh axis runs over, the one named last changes fastest.
Arguments:
- hidden: bfloat16 [256, 2, 512, 1152], P('queue', None, None, 'head'), may hold values from -6 to 6
- keypoints: int32 [256, 512], P('queue'), may hold values from 0 to 18
- tsteps: int32 [64], P('queue'), may hold values from 0 to 63
- mod_table: float32 [64, 3, 1152], replicated, may hold values from -3 to 3
- ctrl_table: bfloat16 [19, 1152], replicated, may hold values from -6 to 6
- ctrl_proj: bfloat16 [1152, 1152], P(None, 'head'), may hold values from -0.1875 to 0.1875
- w_qkv: bfloat16 [1152, 3, 1152], P(None, None, 'head'), may hold values from -0.1875 to 0.1875
- q_gain: float32 [16, 72], P('head'), may hold values from 0.5 to 6, as said below
- k_gain: float32 [16, 72], P('head'), may hold values from 0.5 to 6, as said below
- w_out: bfloat16 [1152, 1152], P('head'), may hold values from -0.1875 to 0.1875
Outputs:
- block_out: bfloat16 [256, 2, 512, 1152], P('queue', None, None, 'head')
The draws below stay inside these ranges and needn't reach their ends.
Inputs may be any that keep to these rules, and one draw needn't show every extreme that they name: `q_gain`: positive gains. `k_gain`: positive gains.
All inputs are finite; a program needn't handle non-finite values.
Results may differ from the reference program's by a relative error of at most 0.014.
Values may be sent and summed in bfloat16 or wider, within the bound.
No kernel may reach another device: no remote copies, remote signals or barrier semaphores. Data moves between devices by JAX's collectives and lax.ppermute only.
A program may use at most 320 MiB of HBM per device.

```python
import math
import jax
import jax.numpy as jnp
from jax import lax

D = 1152
HEADS = 16
HEAD_DIM = 72
F = 4
P_SIZE = 512
WIN = 4
STEPS = 64
KP = 19
GROUPS = 64
FRAMES = 256


def draw_q_gain(key, part):
    key = jax.random.fold_in(key, 11)
    lowest, highest = (0.5, 2.0)
    fraction = jax.random.uniform(key, (HEADS, HEAD_DIM), jnp.float32)
    return jnp.exp(math.log(lowest) + fraction * (math.log(highest) - math.log(lowest)))


def draw_k_gain(key, part):
    key = jax.random.fold_in(key, 23)
    lowest, highest = (0.5, 2.0)
    fraction = jax.random.uniform(key, (HEADS, HEAD_DIM), jnp.float32)
    return jnp.exp(math.log(lowest) + fraction * (math.log(highest) - math.log(lowest)))


def with_ends(values, own_key, least, high):
    index_at = [jax.random.randint(jax.random.fold_in(own_key, axis), (), 0, length) for axis, length in enumerate(values.shape)]
    main_axis = values.shape.index(max(values.shape))
    next_to = index_at[:main_axis] + [(index_at[main_axis] + 1) % values.shape[main_axis]] + index_at[main_axis + 1:]
    return values.at[tuple(index_at)].set(least).at[tuple(next_to)].set(high)


def block_scale(stream_key, shape, cuts, least, high):
    level, own = 1.0, jax.random.fold_in(stream_key, 6)
    for axis_at, blocks in cuts:
        heights = jnp.exp(jax.random.uniform(jax.random.fold_in(own, axis_at), (blocks,), jnp.float32, least / len(cuts), high / len(cuts)))
        level = level * jnp.repeat(heights, shape[axis_at] // blocks).reshape([-1 if axis == axis_at else 1 for axis in range(len(shape))])
    return level


def gaussian(key, extent, deviation, bound, pieces=(), held_as=jnp.bfloat16):
    level = block_scale(key, extent, pieces, -0.22, 0.18) if pieces else 1.0
    array = jax.random.normal(key, extent, jnp.float32) * deviation * level
    return jnp.minimum(jnp.maximum(array, -bound), bound).astype(held_as)


def setup_inputs(seed: int = 0) -> dict:
    key_list = jax.random.split(jax.random.key(seed), 11)
    hidden = gaussian(key_list[0], (FRAMES, 2, P_SIZE, D), 1.0, 6.0, ((0, 64), (3, 2)))
    keypoints = with_ends(jax.random.randint(key_list[1], (FRAMES, P_SIZE), 0, KP), jax.random.fold_in(key_list[1], 1), 0, KP - 1).astype(jnp.int32)
    tsteps = with_ends(jax.random.randint(key_list[2], (GROUPS,), 0, STEPS), jax.random.fold_in(key_list[2], 1), 0, STEPS - 1).astype(jnp.int32)
    mod_table = gaussian(key_list[3], (STEPS, 3, D), 0.5, 3.0, (), jnp.float32)
    ctrl_table = gaussian(key_list[4], (KP, D), 1.0, 6.0)
    ctrl_proj = gaussian(key_list[5], (D, D), D ** -0.5, 0.1875, ((1, 2),))
    w_qkv = gaussian(key_list[6], (D, 3, HEADS * HEAD_DIM), D ** -0.5, 0.1875, ((2, 2),))
    q_gain = draw_q_gain(jax.random.fold_in(key_list[10], 71), 0)
    k_gain = draw_k_gain(jax.random.fold_in(key_list[10], 71), 0)
    w_out = gaussian(key_list[9], (HEADS * HEAD_DIM, D), (HEADS * HEAD_DIM) ** -0.5, 0.1875, ((0, 2),))
    return {"hidden": hidden, "keypoints": keypoints, "tsteps": tsteps, "mod_table": mod_table, "ctrl_table": ctrl_table, "ctrl_proj": ctrl_proj, "w_qkv": w_qkv, "q_gain": q_gain, "k_gain": k_gain, "w_out": w_out}


EPSILON = 1e-06

def query_norm(vector, scale_gain):
    return vector * lax.rsqrt(lax.optimization_barrier(jnp.mean(vector * vector, -1, keepdims=True)) + EPSILON) * scale_gain

def adaptive_norm(mixed, modulate):
    floated = mixed.astype(jnp.float32)
    centre = lax.optimization_barrier(jnp.mean(floated, -1, keepdims=True))
    spread = lax.optimization_barrier(jnp.mean(jnp.square(floated - centre), -1, keepdims=True))
    return ((floated - centre) * lax.rsqrt(spread + EPSILON) * (1.0 + modulate[1]) + modulate[0]).astype(jnp.bfloat16)

def window_attend(queries, key_ext, value_ext, start_frame, frame_count, reach_frames):
    frames = queries.shape[0]
    head_dim = queries.shape[-1]
    offsets = 2 * reach_frames + 1
    floated = queries.astype(jnp.float32)
    scores = jnp.stack([lax.optimization_barrier(jnp.sum(floated * key_ext[offset:offset + frames].astype(jnp.float32), -1)) for offset in range(offsets)], -1) / math.sqrt(head_dim)
    positions = start_frame + jnp.arange(frames)[:, None] + jnp.arange(offsets)[None, :]
    usable = (positions >= 0) & (positions < frame_count)
    scores = jnp.where(usable[:, None, None, None, :], scores, -1e+30)
    highest = lax.optimization_barrier(jnp.max(scores, -1, keepdims=True))
    raised = jnp.exp(scores - highest)
    weights = (raised / lax.optimization_barrier(jnp.sum(raised, -1, keepdims=True))).astype(jnp.bfloat16)
    total_out = weights[..., 0, None].astype(jnp.float32) * value_ext[0:frames].astype(jnp.float32)
    for offset in range(1, offsets):
        total_out = total_out + weights[..., offset, None].astype(jnp.float32) * value_ext[offset:offset + frames].astype(jnp.float32)
    return total_out.astype(jnp.bfloat16)

def reference(hidden, keypoints, tsteps, mod_table, ctrl_table, ctrl_proj, w_qkv, q_gain, k_gain, w_out):
    groups = tsteps.shape[0]
    frame_mod = mod_table[tsteps]

    def prepare(bundle):
        hidden_group, key_points, modulate = bundle
        embedded = ctrl_table[key_points]
        control = jnp.dot(embedded.reshape(-1, D), ctrl_proj, preferred_element_type=jnp.float32).reshape(F, P_SIZE, D)
        cond_rows = (hidden_group[:, 0].astype(jnp.float32) + control).astype(jnp.bfloat16)
        mixed = jnp.stack([cond_rows, hidden_group[:, 1]], 1)
        normed = adaptive_norm(mixed, modulate)
        projected = jnp.dot(normed.reshape(-1, D), w_qkv.reshape(D, 3 * HEADS * HEAD_DIM), preferred_element_type=jnp.float32)
        projected = projected.reshape(F, 2, P_SIZE, 3, HEADS, HEAD_DIM)
        queries = query_norm(projected[:, :, :, 0], q_gain).astype(jnp.bfloat16)
        key_rows = query_norm(projected[:, :, :, 1], k_gain).astype(jnp.bfloat16)
        value_rows = projected[:, :, :, 2].astype(jnp.bfloat16)
        return (mixed, queries, key_rows, value_rows)
    mixed, queries, key_rows, value_rows = lax.map(prepare, (hidden.reshape(groups, F, 2, P_SIZE, D), keypoints.reshape(groups, F, P_SIZE), frame_mod))
    padding = ((WIN, WIN), (0, 0), (0, 0), (0, 0), (0, 0))
    key_pad = jnp.pad(key_rows.reshape((groups * F,) + key_rows.shape[2:]), padding)
    value_pad = jnp.pad(value_rows.reshape((groups * F,) + value_rows.shape[2:]), padding)

    def finish(bundle):
        group_index, mixed_group, queries_group, modulate = bundle
        start = group_index * F
        key_ext = lax.dynamic_slice_in_dim(key_pad, start, F + 2 * WIN, 0)
        value_ext = lax.dynamic_slice_in_dim(value_pad, start, F + 2 * WIN, 0)
        attended = window_attend(queries_group, key_ext, value_ext, start - WIN, groups * F, WIN)
        attended = attended.reshape(F * 2 * P_SIZE, HEADS * HEAD_DIM)
        mixed_out = jnp.dot(attended, w_out, preferred_element_type=jnp.float32).reshape(F, 2, P_SIZE, D)
        return (mixed_group.astype(jnp.float32) + modulate[2] * mixed_out).astype(jnp.bfloat16)
    block_out = lax.map(finish, (jnp.arange(groups, dtype=jnp.int32), mixed, queries, frame_mod))
    return block_out.reshape(groups * F, 2, P_SIZE, D)
```

```python
import functools
import math

import jax
import jax.numpy as jnp
from jax import lax
from jax.experimental import pallas as pl
from jax.experimental.pallas import tpu as pltpu
from jax.sharding import PartitionSpec as P

WIN = 4
EPSILON = 1e-06
CHUNKS = 4
LANES = 128
VMEM = 60 << 20
F32, BF16 = jnp.float32, jnp.bfloat16


def split_dot(values, ones2):
    high = values.astype(BF16)
    low = (values - high.astype(F32)).astype(BF16)
    return jnp.dot(
        jnp.concatenate([high, low], -1), ones2, preferred_element_type=F32
    )


def classes_kernel(control, table):
    values = control[...]
    high = values.astype(BF16)
    rest = values - high.astype(F32)
    middle = rest.astype(BF16)
    low = (rest - middle.astype(F32)).astype(BF16)
    table[...] = jnp.concatenate([high, middle, low, jnp.zeros_like(low)], -1)


def class_table(control):
    return pl.pallas_call(
        classes_kernel,
        out_shape=jax.ShapeDtypeStruct((control.shape[0], LANES), BF16),
        compiler_params=pltpu.CompilerParams(vmem_limit_bytes=VMEM),
        name="class_table",
    )(control)


def norm_kernel(place, hidden, other, keypoints, table, mod, normed, mixed, values):
    half, size = hidden.shape[-2:]
    own_at = pl.multiple_of(place[0] * half, 64)
    other_at = pl.multiple_of((1 - place[0]) * half, 64)
    values[pl.ds(own_at, half), :] = hidden[0, 0].astype(F32)
    values[pl.ds(other_at, half), :] = other[0].astype(F32)
    points = keypoints[pl.ds(pl.program_id(0), 1), :]
    lane = lax.broadcasted_iota(jnp.int32, (LANES, size), 0)
    picks = ((lane % 32 == points) & (lane < 96) & (place[0] == 0)).astype(F32).astype(BF16)
    control = jnp.dot(table[...], picks, preferred_element_type=F32)
    rounded = (values[...] + control).astype(BF16)
    mixed[0] = rounded
    floated = rounded.astype(F32)
    centre = jnp.mean(floated, 0, keepdims=True)
    floated = floated - centre
    factor = lax.rsqrt(jnp.mean(floated * floated, 0, keepdims=True) + EPSILON)
    result = floated * factor * (1.0 + mod[:, 1:2]) + mod[:, 0:1]
    normed[0] = result.T.astype(BF16)


def adaptive_norm(place, hidden, other, keypoints, table, mod, chunk):
    frames, _, half, places = hidden.shape
    size = places // CHUNKS
    width = 2 * half
    grid_spec = pltpu.PrefetchScalarGridSpec(
        num_scalar_prefetch=1,
        grid=(frames,),
        in_specs=[
            pl.BlockSpec((1, 1, half, size), lambda f, s: (f, s[0], 0, chunk)),
            pl.BlockSpec((1, half, size), lambda f, s: (f, 0, 0)),
            pl.BlockSpec((frames, size), lambda f, s: (0, chunk)),
            pl.BlockSpec((width, LANES), lambda f, s: (0, 0)),
            pl.BlockSpec((width, 3), lambda f, s: (0, 0)),
        ],
        out_specs=[
            pl.BlockSpec((1, size, width), lambda f, s: (f + s[1] * (3 - 2 * f), 0, 0)),
            pl.BlockSpec((1, width, size), lambda f, s: (f + s[1] * (3 - 2 * f), 0, 0)),
        ],
        scratch_shapes=[pltpu.VMEM((width, size), F32)],
    )
    return pl.pallas_call(
        norm_kernel,
        grid_spec=grid_spec,
        out_shape=[
            jax.ShapeDtypeStruct((frames, size, width), BF16),
            jax.ShapeDtypeStruct((frames, width, size), BF16),
        ],
        compiler_params=pltpu.CompilerParams(vmem_limit_bytes=VMEM),
        cost_estimate=pl.CostEstimate(
            flops=frames * size * width * 300, bytes_accessed=6 * frames * size * width,
            transcendentals=0,
        ),
        name="adaptive_norm",
    )(place, hidden, other, keypoints, table, mod)


def order_kernel(head_dim, place, weight, ordered, piece):
    half = weight.shape[-2]
    heads = half // head_dim
    target = lax.broadcasted_iota(jnp.int32, (half, half), 0)
    source = lax.broadcasted_iota(jnp.int32, (half, half), 1)
    mover = (source == (target % heads) * head_dim + target // heads).astype(F32).astype(BF16)
    ordered[...] = jnp.dot(
        mover, weight[...].reshape(weight.shape[-2:]), preferred_element_type=F32
    ).astype(BF16)
    piece[...] = ordered[pl.ds(pl.multiple_of(place[1] * (half // 2), 32), half // 2), :]


def order_heads(place, weight, at, head_dim):
    half, width = weight.shape[-2:]
    if at is None:
        spec = pl.BlockSpec((half, width), lambda i, s: (0, 0))
    else:
        spec = pl.BlockSpec((1, half, width), lambda i, s: (at, 0, 0))
    grid_spec = pltpu.PrefetchScalarGridSpec(
        num_scalar_prefetch=1,
        grid=(1,),
        in_specs=[spec],
        out_specs=[
            pl.BlockSpec((half, width), lambda i, s: (0, 0)),
            pl.BlockSpec((half // 2, width), lambda i, s: (0, 0)),
        ],
    )
    return pl.pallas_call(
        functools.partial(order_kernel, head_dim),
        grid_spec=grid_spec,
        out_shape=[
            jax.ShapeDtypeStruct((half, width), BF16),
            jax.ShapeDtypeStruct((half // 2, width), BF16),
        ],
        compiler_params=pltpu.CompilerParams(vmem_limit_bytes=VMEM),
        cost_estimate=pl.CostEstimate(
            flops=half * half * width * 2, bytes_accessed=half * width * 5, transcendentals=0
        ),
        name="order_heads",
    )(place, weight)


def merge_kernel(flip, place, own, near, far, out, *scratch):
    half = own.shape[0]
    merged = scratch[0] if flip else out

    def write(pieces):
        for tile in range(half // 64):
            merged[tile * 128 : tile * 128 + 64] = own[tile * 64 : tile * 64 + 64]
        for row in range(0, half, 32):
            ref, start = pieces[row // (half // 2)], row % (half // 2)
            to = row // 64 * 128 + 64 + row % 64
            merged[to : to + 32] = ref[start : start + 32]

    @pl.when(place[1] == 0)
    def _():
        write((near, far))

    @pl.when(place[1] != 0)
    def _():
        write((far, near))

    if flip:
        out[...] = merged[...].T


def merge_heads(place, own, near, far, flip):
    half, width = own.shape
    grid_spec = pltpu.PrefetchScalarGridSpec(
        num_scalar_prefetch=1,
        grid=(1,),
        in_specs=[
            pl.BlockSpec((half, width), lambda i, s: (0, 0)),
            pl.BlockSpec((half // 2, width), lambda i, s: (0, 0)),
            pl.BlockSpec((half // 2, width), lambda i, s: (0, 0)),
        ],
        out_specs=pl.BlockSpec((2 * half, width), lambda i, s: (0, 0)),
        scratch_shapes=[pltpu.VMEM((2 * half, width), BF16)] if flip else [],
    )
    return pl.pallas_call(
        functools.partial(merge_kernel, flip),
        grid_spec=grid_spec,
        out_shape=jax.ShapeDtypeStruct((2 * half, width), BF16),
        compiler_params=pltpu.CompilerParams(vmem_limit_bytes=VMEM),
        cost_estimate=pl.CostEstimate(
            flops=half * width * 100, bytes_accessed=half * width * 8, transcendentals=0
        ),
        name="merge_heads",
    )(place, own, near, far)


def dot_rows(values, weight):
    return lax.dot_general(values, weight, (((1,), (1,)), ((), ())), preferred_element_type=F32)


def head_norm(values, gain, ones2, head_dim):
    tiles = values.shape[-1] // LANES
    total = None
    for tile in range(tiles):
        part = values[:, tile * LANES : (tile + 1) * LANES]
        total = part * part if total is None else total + part * part
    factor = lax.rsqrt(split_dot(total, ones2) * (1.0 / head_dim) + EPSILON)
    return [
        (values[:, tile * LANES : (tile + 1) * LANES] * factor
         * gain[:, tile * LANES : (tile + 1) * LANES]).astype(BF16)
        for tile in range(tiles)
    ]


def project_kernel(head_dim, own, halo, w_q, w_k, w_v, gains, ones2, query, kv_own, kv_halo):
    rows = own.shape[0]
    ones = ones2[...]
    both = jnp.concatenate([own[...], halo[...]], 0)
    keys = dot_rows(both, w_k[...])
    for tile, part in enumerate(head_norm(keys, gains[1:2], ones, head_dim)):
        cols = slice(tile * LANES, (tile + 1) * LANES)
        kv_own[0, :, cols] = part[:rows]
        kv_halo[0, :, cols] = part[rows:]
    values = dot_rows(both, w_v[...])
    kv_own[1] = values[:rows].astype(BF16)
    kv_halo[1] = values[rows:].astype(BF16)
    queries = dot_rows(own[...], w_q[...])
    for tile, part in enumerate(head_norm(queries, gains[0:1], ones, head_dim)):
        query[:, tile * LANES : (tile + 1) * LANES] = part


def project(own, halo, w_q, w_k, w_v, gains, ones2, head_dim):
    rows, width = own.shape
    block = 256
    once = pl.Buffered(1)
    weight = pl.BlockSpec((width, width), lambda r: (0, 0), pipeline_mode=once)
    row = pl.BlockSpec((block, width), lambda r: (r, 0))
    pair = pl.BlockSpec((2, block, width), lambda r: (0, r, 0))
    return pl.pallas_call(
        functools.partial(project_kernel, head_dim),
        grid=(rows // block,),
        in_specs=[
            row, row, weight, weight, weight,
            pl.BlockSpec((2, width), lambda r: (0, 0)),
            pl.BlockSpec((2 * LANES, LANES), lambda r: (0, 0)),
        ],
        out_specs=[row, pair, pair],
        out_shape=[
            jax.ShapeDtypeStruct((rows, width), BF16),
            jax.ShapeDtypeStruct((2, rows, width), BF16),
            jax.ShapeDtypeStruct((2, rows, width), BF16),
        ],
        compiler_params=pltpu.CompilerParams(vmem_limit_bytes=VMEM),
        cost_estimate=pl.CostEstimate(
            flops=10 * rows * width * width, bytes_accessed=20 * rows * width, transcendentals=0
        ),
        name="project",
    )(own, halo, w_q, w_k, w_v, gains, ones2)


def attend_kernel(
    head_dim, place, query, kv_own, kv_halo, kv_core, mixed, w_out, mod, ones2, carry,
    out, send, scores, attended,
):
    frames, size, width = query.shape
    tiles = width // LANES
    offsets = 2 * WIN + 1
    half = width // 2
    block = pl.program_id(0)

    def window(kind, frame, rows, cols):
        if frame < frames:
            return kv_halo[kind, frames - 1 - frame, rows, cols].astype(F32)
        if frame < 2 * frames:
            return kv_own[kind, frame - frames, rows, cols].astype(F32)
        return kv_core[kind, 3 * frames - 1 - frame, rows, cols].astype(F32)

    @pl.loop(0, size // 16)
    def _(step):
        rows = pl.ds(pl.multiple_of(step * 16, 16), 16)
        for first in range(0, frames, 2):
            pair = (first, first + 1)
            sums = {}
            for tile in range(tiles):
                cols = slice(tile * LANES, (tile + 1) * LANES)
                asked = [query[frame, rows, cols].astype(F32) for frame in pair]
                for reached in range(first, first + 1 + offsets):
                    key = window(0, reached, rows, cols)
                    for frame, one in zip(pair, asked):
                        offset = reached - frame
                        if 0 <= offset < offsets:
                            at = frame * offsets + offset
                            sums[at] = one * key if tile == 0 else sums[at] + one * key
            for at, value in sums.items():
                scores[at, rows] = value

    scale = 1.0 / math.sqrt(head_dim)
    halo_there = place[2] > 0
    sub = 32

    @pl.loop(0, size // sub)
    def _(step):
        rows = pl.ds(pl.multiple_of(step * sub, sub), sub)
        for frame in range(frames):
            raw = scores[frame * offsets : (frame + 1) * offsets, rows]
            full = split_dot(raw.reshape(offsets * sub, LANES), ones2[...]).reshape(
                offsets, sub, LANES
            ) * scale
            parts = [
                jnp.where(halo_there, full[offset], -1e30)
                if frame + offset < frames
                else full[offset]
                for offset in range(offsets)
            ]
            highest = functools.reduce(jnp.maximum, parts)
            parts = [jnp.exp(part - highest) for part in parts]
            total = functools.reduce(jnp.add, parts)
            for offset, part in enumerate(parts):
                scores[frame * offsets + offset, rows] = (
                    (part / total).astype(BF16).astype(F32)
                )

    @pl.loop(0, size // 16)
    def _(step):
        rows = pl.ds(pl.multiple_of(step * 16, 16), 16)
        for first in range(0, frames, 2):
            pair = (first, first + 1)
            weights = {
                frame: [scores[frame * offsets + offset, rows] for offset in range(offsets)]
                for frame in pair
            }
            for tile in range(tiles):
                cols = slice(tile * LANES, (tile + 1) * LANES)
                sums = {}
                for reached in range(first, first + 1 + offsets):
                    value = window(1, reached, rows, cols)
                    for frame in pair:
                        offset = reached - frame
                        if 0 <= offset < offsets:
                            term = weights[frame][offset] * value
                            sums[frame] = term if offset == 0 else sums[frame] + term
                for frame in pair:
                    attended[frame, pl.ds(pl.multiple_of(block * size + step * 16, 16), 16), cols] = (
                        sums[frame].astype(BF16)
                    )

    @pl.when(block == pl.num_programs(0) - 1)
    def _():
        places = attended.shape[1]
        flat = attended[...].reshape(frames * places, width)
        for side in range(2):
            start = place[0] * half if side == 0 else (1 - place[0]) * half
            rows = pl.ds(pl.multiple_of(start, 64), half)
            result = dot_rows(w_out[rows, :], flat)
            for frame in range(frames):
                rounded = (
                    mixed[frame, rows].astype(F32)
                    + mod[rows, 2:3] * result[:, frame * places : (frame + 1) * places]
                ).astype(BF16)
                target = frame + place[1] * (3 - 2 * frame)
                if side == 0:
                    out[target, 0] = rounded
                else:
                    send[target] = rounded


def attend(place, query, kv_own, kv_halo, kv_core, mixed, w_out, mod, ones2, carry, head_dim,
           chunk, places):
    frames, size, width = query.shape
    half = width // 2
    block = 32
    once = pl.Buffered(1)
    pair = pl.BlockSpec((2, frames, block, width), lambda p, s: (0, 0, p, 0))
    in_specs = [
        pl.BlockSpec((frames, block, width), lambda p, s: (0, p, 0)),
        pair, pair, pair,
        pl.BlockSpec((frames, width, size), lambda p, s: (0, 0, 0), pipeline_mode=once),
        pl.BlockSpec((width, width), lambda p, s: (0, 0), pipeline_mode=once),
        pl.BlockSpec((width, 3), lambda p, s: (0, 0)),
        pl.BlockSpec((2 * LANES, LANES), lambda p, s: (0, 0)),
    ]
    args = [place, query, kv_own, kv_halo, kv_core, mixed, w_out, mod, ones2]
    body = functools.partial(attend_kernel, head_dim)
    aliases = {}
    if carry is None:
        def kernel(*refs):
            return body(*refs[:9], None, *refs[9:])
    else:
        kernel = body
        in_specs.append(pl.BlockSpec(memory_space=pl.ANY))
        args.append(carry)
        aliases = {9: 0}
    grid_spec = pltpu.PrefetchScalarGridSpec(
        num_scalar_prefetch=1,
        grid=(size // block,),
        in_specs=in_specs,
        out_specs=[
            pl.BlockSpec((frames, 1, half, size), lambda p, s: (0, s[0], 0, chunk)),
            pl.BlockSpec((frames, half, size), lambda p, s: (0, 0, 0)),
        ],
        scratch_shapes=[
            pltpu.VMEM((frames * (2 * WIN + 1), block, LANES), F32),
            pltpu.VMEM((frames, size, width), BF16),
        ],
    )
    return pl.pallas_call(
        kernel,
        grid_spec=grid_spec,
        out_shape=[
            jax.ShapeDtypeStruct((frames, 2, half, places), BF16),
            jax.ShapeDtypeStruct((frames, half, size), BF16),
        ],
        input_output_aliases=aliases,
        compiler_params=pltpu.CompilerParams(vmem_limit_bytes=VMEM),
        cost_estimate=pl.CostEstimate(
            flops=10 * frames * size * width * width, bytes_accessed=24 * frames * size * width,
            transcendentals=0,
        ),
        name="attend",
    )(*args)


def on_device(
    mesh_sizes, hidden, keypoints, tsteps, mod_table, ctrl_table, ctrl_proj, w_qkv, q_gain, k_gain,
    w_out,
):
    queue_size, head_size = mesh_sizes
    frames, _, places, half = hidden.shape
    width = 2 * half
    heads, head_dim = q_gain.shape
    classes = ctrl_table.shape[0]
    size = places // CHUNKS
    head = lax.axis_index("head")
    queue = lax.axis_index("queue")
    core = queue % 2
    swap = [(0, 1), (1, 0)]
    across = [
        (2 * q + h, 2 * ((q + queue_size // 2) % queue_size) + 1 - h)
        for q in range(queue_size)
        for h in range(2)
    ]
    cores = [(q, q ^ 1) for q in range(queue_size)]
    halos = [(q, q + 1) for q in range(1, queue_size - 1, 2)]
    halos += [(b, a) for a, b in halos]

    halo_there = ((queue > 0) & (queue < queue_size - 1)).astype(jnp.int32)
    place = jnp.stack([head, core, halo_there]).astype(jnp.int32)
    hidden = hidden.transpose(0, 1, 3, 2)
    w_qkv = w_qkv.transpose(1, 2, 0)

    parts = [
        lax.dynamic_slice(
            hidden, (0, 1 - head, 0, chunk * size), (frames, 1, half, size)
        ).reshape(frames, half, size)
        for chunk in range(CHUNKS)
    ]
    parts, w_qkv, w_out = lax.optimization_barrier((parts, w_qkv, w_out))
    arrived = [lax.ppermute(part, "head", swap) for part in parts]

    own, near, far = [], [], []
    for weight, at in ((w_qkv, 1), (w_qkv, 2), (w_qkv, 0), (w_out, None)):
        ordered, piece = order_heads(place, weight, at, head_dim)
        piece = lax.ppermute(piece, ("queue", "head"), across)
        own.append(ordered)
        near.append(piece)
        far.append(lax.ppermute(piece, "queue", cores))

    control = jnp.dot(ctrl_table, ctrl_proj, preferred_element_type=F32)
    small = jnp.concatenate(
        [control, q_gain.T.reshape(1, half), k_gain.T.reshape(1, half)], 0
    )
    small_other = lax.ppermute(small, "head", swap)
    both = jnp.stack([small, small_other])
    gains = both[:, classes:].reshape(2, 2, half // 64, 64).transpose(1, 2, 0, 3).reshape(2, width)
    natural = jnp.where(head == 0, both, both[::-1])[:, :classes]
    natural = natural.transpose(0, 2, 1).reshape(width, classes)
    table = class_table(jnp.pad(natural, ((0, 0), (0, 32 - classes))))
    mod = lax.dynamic_index_in_dim(mod_table, tsteps[0], 0, keepdims=False).T
    lane = jnp.arange(LANES)
    row = jnp.arange(2 * LANES)
    ones2 = (
        ((row % LANES // 64)[:, None] == (lane // 64)[None, :])
        & ((row % 8)[:, None] == (lane % 8)[None, :])
    ).astype(BF16)

    normed, mixed, halo = [], [], []
    for chunk in range(CHUNKS):
        one, two = adaptive_norm(place, hidden, arrived[chunk], keypoints, table, mod, chunk)
        normed.append(one)
        mixed.append(two)
        halo.append(lax.ppermute(one, "queue", halos))

    w_k, w_v, w_q, w_o = (
        merge_heads(place, own[at], near[at], far[at], at == 3) for at in range(4)
    )

    carry = None
    back = []
    for chunk in range(CHUNKS):
        query, kv_own, kv_halo = project(
            normed[chunk].reshape(frames * size, width),
            halo[chunk].reshape(frames * size, width),
            w_q, w_k, w_v, gains, ones2, head_dim,
        )
        kv_core = lax.ppermute(kv_own, "queue", cores)
        shape = (2, frames, size, width)
        carry, send = attend(
            place, query.reshape(frames, size, width), kv_own.reshape(shape),
            kv_halo.reshape(shape), kv_core.reshape(shape), mixed[chunk], w_o, mod, ones2, carry,
            head_dim, chunk, places,
        )
        back.append(lax.ppermute(send, "head", swap))
    for chunk in range(CHUNKS):
        carry = lax.dynamic_update_slice(
            carry, back[chunk][:, None], (0, 1 - head, 0, chunk * size)
        )
    return carry.transpose(0, 1, 3, 2)


def solution(mesh):
    placed = (
        P("queue", None, None, "head"),
        P("queue", None),
        P("queue"),
        P(),
        P(),
        P(None, "head"),
        P(None, None, "head"),
        P("head", None),
        P("head", None),
        P("head", None),
    )
    return jax.shard_map(
        functools.partial(on_device, (mesh.shape["queue"], mesh.shape["head"])),
        mesh=mesh,
        in_specs=placed,
        out_specs=P("queue", None, None, "head"),
        check_vma=False,
    )
```

```python
import functools
import math

import jax
import jax.numpy as jnp
from jax import lax
from jax.experimental import pallas as pl
from jax.experimental.pallas import tpu as pltpu
from jax.sharding import PartitionSpec as P

WIN = 4
EPSILON = 1e-06
CHUNKS = 4
LANES = 128
VMEM = 60 << 20
BLOCK = 64
COLUMNS = 256
KEY, VALUE, QUERY, OUT = range(4)
F32, BF16 = jnp.float32, jnp.bfloat16


def split_dot(values, ones2):
    high = values.astype(BF16)
    low = (values - high.astype(F32)).astype(BF16)
    return jnp.dot(
        jnp.concatenate([high, low], -1), ones2, preferred_element_type=F32
    )


def classes_kernel(control, table):
    values = control[...]
    high = values.astype(BF16)
    rest = values - high.astype(F32)
    middle = rest.astype(BF16)
    low = (rest - middle.astype(F32)).astype(BF16)
    table[...] = jnp.concatenate([high, middle, low, jnp.zeros_like(low)], -1)


def class_table(control):
    return pl.pallas_call(
        classes_kernel,
        out_shape=jax.ShapeDtypeStruct((control.shape[0], LANES), BF16),
        compiler_params=pltpu.CompilerParams(vmem_limit_bytes=VMEM),
        name="class_table",
    )(control)


def norm_kernel(place, hidden, other, keypoints, table, mod, normed, mixed):
    half, size = hidden.shape[-2:]
    points = keypoints[pl.ds(pl.program_id(0), 1), :]
    lane = lax.broadcasted_iota(jnp.int32, (LANES, size), 0)
    picks = ((lane % 32 == points) & (lane < 96) & (place[0] == 0)).astype(F32).astype(BF16)
    total = jnp.zeros((1, size), F32)
    for side, values in enumerate((hidden[0, 0], other[0])):
        start = place[0] * half if side == 0 else (1 - place[0]) * half
        rows = pl.ds(pl.multiple_of(start, 64), half)
        control = jnp.dot(table[rows, :], picks, preferred_element_type=F32)
        rounded = (values.astype(F32) + control).astype(BF16)
        mixed[0, rows] = rounded
        total = total + jnp.sum(rounded.astype(F32), 0, keepdims=True)
    centre = total * (1.0 / (2 * half))
    spread = jnp.zeros((1, size), F32)
    for side in range(2):
        part = mixed[0, side * half : (side + 1) * half].astype(F32) - centre
        spread = spread + jnp.sum(part * part, 0, keepdims=True)
    factor = lax.rsqrt(spread * (1.0 / (2 * half)) + EPSILON)
    for tile in range(2 * half // LANES):
        cols = slice(tile * LANES, (tile + 1) * LANES)
        part = ((mixed[0, cols].astype(F32) - centre) * factor).T
        normed[0, :, cols] = (part * (1.0 + mod[1:2, cols]) + mod[0:1, cols]).astype(BF16)


def adaptive_norm(place, hidden, other, keypoints, table, mod, chunk):
    frames, _, half, places = hidden.shape
    size = places // CHUNKS
    width = 2 * half
    grid_spec = pltpu.PrefetchScalarGridSpec(
        num_scalar_prefetch=1,
        grid=(frames,),
        in_specs=[
            pl.BlockSpec((1, 1, half, size), lambda f, s: (f, s[0], 0, chunk)),
            pl.BlockSpec((1, half, size), lambda f, s: (f, 0, 0)),
            pl.BlockSpec((frames, size), lambda f, s: (0, chunk)),
            pl.BlockSpec((width, LANES), lambda f, s: (0, 0)),
            pl.BlockSpec((3, width), lambda f, s: (0, 0)),
        ],
        out_specs=[
            pl.BlockSpec((1, size, width), lambda f, s: (f + s[1] * (3 - 2 * f), 0, 0)),
            pl.BlockSpec((1, width, size), lambda f, s: (f + s[1] * (3 - 2 * f), 0, 0)),
        ],
    )
    return pl.pallas_call(
        norm_kernel,
        grid_spec=grid_spec,
        out_shape=[
            jax.ShapeDtypeStruct((frames, size, width), BF16),
            jax.ShapeDtypeStruct((frames, width, size), BF16),
        ],
        compiler_params=pltpu.CompilerParams(vmem_limit_bytes=VMEM),
        cost_estimate=pl.CostEstimate(
            flops=frames * size * width * 300, bytes_accessed=6 * frames * size * width,
            transcendentals=0,
        ),
        name="adaptive_norm",
    )(place, hidden, other, keypoints, table, mod)


def piece_kernel(place, w_qkv, w_out, mover, piece):
    def write(weight):
        piece[...] = jnp.dot(mover[...], weight, preferred_element_type=F32).astype(BF16)

    @pl.when(place[3] < 3)
    def _():
        write(w_qkv[0])

    @pl.when(place[3] == 3)
    def _():
        write(w_out[...])


def order_kernel(w_qkv, w_out, mover, ordered):
    def write(weight):
        ordered[0] = jnp.dot(mover[...], weight, preferred_element_type=F32).astype(BF16)

    @pl.when(pl.program_id(0) < 3)
    def _():
        write(w_qkv[0])

    @pl.when(pl.program_id(0) == 3)
    def _():
        write(w_out[...])


def order_heads(w_qkv, w_out, mover):
    half, width = w_out.shape
    return pl.pallas_call(
        order_kernel,
        grid=(4,),
        in_specs=[
            pl.BlockSpec((1, half, width), lambda i: ((i + 1) % 3, 0, 0)),
            pl.BlockSpec((half, width), lambda i: (0, 0)),
            pl.BlockSpec((half, half), lambda i: (0, 0)),
        ],
        out_specs=pl.BlockSpec((1, half, width), lambda i: (i, 0, 0)),
        out_shape=jax.ShapeDtypeStruct((4, half, width), BF16),
        compiler_params=pltpu.CompilerParams(vmem_limit_bytes=VMEM),
        cost_estimate=pl.CostEstimate(
            flops=8 * half * half * width, bytes_accessed=half * width * 20, transcendentals=0
        ),
        name="order_heads",
    )(w_qkv, w_out, mover)


def piece_of_heads(place, w_qkv, w_out, mover):
    half, width = w_out.shape
    grid_spec = pltpu.PrefetchScalarGridSpec(
        num_scalar_prefetch=1,
        grid=(1,),
        in_specs=[
            pl.BlockSpec((1, half, width), lambda i, s: ((s[3] + 1) % 3, 0, 0)),
            pl.BlockSpec((half, width), lambda i, s: (0, 0)),
            pl.BlockSpec((half // 2, half), lambda i, s: (s[1], 0)),
        ],
        out_specs=pl.BlockSpec((half // 2, width), lambda i, s: (0, 0)),
    )
    return pl.pallas_call(
        piece_kernel,
        grid_spec=grid_spec,
        out_shape=jax.ShapeDtypeStruct((half // 2, width), BF16),
        compiler_params=pltpu.CompilerParams(vmem_limit_bytes=VMEM),
        cost_estimate=pl.CostEstimate(
            flops=half * half * width, bytes_accessed=half * width * 5, transcendentals=0
        ),
        name="piece_of_heads",
    )(place, w_qkv, w_out, mover)


def dot_rows(values, weight):
    return lax.dot_general(values, weight, (((1,), (1,)), ((), ())), preferred_element_type=F32)


def head_norm(values, gain, ones2, head_dim):
    tiles = values.shape[-1] // LANES
    total = None
    for tile in range(tiles):
        part = values[:, tile * LANES : (tile + 1) * LANES]
        total = part * part if total is None else total + part * part
    factor = lax.rsqrt(split_dot(total, ones2) * (1.0 / head_dim) + EPSILON)
    return [
        (values[:, tile * LANES : (tile + 1) * LANES] * factor
         * gain[:, tile * LANES : (tile + 1) * LANES]).astype(BF16)
        for tile in range(tiles)
    ]


def block_kernel(
    head_dim, place, own, halo, core, mixed, mine, others, mod, gains, ones2, carry,
    out, send, weights, sems, rows_in, query, kv, scores, attended, final,
):
    frames, size, width = own.shape
    tiles = width // LANES
    offsets = 2 * WIN + 1
    half = width // 2
    step = pl.program_id(0)
    ones = ones2[...]

    def fetches(kind):
        return [
            pltpu.make_async_copy(
                source.at[kind], weights.at[kind, :, at : at + 64], sems.at[kind, at // 64]
            )
            for at, source in ((0, mine), (64, others))
        ]

    @pl.when(step == 0)
    def _():
        for kind in (KEY, QUERY, VALUE, OUT):
            for fetch in fetches(kind):
                fetch.start()

    def arrived(kind):
        @pl.when(step == 0)
        def _():
            for fetch in fetches(kind):
                fetch.wait()

    for frame in range(frames):
        rows_in[frame] = halo[frames - 1 - frame]
        rows_in[frames + frame] = own[frame]
        rows_in[2 * frames + frame] = core[frames - 1 - frame]
    reach = 3 * frames * size

    arrived(KEY)
    all_rows = rows_in[...].reshape(reach, width)
    keys = dot_rows(all_rows, weights[KEY].reshape(width, width))
    for tile, part in enumerate(head_norm(keys, gains[1:2], ones, head_dim)):
        kv[0, :, :, tile * LANES : (tile + 1) * LANES] = part.reshape(3 * frames, size, LANES)
    arrived(QUERY)
    own_rows = rows_in[frames : 2 * frames].reshape(frames * size, width)
    queries = dot_rows(own_rows, weights[QUERY].reshape(width, width))
    for tile, part in enumerate(head_norm(queries, gains[0:1], ones, head_dim)):
        query[:, :, tile * LANES : (tile + 1) * LANES] = part.reshape(frames, size, LANES)

    def window(kind, frame, rows, cols):
        return kv[kind, frame, rows, cols].astype(F32)

    def score(start, first):
        rows = slice(start, start + 16)
        pair = (first, first + 1)
        sums = {}
        for tile in range(tiles):
            cols = slice(tile * LANES, (tile + 1) * LANES)
            asked = [query[frame, rows, cols].astype(F32) for frame in pair]
            for reached in range(first, first + 1 + offsets):
                key = window(0, reached, rows, cols)
                for frame, one in zip(pair, asked):
                    offset = reached - frame
                    if 0 <= offset < offsets:
                        at = frame * offsets + offset
                        sums[at] = one * key if tile == 0 else sums[at] + one * key
        for at, value in sums.items():
            scores[at, rows] = value

    scale = 1.0 / math.sqrt(head_dim)
    halo_there = place[2] > 0

    def soften(start, frame, sub=32):
        rows = slice(start, start + sub)
        raw = scores[frame * offsets : (frame + 1) * offsets, rows]
        full = split_dot(raw.reshape(offsets * sub, LANES), ones).reshape(
            offsets, sub, LANES
        ) * scale
        parts = [
            jnp.where(halo_there, full[offset], -1e30) if frame + offset < frames else full[offset]
            for offset in range(offsets)
        ]
        highest = functools.reduce(jnp.maximum, parts)
        parts = [jnp.exp(part - highest) for part in parts]
        inverse = 1.0 / functools.reduce(jnp.add, parts)
        for offset, part in enumerate(parts):
            scores[frame * offsets + offset, rows] = (part * inverse).astype(BF16).astype(F32)

    arrived(VALUE)
    steps = [functools.partial(score, start, first)
             for start in range(0, size, 16) for first in range(0, frames, 2)]
    steps += [functools.partial(soften, start, frame)
              for start in range(0, size, 32) for frame in range(frames)]
    starts = list(range(0, width, COLUMNS))
    done = 0
    for at, start in enumerate(starts):
        high = min(start + COLUMNS, width)
        kv[1, :, :, start:high] = dot_rows(
            all_rows, weights[VALUE].reshape(width, width)[start:high]
        ).astype(BF16).reshape(3 * frames, size, high - start)
        until = len(steps) * (at + 1) // len(starts)
        for unit in steps[done:until]:
            unit()
        done = until

    @pl.loop(0, size // 16)
    def _(at):
        rows = pl.ds(pl.multiple_of(at * 16, 16), 16)
        for first in range(0, frames, 2):
            pair = (first, first + 1)
            shares = {
                frame: [scores[frame * offsets + offset, rows] for offset in range(offsets)]
                for frame in pair
            }
            for tile in range(tiles):
                cols = slice(tile * LANES, (tile + 1) * LANES)
                sums = {}
                for reached in range(first, first + 1 + offsets):
                    value = window(1, reached, rows, cols)
                    for frame in pair:
                        offset = reached - frame
                        if 0 <= offset < offsets:
                            term = shares[frame][offset] * value
                            sums[frame] = term if offset == 0 else sums[frame] + term
                for frame in pair:
                    attended[frame, pl.ds(pl.multiple_of(step * size + at * 16, 16), 16), cols] = (
                        sums[frame].astype(BF16)
                    )

    arrived(OUT)

    @pl.when(step == pl.num_programs(0) - 1)
    def _():
        places = attended.shape[1]
        own_half = pl.ds(pl.multiple_of(place[0] * half, 64), half)
        send_half = pl.ds(pl.multiple_of((1 - place[0]) * half, 64), half)
        flat = attended[...].reshape(frames * places, width)
        result = jnp.dot(flat, weights[OUT].reshape(width, width), preferred_element_type=F32)
        result = result * mod[2:3, :]
        for frame in range(frames):
            target = frame + place[1] * (3 - 2 * frame)
            for tile in range(tiles):
                cols = slice(tile * LANES, (tile + 1) * LANES)
                turned = result[frame * places : (frame + 1) * places, cols].T
                final[cols] = (mixed[frame, cols].astype(F32) + turned).astype(BF16)
            out[target, 0] = final[own_half]
            send[target] = final[send_half]


def whole_block(place, own, halo, core, mixed, mine, others, mod, gains, ones2, carry, head_dim,
                chunk, places):
    frames, size, width = own.shape
    half = width // 2
    block = BLOCK
    once = pl.Buffered(1)
    rows = pl.BlockSpec((frames, block, width), lambda p, s: (0, p, 0))
    in_specs = [
        rows, rows, rows,
        pl.BlockSpec((frames, width, size), lambda p, s: (0, 0, 0), pipeline_mode=once),
        pl.BlockSpec(memory_space=pl.ANY),
        pl.BlockSpec(memory_space=pl.ANY),
        pl.BlockSpec((3, width), lambda p, s: (0, 0)),
        pl.BlockSpec((2, width), lambda p, s: (0, 0)),
        pl.BlockSpec((2 * LANES, LANES), lambda p, s: (0, 0)),
    ]
    blocked = (4, half // 64, 64, width)
    args = [place, own, halo, core, mixed, mine.reshape(blocked), others.reshape(blocked), mod,
            gains, ones2]
    body = functools.partial(block_kernel, head_dim)
    aliases = {}
    if carry is None:
        def kernel(*refs):
            return body(*refs[:10], None, *refs[10:])
    else:
        kernel = body
        in_specs.append(pl.BlockSpec(memory_space=pl.ANY))
        args.append(carry)
        aliases = {10: 0}
    grid_spec = pltpu.PrefetchScalarGridSpec(
        num_scalar_prefetch=1,
        grid=(size // block,),
        in_specs=in_specs,
        out_specs=[
            pl.BlockSpec((frames, 1, half, size), lambda p, s: (0, s[0], 0, chunk)),
            pl.BlockSpec((frames, half, size), lambda p, s: (0, 0, 0)),
        ],
        scratch_shapes=[
            pltpu.VMEM((4, half // 64, 128, width), BF16),
            pltpu.SemaphoreType.DMA((4, 2)),
            pltpu.VMEM((3 * frames, block, width), BF16),
            pltpu.VMEM((frames, block, width), BF16),
            pltpu.VMEM((2, 3 * frames, block, width), BF16),
            pltpu.VMEM((frames * (2 * WIN + 1), block, LANES), F32),
            pltpu.VMEM((frames, size, width), BF16),
            pltpu.VMEM((width, size), BF16),
        ],
    )
    return pl.pallas_call(
        kernel,
        grid_spec=grid_spec,
        out_shape=[
            jax.ShapeDtypeStruct((frames, 2, half, places), BF16),
            jax.ShapeDtypeStruct((frames, half, size), BF16),
        ],
        input_output_aliases=aliases,
        compiler_params=pltpu.CompilerParams(vmem_limit_bytes=VMEM),
        cost_estimate=pl.CostEstimate(
            flops=18 * frames * size * width * width, bytes_accessed=12 * frames * size * width,
            transcendentals=0,
        ),
        name="whole_block",
    )(*args)


def on_device(
    mesh_sizes, hidden, keypoints, tsteps, mod_table, ctrl_table, ctrl_proj, w_qkv, q_gain, k_gain,
    w_out,
):
    queue_size, head_size = mesh_sizes
    frames, _, places, half = hidden.shape
    width = 2 * half
    heads, head_dim = q_gain.shape
    classes = ctrl_table.shape[0]
    size = places // CHUNKS
    head = lax.axis_index("head")
    queue = lax.axis_index("queue")
    core = queue % 2
    swap = [(0, 1), (1, 0)]
    across = [
        (2 * q + h, 2 * ((q + queue_size // 2) % queue_size) + 1 - h)
        for q in range(queue_size)
        for h in range(2)
    ]
    cores = [(q, q ^ 1) for q in range(queue_size)]
    halos = [(q, q + 1) for q in range(1, queue_size - 1, 2)]
    halos += [(b, a) for a, b in halos]

    halo_there = ((queue > 0) & (queue < queue_size - 1)).astype(jnp.int32)
    place = jnp.stack([head, core, halo_there, queue // 8 % 4]).astype(jnp.int32)
    hidden = hidden.transpose(0, 1, 3, 2)
    w_qkv = w_qkv.transpose(1, 2, 0)

    parts = [
        lax.dynamic_slice(
            hidden, (0, 1 - head, 0, chunk * size), (frames, 1, half, size)
        ).reshape(frames, half, size)
        for chunk in range(CHUNKS)
    ]
    parts, w_qkv, w_out = lax.optimization_barrier((parts, w_qkv, w_out))
    arrived = [lax.ppermute(part, "head", swap) for part in parts]

    source = jnp.arange(half)
    mover = (
        source[None, :] == ((source % heads) * head_dim + source // heads)[:, None]
    ).astype(BF16)
    piece = piece_of_heads(place, w_qkv, w_out, mover)
    piece = lax.ppermute(piece, ("queue", "head"), across)
    sharers = [
        [((top * 4 + x) * 4 + y) * 2 + c for x in range(4) for c in range(2)]
        for top in range(queue_size // 32)
        for y in range(4)
    ]
    others = lax.all_gather(piece, "queue", axis=0, tiled=True, axis_index_groups=sharers)
    mine = order_heads(w_qkv, w_out, mover)

    control = jnp.dot(ctrl_table, ctrl_proj, preferred_element_type=F32)
    small = jnp.concatenate(
        [control, q_gain.T.reshape(1, half), k_gain.T.reshape(1, half)], 0
    )
    small_other = lax.ppermute(small, "head", swap)
    both = jnp.stack([small, small_other])
    gains = both[:, classes:].reshape(2, 2, half // 64, 64).transpose(1, 2, 0, 3).reshape(2, width)
    natural = jnp.where(head == 0, both, both[::-1])[:, :classes]
    natural = natural.transpose(0, 2, 1).reshape(width, classes)
    table = class_table(jnp.pad(natural, ((0, 0), (0, 32 - classes))))
    mod = lax.dynamic_index_in_dim(mod_table, tsteps[0], 0, keepdims=False)
    lane = jnp.arange(LANES)
    row = jnp.arange(2 * LANES)
    ones2 = (
        ((row % LANES // 64)[:, None] == (lane // 64)[None, :])
        & ((row % 8)[:, None] == (lane % 8)[None, :])
    ).astype(BF16)

    normed, mixed, halo, beside = [], [], [], []
    for chunk in range(CHUNKS):
        one, two = adaptive_norm(place, hidden, arrived[chunk], keypoints, table, mod, chunk)
        normed.append(one)
        mixed.append(two)
        halo.append(lax.ppermute(one, "queue", halos))
        beside.append(lax.ppermute(one, "queue", cores))

    carry = None
    back = []
    for chunk in range(CHUNKS):
        carry, send = whole_block(
            place, normed[chunk], halo[chunk], beside[chunk], mixed[chunk], mine, others, mod, gains,
            ones2, carry, head_dim, chunk, places,
        )
        back.append(lax.ppermute(send, "head", swap))
    for chunk in range(CHUNKS):
        carry = lax.dynamic_update_slice(
            carry, back[chunk][:, None], (0, 1 - head, 0, chunk * size)
        )
    return carry.transpose(0, 1, 3, 2)


def solution(mesh):
    placed = (
        P("queue", None, None, "head"),
        P("queue", None),
        P("queue"),
        P(),
        P(),
        P(None, "head"),
        P(None, None, "head"),
        P("head", None),
        P("head", None),
        P("head", None),
    )
    return jax.shard_map(
        functools.partial(on_device, (mesh.shape["queue"], mesh.shape["head"])),
        mesh=mesh,
        in_specs=placed,
        out_specs=P("queue", None, None, "head"),
        check_vma=False,
    )
```

```python
import functools
import math

import jax
import jax.numpy as jnp
from jax import lax
from jax.experimental import pallas as pl
from jax.experimental.pallas import tpu as pltpu
from jax.sharding import PartitionSpec as P

WIN = 4
EPSILON = 1e-06
CHUNKS = 4
LANES = 128
VMEM = 46 << 20
SMALL_VMEM = 32 << 20
BLOCK = 64
COLUMNS = 256
COST = 0.05
KEY, VALUE, QUERY, OUT = range(4)
F32, BF16 = jnp.float32, jnp.bfloat16


def split_dot(values, ones2):
    high = values.astype(BF16)
    low = (values - high.astype(F32)).astype(BF16)
    return jnp.dot(
        jnp.concatenate([high, low], -1), ones2, preferred_element_type=F32
    )


def cost(flops):
    return pl.CostEstimate(flops=int(flops * COST), bytes_accessed=0, transcendentals=0)


def classes_kernel(control, table):
    values = control[...]
    high = values.astype(BF16)
    rest = values - high.astype(F32)
    middle = rest.astype(BF16)
    low = (rest - middle.astype(F32)).astype(BF16)
    table[...] = jnp.concatenate([high, middle, low, jnp.zeros_like(low)], -1)


def class_table(control):
    return pl.pallas_call(
        classes_kernel,
        out_shape=jax.ShapeDtypeStruct((control.shape[0], LANES), BF16),
        compiler_params=pltpu.CompilerParams(vmem_limit_bytes=VMEM),
        name="class_table",
    )(control)


def norm_kernel(place, hidden, other, keypoints, table, mod, normed, mixed):
    half, size = hidden.shape[-2:]
    points = keypoints[pl.ds(pl.program_id(0), 1), :]
    lane = lax.broadcasted_iota(jnp.int32, (LANES, size), 0)
    picks = ((lane % 32 == points) & (lane < 96) & (place[0] == 0)).astype(F32).astype(BF16)
    total = jnp.zeros((1, size), F32)
    for side, values in enumerate((hidden[0, 0], other[0])):
        start = place[0] * half if side == 0 else (1 - place[0]) * half
        rows = pl.ds(pl.multiple_of(start, 64), half)
        control = jnp.dot(table[rows, :], picks, preferred_element_type=F32)
        rounded = (values.astype(F32) + control).astype(BF16)
        mixed[0, rows] = rounded
        total = total + jnp.sum(rounded.astype(F32), 0, keepdims=True)
    centre = total * (1.0 / (2 * half))
    spread = jnp.zeros((1, size), F32)
    for side in range(2):
        part = mixed[0, side * half : (side + 1) * half].astype(F32) - centre
        spread = spread + jnp.sum(part * part, 0, keepdims=True)
    factor = lax.rsqrt(spread * (1.0 / (2 * half)) + EPSILON)
    for tile in range(2 * half // LANES):
        cols = slice(tile * LANES, (tile + 1) * LANES)
        part = ((mixed[0, cols].astype(F32) - centre) * factor).T
        normed[0, :, cols] = (part * (1.0 + mod[1:2, cols]) + mod[0:1, cols]).astype(BF16)


def adaptive_norm(place, hidden, other, keypoints, table, mod, chunk):
    frames, _, half, places = hidden.shape
    size = places // CHUNKS
    width = 2 * half
    grid_spec = pltpu.PrefetchScalarGridSpec(
        num_scalar_prefetch=1,
        grid=(frames,),
        in_specs=[
            pl.BlockSpec((1, 1, half, size), lambda f, s: (f, s[0], 0, chunk)),
            pl.BlockSpec((1, half, size), lambda f, s: (f, 0, 0)),
            pl.BlockSpec((frames, size), lambda f, s: (0, chunk)),
            pl.BlockSpec((width, LANES), lambda f, s: (0, 0)),
            pl.BlockSpec((3, width), lambda f, s: (0, 0)),
        ],
        out_specs=[
            pl.BlockSpec((1, size, width), lambda f, s: (f + s[1] * (3 - 2 * f), 0, 0)),
            pl.BlockSpec((1, width, size), lambda f, s: (f + s[1] * (3 - 2 * f), 0, 0)),
        ],
    )
    return pl.pallas_call(
        norm_kernel,
        grid_spec=grid_spec,
        out_shape=[
            jax.ShapeDtypeStruct((frames, size, width), BF16),
            jax.ShapeDtypeStruct((frames, width, size), BF16),
        ],
        compiler_params=pltpu.CompilerParams(vmem_limit_bytes=SMALL_VMEM),
        cost_estimate=cost(4000 * frames * size * width),
        name="adaptive_norm",
    )(place, hidden, other, keypoints, table, mod)


def order_kernel(place, weight, mover, ordered, piece):
    half = mover.shape[0]
    ordered[...] = jnp.dot(
        mover[...], weight[...].reshape(weight.shape[-2:]), preferred_element_type=F32
    ).astype(BF16)
    piece[...] = ordered[pl.ds(pl.multiple_of(place[1] * (half // 2), 32), half // 2), :]


def order_heads(place, weight, at, mover):
    half, width = weight.shape[-2:]
    if at is None:
        spec = pl.BlockSpec((half, width), lambda i, s: (0, 0))
    else:
        spec = pl.BlockSpec((1, half, width), lambda i, s: (at, 0, 0))
    grid_spec = pltpu.PrefetchScalarGridSpec(
        num_scalar_prefetch=1,
        grid=(1,),
        in_specs=[spec, pl.BlockSpec((half, half), lambda i, s: (0, 0))],
        out_specs=[
            pl.BlockSpec((half, width), lambda i, s: (0, 0)),
            pl.BlockSpec((half // 2, width), lambda i, s: (0, 0)),
        ],
    )
    return pl.pallas_call(
        order_kernel,
        grid_spec=grid_spec,
        out_shape=[
            jax.ShapeDtypeStruct((half, width), BF16),
            jax.ShapeDtypeStruct((half // 2, width), BF16),
        ],
        compiler_params=pltpu.CompilerParams(vmem_limit_bytes=VMEM),
        cost_estimate=cost(2 * half * half * width),
        name="order_heads",
    )(place, weight, mover)


def dot_rows(values, weight):
    return lax.dot_general(values, weight, (((1,), (1,)), ((), ())), preferred_element_type=F32)


def head_norm(values, gain, ones2, head_dim):
    tiles = values.shape[-1] // LANES
    total = None
    for tile in range(tiles):
        part = values[:, tile * LANES : (tile + 1) * LANES]
        total = part * part if total is None else total + part * part
    factor = lax.rsqrt(split_dot(total, ones2) * (1.0 / head_dim) + EPSILON)
    return [
        (values[:, tile * LANES : (tile + 1) * LANES] * factor
         * gain[:, tile * LANES : (tile + 1) * LANES]).astype(BF16)
        for tile in range(tiles)
    ]


def merge_kernel(place, *refs):
    mine, near, far, (weights, sems) = refs[:4], refs[4:8], refs[8:12], refs[12:]
    part = weights.shape[1] // 2
    copies = []
    for kind in range(4):
        target = weights.at[kind]
        pairs = [
            (mine[kind], target.at[:, 0:32]),
            (near[kind], target.at[pl.ds(place[1] * part, part), 32:64]),
            (far[kind], target.at[pl.ds((1 - place[1]) * part, part), 32:64]),
        ]
        for at, (source, to) in enumerate(pairs):
            copies.append(pltpu.make_async_copy(source, to, sems.at[kind, at]))
            copies[-1].start()
    for copy in copies:
        copy.wait()


def merge_heads(place, mine, near, far):
    half, width = mine[0].shape
    grid_spec = pltpu.PrefetchScalarGridSpec(
        num_scalar_prefetch=1,
        grid=(1,),
        in_specs=[pl.BlockSpec(memory_space=pl.ANY)] * 12,
        out_specs=pl.BlockSpec(memory_space=pltpu.VMEM),
        scratch_shapes=[pltpu.SemaphoreType.DMA((4, 3))],
    )
    return pl.pallas_call(
        merge_kernel,
        grid_spec=grid_spec,
        out_shape=pltpu.VMEM((4, half // 32, 64, width), BF16),
        compiler_params=pltpu.CompilerParams(vmem_limit_bytes=VMEM),
        cost_estimate=cost(8 * half * half * width),
        name="merge_heads",
    )(place, *[weight.reshape(-1, 32, width) for weight in (*mine, *near, *far)])


def block_kernel(
    head_dim, place, own, halo, core, mixed, mod, gains, ones2, weights, carry,
    out, send, rows_in, query, kv, scores, attended, final,
):
    frames, size, width = own.shape
    tiles = width // LANES
    offsets = 2 * WIN + 1
    half = width // 2
    step = pl.program_id(0)
    ones = ones2[...]

    for frame in range(frames):
        rows_in[frame] = halo[frames - 1 - frame]
        rows_in[frames + frame] = own[frame]
        rows_in[2 * frames + frame] = core[frames - 1 - frame]
    reach = 3 * frames * size

    all_rows = rows_in[...].reshape(reach, width)
    edge = width + LANES
    key_value = weights[KEY : VALUE + 1].reshape(2 * width, width)
    keys = dot_rows(all_rows, key_value[0:edge])
    for tile, part in enumerate(head_norm(keys[:, :width], gains[1:2], ones, head_dim)):
        kv[0, :, :, tile * LANES : (tile + 1) * LANES] = part.reshape(3 * frames, size, LANES)
    kv[1, :, :, :LANES] = keys[:, width:].astype(BF16).reshape(3 * frames, size, LANES)
    own_rows = rows_in[frames : 2 * frames].reshape(frames * size, width)
    queries = dot_rows(own_rows, weights[QUERY].reshape(width, width))
    for tile, part in enumerate(head_norm(queries, gains[0:1], ones, head_dim)):
        query[:, :, tile * LANES : (tile + 1) * LANES] = part.reshape(frames, size, LANES)

    def window(kind, frame, rows, cols):
        return kv[kind, frame, rows, cols].astype(F32)

    def score(start, first):
        rows = slice(start, start + 16)
        pair = (first, first + 1)
        sums = {}
        for tile in range(tiles):
            cols = slice(tile * LANES, (tile + 1) * LANES)
            asked = [query[frame, rows, cols].astype(F32) for frame in pair]
            for reached in range(first, first + 1 + offsets):
                key = window(0, reached, rows, cols)
                for frame, one in zip(pair, asked):
                    offset = reached - frame
                    if 0 <= offset < offsets:
                        at = frame * offsets + offset
                        sums[at] = one * key if tile == 0 else sums[at] + one * key
        for at, value in sums.items():
            scores[at, rows] = value

    scale = 1.0 / math.sqrt(head_dim)
    halo_there = place[2] > 0

    def soften(start, frame, sub=32):
        rows = slice(start, start + sub)
        raw = scores[frame * offsets : (frame + 1) * offsets, rows]
        full = split_dot(raw.reshape(offsets * sub, LANES), ones).reshape(
            offsets, sub, LANES
        ) * scale
        parts = [
            jnp.where(halo_there, full[offset], -1e30) if frame + offset < frames else full[offset]
            for offset in range(offsets)
        ]
        highest = functools.reduce(jnp.maximum, parts)
        parts = [jnp.exp(part - highest) for part in parts]
        inverse = 1.0 / functools.reduce(jnp.add, parts)
        for offset, part in enumerate(parts):
            scores[frame * offsets + offset, rows] = (part * inverse).astype(BF16).astype(F32)

    steps = [functools.partial(score, start, first)
             for start in range(0, size, 16) for first in range(0, frames, 2)]
    steps += [functools.partial(soften, start, frame)
              for start in range(0, size, 32) for frame in range(frames)]
    starts = list(range(LANES, width, COLUMNS))
    done = 0
    for at, start in enumerate(starts):
        high = min(start + COLUMNS, width)
        kv[1, :, :, start:high] = dot_rows(
            all_rows, key_value[width + start : width + high]
        ).astype(BF16).reshape(3 * frames, size, high - start)
        until = len(steps) * (at + 1) // len(starts)
        for unit in steps[done:until]:
            unit()
        done = until

    @pl.loop(0, size // 16)
    def _(at):
        rows = pl.ds(pl.multiple_of(at * 16, 16), 16)
        for first in range(0, frames, 2):
            pair = (first, first + 1)
            shares = {
                frame: [scores[frame * offsets + offset, rows] for offset in range(offsets)]
                for frame in pair
            }
            for tile in range(tiles):
                cols = slice(tile * LANES, (tile + 1) * LANES)
                sums = {}
                for reached in range(first, first + 1 + offsets):
                    value = window(1, reached, rows, cols)
                    for frame in pair:
                        offset = reached - frame
                        if 0 <= offset < offsets:
                            term = shares[frame][offset] * value
                            sums[frame] = term if offset == 0 else sums[frame] + term
                for frame in pair:
                    attended[frame, pl.ds(pl.multiple_of(step * size + at * 16, 16), 16), cols] = (
                        sums[frame].astype(BF16)
                    )

    @pl.when(step == pl.num_programs(0) - 1)
    def _():
        places = attended.shape[1]
        own_half = pl.ds(pl.multiple_of(place[0] * half, 64), half)
        send_half = pl.ds(pl.multiple_of((1 - place[0]) * half, 64), half)
        flat = attended[...].reshape(frames * places, width)
        result = jnp.dot(flat, weights[OUT].reshape(width, width), preferred_element_type=F32)
        result = result * mod[2:3, :]
        for frame in range(frames):
            target = frame + place[1] * (3 - 2 * frame)
            for tile in range(tiles):
                cols = slice(tile * LANES, (tile + 1) * LANES)
                turned = result[frame * places : (frame + 1) * places, cols].T
                final[cols] = (mixed[frame, cols].astype(F32) + turned).astype(BF16)
            out[target, 0] = final[own_half]
            send[target] = final[send_half]


def whole_block(place, own, halo, core, mixed, mod, gains, ones2, weights, carry, head_dim,
                chunk, places):
    frames, size, width = own.shape
    half = width // 2
    block = BLOCK
    once = pl.Buffered(1)
    rows = pl.BlockSpec((frames, block, width), lambda p, s: (0, p, 0))
    in_specs = [
        rows, rows, rows,
        pl.BlockSpec((frames, width, size), lambda p, s: (0, 0, 0), pipeline_mode=once),
        pl.BlockSpec((3, width), lambda p, s: (0, 0)),
        pl.BlockSpec((2, width), lambda p, s: (0, 0)),
        pl.BlockSpec((2 * LANES, LANES), lambda p, s: (0, 0)),
    ]
    in_specs.append(pl.BlockSpec(memory_space=pltpu.VMEM))
    weights = pltpu.with_memory_space_constraint(weights, pltpu.VMEM)
    args = [place, own, halo, core, mixed, mod, gains, ones2, weights]
    aliases = {}
    if carry is not None:
        in_specs.append(pl.BlockSpec(memory_space=pl.ANY))
        aliases = {len(args): 0}
        args.append(carry)

    def kernel(*refs):
        block_kernel(head_dim, *refs[:9], None, *refs[9 + len(aliases) :])

    grid_spec = pltpu.PrefetchScalarGridSpec(
        num_scalar_prefetch=1,
        grid=(size // block,),
        in_specs=in_specs,
        out_specs=[
            pl.BlockSpec((frames, 1, half, size), lambda p, s: (0, s[0], 0, chunk)),
            pl.BlockSpec((frames, half, size), lambda p, s: (0, 0, 0)),
        ],
        scratch_shapes=[
            pltpu.VMEM((3 * frames, block, width), BF16),
            pltpu.VMEM((frames, block, width), BF16),
            pltpu.VMEM((2, 3 * frames, block, width), BF16),
            pltpu.VMEM((frames * (2 * WIN + 1), block, LANES), F32),
            pltpu.VMEM((frames, size, width), BF16),
            pltpu.VMEM((width, size), BF16),
        ],
    )
    return pl.pallas_call(
        kernel,
        grid_spec=grid_spec,
        out_shape=[
            jax.ShapeDtypeStruct((frames, 2, half, places), BF16),
            jax.ShapeDtypeStruct((frames, half, size), BF16),
        ],
        input_output_aliases=aliases,
        compiler_params=pltpu.CompilerParams(vmem_limit_bytes=VMEM),
        cost_estimate=cost(36 * frames * size * width * width),
        name="whole_block",
    )(*args)


def on_device(
    mesh_sizes, hidden, keypoints, tsteps, mod_table, ctrl_table, ctrl_proj, w_qkv, q_gain, k_gain,
    w_out,
):
    queue_size, head_size = mesh_sizes
    frames, _, places, half = hidden.shape
    width = 2 * half
    heads, head_dim = q_gain.shape
    classes = ctrl_table.shape[0]
    size = places // CHUNKS
    head = lax.axis_index("head")
    queue = lax.axis_index("queue")
    core = queue % 2
    swap = [(0, 1), (1, 0)]
    across = [
        (2 * q + h, 2 * ((q + queue_size // 2) % queue_size) + 1 - h)
        for q in range(queue_size)
        for h in range(2)
    ]
    cores = [(q, q ^ 1) for q in range(queue_size)]
    halos = [(q, q + 1) for q in range(1, queue_size - 1, 2)]
    halos += [(b, a) for a, b in halos]

    halo_there = ((queue > 0) & (queue < queue_size - 1)).astype(jnp.int32)
    place = jnp.stack([head, core, halo_there]).astype(jnp.int32)
    hidden = hidden.transpose(0, 1, 3, 2)
    w_qkv = w_qkv.transpose(1, 2, 0)

    parts = [
        lax.dynamic_slice(
            hidden, (0, 1 - head, 0, chunk * size), (frames, 1, half, size)
        ).reshape(frames, half, size)
        for chunk in range(CHUNKS)
    ]
    parts, w_qkv, w_out = lax.optimization_barrier((parts, w_qkv, w_out))
    arrived = [lax.ppermute(parts[0], "head", swap)]
    for part in lax.optimization_barrier((parts[1:], arrived[0]))[0]:
        arrived.append(lax.ppermute(part, "head", swap))

    source = jnp.arange(half)
    mover = (
        source[None, :] == ((source % heads) * head_dim + source // heads)[:, None]
    ).astype(BF16)
    mine, near = [None] * 4, [None] * 4
    for kind, weight, at in (
        (KEY, w_qkv, 1), (OUT, w_out, None), (VALUE, w_qkv, 2), (QUERY, w_qkv, 0)
    ):
        mine[kind], piece = order_heads(place, weight, at, mover)
        if kind == OUT:
            near[kind] = lax.ppermute(piece, "head", swap)
        else:
            near[kind] = lax.ppermute(piece, ("queue", "head"), across)

    control = jnp.dot(ctrl_table, ctrl_proj, preferred_element_type=F32)
    small = jnp.concatenate(
        [control, q_gain.T.reshape(1, half), k_gain.T.reshape(1, half)], 0
    )
    small_other = lax.ppermute(small, "head", swap)
    both = jnp.stack([small, small_other])
    gains = both[:, classes:].reshape(2, 2, half // 32, 32).transpose(1, 2, 0, 3).reshape(2, width)
    natural = jnp.where(head == 0, both, both[::-1])[:, :classes]
    natural = natural.transpose(0, 2, 1).reshape(width, classes)
    table = class_table(jnp.pad(natural, ((0, 0), (0, 32 - classes))))
    mod = lax.dynamic_index_in_dim(mod_table, tsteps[0], 0, keepdims=False)
    lane = jnp.arange(LANES)
    row = jnp.arange(2 * LANES)
    ones2 = (
        ((row // 32 % 2)[:, None] == (lane // 32 % 2)[None, :])
        & ((row % 8)[:, None] == (lane % 8)[None, :])
    ).astype(BF16)

    normed, mixed, halo, beside = [], [], [], []

    def prepare(chunk, other):
        one, two = adaptive_norm(place, hidden, other, keypoints, table, mod, chunk)
        normed.append(one)
        mixed.append(two)
        halo.append(lax.ppermute(one, "queue", halos))
        beside.append(lax.ppermute(one, "queue", cores))

    ahead = 2
    prepare(0, arrived[0])
    near, _ = lax.optimization_barrier((near, normed[0]))
    far = [lax.ppermute(piece, "queue", cores) for piece in near]
    prepare(1, arrived[1])
    weights = merge_heads(place, mine, near, far)
    carry = None
    back = []
    for chunk in range(CHUNKS):
        carry, send = whole_block(
            place, normed[chunk], halo[chunk], beside[chunk], mixed[chunk], mod, gains, ones2, weights,
            carry, head_dim, chunk, places,
        )
        if chunk + ahead < CHUNKS:
            other, send = lax.optimization_barrier((arrived[chunk + ahead], send))
            prepare(chunk + ahead, other)
        back.append(lax.ppermute(send, "head", swap))
    for chunk in range(CHUNKS):
        carry = lax.dynamic_update_slice(
            carry, back[chunk][:, None], (0, 1 - head, 0, chunk * size)
        )
    return carry.transpose(0, 1, 3, 2)


def solution(mesh):
    placed = (
        P("queue", None, None, "head"),
        P("queue", None),
        P("queue"),
        P(),
        P(),
        P(None, "head"),
        P(None, None, "head"),
        P("head", None),
        P("head", None),
        P("head", None),
    )
    return jax.shard_map(
        functools.partial(on_device, (mesh.shape["queue"], mesh.shape["head"])),
        mesh=mesh,
        in_specs=placed,
        out_specs=P("queue", None, None, "head"),
        check_vma=False,
    )
```

```python
import functools
import math

import jax
import jax.numpy as jnp
from jax import lax
from jax.experimental import pallas as pl
from jax.experimental.pallas import tpu as pltpu
from jax.sharding import PartitionSpec as P

WIN = 4
EPSILON = 1e-06
CHUNKS = 4
LANES = 128
VMEM = 46 << 20
SMALL_VMEM = 32 << 20
BLOCK = 64
COLUMNS = 256
COST = 0.05
KEY, VALUE, QUERY, OUT = range(4)
F32, BF16 = jnp.float32, jnp.bfloat16


def split_dot(values, ones2):
    high = values.astype(BF16)
    low = (values - high.astype(F32)).astype(BF16)
    return jnp.dot(
        jnp.concatenate([high, low], -1), ones2, preferred_element_type=F32
    )


def cost(flops):
    return pl.CostEstimate(flops=int(flops * COST), bytes_accessed=0, transcendentals=0)


def classes_kernel(control, table):
    values = control[...]
    high = values.astype(BF16)
    rest = values - high.astype(F32)
    middle = rest.astype(BF16)
    low = (rest - middle.astype(F32)).astype(BF16)
    table[...] = jnp.concatenate([high, middle, low, jnp.zeros_like(low)], -1)


def class_table(control):
    return pl.pallas_call(
        classes_kernel,
        out_shape=jax.ShapeDtypeStruct((control.shape[0], LANES), BF16),
        compiler_params=pltpu.CompilerParams(vmem_limit_bytes=VMEM),
        name="class_table",
    )(control)


def norm_kernel(place, hidden, other, keypoints, table, mod, normed, mixed):
    half, size = hidden.shape[-2:]
    points = keypoints[pl.ds(pl.program_id(0), 1), :]
    lane = lax.broadcasted_iota(jnp.int32, (LANES, size), 0)
    picks = ((lane % 32 == points) & (lane < 96) & (place[0] == 0)).astype(F32).astype(BF16)
    total = jnp.zeros((1, size), F32)
    for side, values in enumerate((hidden[0, 0], other[0])):
        start = place[0] * half if side == 0 else (1 - place[0]) * half
        rows = pl.ds(pl.multiple_of(start, 64), half)
        control = jnp.dot(table[rows, :], picks, preferred_element_type=F32)
        rounded = (values.astype(F32) + control).astype(BF16)
        mixed[0, rows] = rounded
        total = total + jnp.sum(rounded.astype(F32), 0, keepdims=True)
    centre = total * (1.0 / (2 * half))
    spread = jnp.zeros((1, size), F32)
    for side in range(2):
        part = mixed[0, side * half : (side + 1) * half].astype(F32) - centre
        spread = spread + jnp.sum(part * part, 0, keepdims=True)
    factor = lax.rsqrt(spread * (1.0 / (2 * half)) + EPSILON)
    for tile in range(2 * half // LANES):
        cols = slice(tile * LANES, (tile + 1) * LANES)
        part = ((mixed[0, cols].astype(F32) - centre) * factor).T
        normed[0, :, cols] = (part * (1.0 + mod[1:2, cols]) + mod[0:1, cols]).astype(BF16)


def adaptive_norm(place, hidden, other, keypoints, table, mod, chunk):
    frames, _, half, places = hidden.shape
    size = places // CHUNKS
    width = 2 * half
    grid_spec = pltpu.PrefetchScalarGridSpec(
        num_scalar_prefetch=1,
        grid=(frames,),
        in_specs=[
            pl.BlockSpec((1, 1, half, size), lambda f, s: (f, s[0], 0, chunk)),
            pl.BlockSpec((1, half, size), lambda f, s: (f, 0, 0)),
            pl.BlockSpec((frames, size), lambda f, s: (0, chunk)),
            pl.BlockSpec((width, LANES), lambda f, s: (0, 0)),
            pl.BlockSpec((3, width), lambda f, s: (0, 0)),
        ],
        out_specs=[
            pl.BlockSpec((1, size, width), lambda f, s: (f + s[1] * (3 - 2 * f), 0, 0)),
            pl.BlockSpec((1, width, size), lambda f, s: (f + s[1] * (3 - 2 * f), 0, 0)),
        ],
    )
    return pl.pallas_call(
        norm_kernel,
        grid_spec=grid_spec,
        out_shape=[
            jax.ShapeDtypeStruct((frames, size, width), BF16),
            jax.ShapeDtypeStruct((frames, width, size), BF16),
        ],
        compiler_params=pltpu.CompilerParams(vmem_limit_bytes=SMALL_VMEM),
        cost_estimate=cost(4000 * frames * size * width),
        name="adaptive_norm",
    )(place, hidden, other, keypoints, table, mod)


def order_kernel(place, weight, mover, ordered, piece):
    half = mover.shape[0]
    ordered[...] = jnp.dot(
        mover[...], weight[...].reshape(weight.shape[-2:]), preferred_element_type=F32
    ).astype(BF16)
    piece[...] = ordered[pl.ds(pl.multiple_of(place[1] * (half // 2), 32), half // 2), :]


def order_heads(place, weight, at, mover):
    half, width = weight.shape[-2:]
    if at is None:
        spec = pl.BlockSpec((half, width), lambda i, s: (0, 0))
    else:
        spec = pl.BlockSpec((1, half, width), lambda i, s: (at, 0, 0))
    grid_spec = pltpu.PrefetchScalarGridSpec(
        num_scalar_prefetch=1,
        grid=(1,),
        in_specs=[spec, pl.BlockSpec((half, half), lambda i, s: (0, 0))],
        out_specs=[
            pl.BlockSpec((half, width), lambda i, s: (0, 0)),
            pl.BlockSpec((half // 2, width), lambda i, s: (0, 0)),
        ],
    )
    return pl.pallas_call(
        order_kernel,
        grid_spec=grid_spec,
        out_shape=[
            jax.ShapeDtypeStruct((half, width), BF16),
            jax.ShapeDtypeStruct((half // 2, width), BF16),
        ],
        compiler_params=pltpu.CompilerParams(vmem_limit_bytes=60 << 20),
        cost_estimate=cost(2 * half * half * width),
        name="order_heads",
    )(place, weight, mover)


def dot_rows(values, weight):
    return lax.dot_general(values, weight, (((1,), (1,)), ((), ())), preferred_element_type=F32)


def head_norm(values, gain, ones2, head_dim):
    tiles = values.shape[-1] // LANES
    total = None
    for tile in range(tiles):
        part = values[:, tile * LANES : (tile + 1) * LANES]
        total = part * part if total is None else total + part * part
    factor = lax.rsqrt(split_dot(total, ones2) * (1.0 / head_dim) + EPSILON)
    return [
        (values[:, tile * LANES : (tile + 1) * LANES] * factor
         * gain[:, tile * LANES : (tile + 1) * LANES]).astype(BF16)
        for tile in range(tiles)
    ]


def merge_kernel(place, *refs):
    mine, near, far, (weights, sems) = refs[:4], refs[4:8], refs[8:12], refs[12:]
    part = weights.shape[1] // 2
    copies = []
    for kind in range(4):
        target = weights.at[kind]
        pairs = [
            (mine[kind], target.at[:, 0:32]),
            (near[kind], target.at[pl.ds(place[1] * part, part), 32:64]),
            (far[kind], target.at[pl.ds((1 - place[1]) * part, part), 32:64]),
        ]
        for at, (source, to) in enumerate(pairs):
            copies.append(pltpu.make_async_copy(source, to, sems.at[kind, at]))
            copies[-1].start()
    for copy in copies:
        copy.wait()


def merge_heads(place, mine, near, far):
    half, width = mine[0].shape
    grid_spec = pltpu.PrefetchScalarGridSpec(
        num_scalar_prefetch=1,
        grid=(1,),
        in_specs=[pl.BlockSpec(memory_space=pl.ANY)] * 12,
        out_specs=pl.BlockSpec(memory_space=pltpu.VMEM),
        scratch_shapes=[pltpu.SemaphoreType.DMA((4, 3))],
    )
    return pl.pallas_call(
        merge_kernel,
        grid_spec=grid_spec,
        out_shape=pltpu.VMEM((4, half // 32, 64, width), BF16),
        compiler_params=pltpu.CompilerParams(vmem_limit_bytes=VMEM),
        cost_estimate=cost(8 * half * half * width),
        name="merge_heads",
    )(place, *[weight.reshape(-1, 32, width) for weight in (*mine, *near, *far)])


def block_kernel(
    head_dim, place, own, halo, core, mixed, mod, gains, ones2, weights, carry,
    out, send, rows_in, query, kv, scores, attended, final,
):
    frames, size, width = own.shape
    tiles = width // LANES
    offsets = 2 * WIN + 1
    half = width // 2
    step = pl.program_id(0)
    ones = ones2[...]

    for frame in range(frames):
        rows_in[frame] = halo[frames - 1 - frame]
        rows_in[frames + frame] = own[frame]
        rows_in[2 * frames + frame] = core[frames - 1 - frame]
    reach = 3 * frames * size

    all_rows = rows_in[...].reshape(reach, width)
    edge = width + LANES
    key_value = weights[KEY : VALUE + 1].reshape(2 * width, width)
    keys = dot_rows(all_rows, key_value[0:edge])
    for tile, part in enumerate(head_norm(keys[:, :width], gains[1:2], ones, head_dim)):
        kv[0, :, :, tile * LANES : (tile + 1) * LANES] = part.reshape(3 * frames, size, LANES)
    kv[1, :, :, :LANES] = keys[:, width:].astype(BF16).reshape(3 * frames, size, LANES)
    own_rows = rows_in[frames : 2 * frames].reshape(frames * size, width)
    queries = dot_rows(own_rows, weights[QUERY].reshape(width, width))
    for tile, part in enumerate(head_norm(queries, gains[0:1], ones, head_dim)):
        query[:, :, tile * LANES : (tile + 1) * LANES] = part.reshape(frames, size, LANES)

    def window(kind, frame, rows, cols):
        return kv[kind, frame, rows, cols].astype(F32)

    def score(start, first):
        rows = slice(start, start + 16)
        pair = (first, first + 1)
        sums = {}
        for tile in range(tiles):
            cols = slice(tile * LANES, (tile + 1) * LANES)
            asked = [query[frame, rows, cols].astype(F32) for frame in pair]
            for reached in range(first, first + 1 + offsets):
                key = window(0, reached, rows, cols)
                for frame, one in zip(pair, asked):
                    offset = reached - frame
                    if 0 <= offset < offsets:
                        at = frame * offsets + offset
                        sums[at] = one * key if tile == 0 else sums[at] + one * key
        for at, value in sums.items():
            scores[at, rows] = value

    scale = 1.0 / math.sqrt(head_dim)
    halo_there = place[2] > 0

    def soften(start, frame, sub=32):
        rows = slice(start, start + sub)
        raw = scores[frame * offsets : (frame + 1) * offsets, rows]
        full = split_dot(raw.reshape(offsets * sub, LANES), ones).reshape(
            offsets, sub, LANES
        ) * scale
        parts = [
            jnp.where(halo_there, full[offset], -1e30) if frame + offset < frames else full[offset]
            for offset in range(offsets)
        ]
        highest = functools.reduce(jnp.maximum, parts)
        parts = [jnp.exp(part - highest) for part in parts]
        inverse = 1.0 / functools.reduce(jnp.add, parts)
        for offset, part in enumerate(parts):
            scores[frame * offsets + offset, rows] = (part * inverse).astype(BF16).astype(F32)

    steps = [functools.partial(score, start, first)
             for start in range(0, size, 16) for first in range(0, frames, 2)]
    steps += [functools.partial(soften, start, frame)
              for start in range(0, size, 32) for frame in range(frames)]
    starts = list(range(LANES, width, COLUMNS))
    done = 0
    for at, start in enumerate(starts):
        high = min(start + COLUMNS, width)
        kv[1, :, :, start:high] = dot_rows(
            all_rows, key_value[width + start : width + high]
        ).astype(BF16).reshape(3 * frames, size, high - start)
        until = len(steps) * (at + 1) // len(starts)
        for unit in steps[done:until]:
            unit()
        done = until

    @pl.loop(0, size // 16)
    def _(at):
        rows = pl.ds(pl.multiple_of(at * 16, 16), 16)
        for first in range(0, frames, 2):
            pair = (first, first + 1)
            shares = {
                frame: [scores[frame * offsets + offset, rows] for offset in range(offsets)]
                for frame in pair
            }
            for tile in range(tiles):
                cols = slice(tile * LANES, (tile + 1) * LANES)
                sums = {}
                for reached in range(first, first + 1 + offsets):
                    value = window(1, reached, rows, cols)
                    for frame in pair:
                        offset = reached - frame
                        if 0 <= offset < offsets:
                            term = shares[frame][offset] * value
                            sums[frame] = term if offset == 0 else sums[frame] + term
                for frame in pair:
                    attended[frame, pl.ds(pl.multiple_of(step * size + at * 16, 16), 16), cols] = (
                        sums[frame].astype(BF16)
                    )

    @pl.when(step == pl.num_programs(0) - 1)
    def _():
        places = attended.shape[1]
        own_half = pl.ds(pl.multiple_of(place[0] * half, 64), half)
        send_half = pl.ds(pl.multiple_of((1 - place[0]) * half, 64), half)
        flat = attended[...].reshape(frames * places, width)
        result = jnp.dot(flat, weights[OUT].reshape(width, width), preferred_element_type=F32)
        result = result * mod[2:3, :]
        for frame in range(frames):
            target = frame + place[1] * (3 - 2 * frame)
            for tile in range(tiles):
                cols = slice(tile * LANES, (tile + 1) * LANES)
                turned = result[frame * places : (frame + 1) * places, cols].T
                final[cols] = (mixed[frame, cols].astype(F32) + turned).astype(BF16)
            out[target, 0] = final[own_half]
            send[target] = final[send_half]


def whole_block(place, own, halo, core, mixed, mod, gains, ones2, weights, carry, head_dim,
                chunk, places):
    frames, size, width = own.shape
    half = width // 2
    block = BLOCK
    once = pl.Buffered(1)
    rows = pl.BlockSpec((frames, block, width), lambda p, s: (0, p, 0))
    in_specs = [
        rows, rows, rows,
        pl.BlockSpec((frames, width, size), lambda p, s: (0, 0, 0), pipeline_mode=once),
        pl.BlockSpec((3, width), lambda p, s: (0, 0)),
        pl.BlockSpec((2, width), lambda p, s: (0, 0)),
        pl.BlockSpec((2 * LANES, LANES), lambda p, s: (0, 0)),
    ]
    in_specs.append(pl.BlockSpec(memory_space=pltpu.VMEM))
    weights = pltpu.with_memory_space_constraint(weights, pltpu.VMEM)
    args = [place, own, halo, core, mixed, mod, gains, ones2, weights]
    aliases = {}
    if carry is not None:
        in_specs.append(pl.BlockSpec(memory_space=pl.ANY))
        aliases = {len(args): 0}
        args.append(carry)

    def kernel(*refs):
        block_kernel(head_dim, *refs[:9], None, *refs[9 + len(aliases) :])

    grid_spec = pltpu.PrefetchScalarGridSpec(
        num_scalar_prefetch=1,
        grid=(size // block,),
        in_specs=in_specs,
        out_specs=[
            pl.BlockSpec((frames, 1, half, size), lambda p, s: (0, s[0], 0, chunk)),
            pl.BlockSpec((frames, half, size), lambda p, s: (0, 0, 0)),
        ],
        scratch_shapes=[
            pltpu.VMEM((3 * frames, block, width), BF16),
            pltpu.VMEM((frames, block, width), BF16),
            pltpu.VMEM((2, 3 * frames, block, width), BF16),
            pltpu.VMEM((frames * (2 * WIN + 1), block, LANES), F32),
            pltpu.VMEM((frames, size, width), BF16),
            pltpu.VMEM((width, size), BF16),
        ],
    )
    return pl.pallas_call(
        kernel,
        grid_spec=grid_spec,
        out_shape=[
            jax.ShapeDtypeStruct((frames, 2, half, places), BF16),
            jax.ShapeDtypeStruct((frames, half, size), BF16),
        ],
        input_output_aliases=aliases,
        compiler_params=pltpu.CompilerParams(vmem_limit_bytes=VMEM),
        cost_estimate=cost(36 * frames * size * width * width),
        name="whole_block",
    )(*args)


def on_device(
    mesh_sizes, hidden, keypoints, tsteps, mod_table, ctrl_table, ctrl_proj, w_qkv, q_gain, k_gain,
    w_out,
):
    queue_size, head_size = mesh_sizes
    frames, _, places, half = hidden.shape
    width = 2 * half
    heads, head_dim = q_gain.shape
    classes = ctrl_table.shape[0]
    size = places // CHUNKS
    head = lax.axis_index("head")
    queue = lax.axis_index("queue")
    core = queue % 2
    swap = [(0, 1), (1, 0)]
    across = [
        (2 * q + h, 2 * ((q + queue_size // 2) % queue_size) + 1 - h)
        for q in range(queue_size)
        for h in range(2)
    ]
    cores = [(q, q ^ 1) for q in range(queue_size)]
    halos = [(q, q + 1) for q in range(1, queue_size - 1, 2)]
    halos += [(b, a) for a, b in halos]

    halo_there = ((queue > 0) & (queue < queue_size - 1)).astype(jnp.int32)
    place = jnp.stack([head, core, halo_there]).astype(jnp.int32)
    hidden = hidden.transpose(0, 1, 3, 2)
    w_qkv = w_qkv.transpose(1, 2, 0)

    source = jnp.arange(half)
    mover = (
        source[None, :] == ((source % heads) * head_dim + source // heads)[:, None]
    ).astype(BF16)
    mine, near = [None] * 4, [None] * 4
    mine[KEY], piece = order_heads(place, w_qkv, 1, mover)
    near[KEY] = lax.ppermute(piece, ("queue", "head"), across)

    cut, _ = lax.optimization_barrier((hidden, piece))
    parts = [
        lax.dynamic_slice(
            cut, (0, 1 - head, 0, chunk * size), (frames, 1, half, size)
        ).reshape(frames, half, size)
        for chunk in range(CHUNKS)
    ]
    parts, w_qkv, w_out = lax.optimization_barrier((parts, w_qkv, w_out))

    def after(value, *others):
        return lax.optimization_barrier((value, others))[0]

    arrived = [lax.ppermute(parts[0], "head", swap)]
    pieces = {}
    for kind, weight, at in ((VALUE, w_qkv, 2), (QUERY, w_qkv, 0), (OUT, w_out, None)):
        mine[kind], pieces[kind] = order_heads(place, weight, at, mover)
    near[VALUE] = lax.ppermute(pieces[VALUE], ("queue", "head"), across)
    near[QUERY] = lax.ppermute(after(pieces[QUERY], near[KEY]), ("queue", "head"), across)
    near[OUT] = lax.ppermute(after(pieces[OUT], arrived[0]), "head", swap)
    for chunk in range(1, CHUNKS):
        part = after(parts[chunk], arrived[min(chunk - 1, 1)])
        arrived.append(lax.ppermute(part, "head", swap))

    control = jnp.dot(ctrl_table, ctrl_proj, preferred_element_type=F32)
    small = jnp.concatenate(
        [control, q_gain.T.reshape(1, half), k_gain.T.reshape(1, half)], 0
    )
    small_other = lax.ppermute(small, "head", swap)
    both = jnp.stack([small, small_other])
    gains = both[:, classes:].reshape(2, 2, half // 32, 32).transpose(1, 2, 0, 3).reshape(2, width)
    natural = jnp.where(head == 0, both, both[::-1])[:, :classes]
    natural = natural.transpose(0, 2, 1).reshape(width, classes)
    table = class_table(after(jnp.pad(natural, ((0, 0), (0, 32 - classes))), pieces))
    mod = lax.dynamic_index_in_dim(mod_table, tsteps[0], 0, keepdims=False)
    lane = jnp.arange(LANES)
    row = jnp.arange(2 * LANES)
    ones2 = (
        ((row // 32 % 2)[:, None] == (lane // 32 % 2)[None, :])
        & ((row % 8)[:, None] == (lane % 8)[None, :])
    ).astype(BF16)

    normed, mixed, halo, beside = [], [], [], []

    def prepare(chunk, other):
        one, two = adaptive_norm(place, hidden, other, keypoints, table, mod, chunk)
        normed.append(one)
        mixed.append(two)
        halo.append(lax.ppermute(one, "queue", halos))
        beside.append(lax.ppermute(one, "queue", cores))

    ahead = 2
    prepare(0, after(arrived[0], near[KEY]))
    far = [lax.ppermute(after(piece, normed[0]), "queue", cores) for piece in near]
    prepare(1, after(arrived[1], halo[0], beside[0]))
    weights = merge_heads(place, after(mine, arrived[2]), near, far)
    carry = None
    back = []
    for chunk in range(CHUNKS):
        carry, send = whole_block(
            place, normed[chunk], halo[chunk], beside[chunk], mixed[chunk], mod, gains, ones2, weights,
            carry, head_dim, chunk, places,
        )
        if chunk + ahead < CHUNKS:
            other, send = lax.optimization_barrier((arrived[chunk + ahead], send))
            prepare(chunk + ahead, other)
        back.append(lax.ppermute(send, "head", swap))
    for chunk in range(CHUNKS):
        carry = lax.dynamic_update_slice(
            carry, back[chunk][:, None], (0, 1 - head, 0, chunk * size)
        )
    return carry.transpose(0, 1, 3, 2)


def solution(mesh):
    placed = (
        P("queue", None, None, "head"),
        P("queue", None),
        P("queue"),
        P(),
        P(),
        P(None, "head"),
        P(None, None, "head"),
        P("head", None),
        P("head", None),
        P("head", None),
    )
    return jax.shard_map(
        functools.partial(on_device, (mesh.shape["queue"], mesh.shape["head"])),
        mesh=mesh,
        in_specs=placed,
        out_specs=P("queue", None, None, "head"),
        check_vma=False,
    )
```

```python
import functools
import math

import jax
import jax.numpy as jnp
from jax import lax
from jax.experimental import pallas as pl
from jax.experimental.pallas import tpu as pltpu
from jax.sharding import PartitionSpec as P

WIN = 4
EPSILON = 1e-06
CHUNKS = 4
LANES = 128
VMEM = 46 << 20
SMALL_VMEM = 32 << 20
BLOCK = 64
COLUMNS = 256
COST = 0.05
KEY, VALUE, QUERY, OUT = range(4)
F32, BF16 = jnp.float32, jnp.bfloat16


def split_dot(values, ones2):
    high = values.astype(BF16)
    low = (values - high.astype(F32)).astype(BF16)
    return jnp.dot(
        jnp.concatenate([high, low], -1), ones2, preferred_element_type=F32
    )


def cost(flops):
    return pl.CostEstimate(flops=int(flops * COST), bytes_accessed=0, transcendentals=0)


def classes_kernel(control, table):
    values = control[...]
    high = values.astype(BF16)
    rest = values - high.astype(F32)
    middle = rest.astype(BF16)
    low = (rest - middle.astype(F32)).astype(BF16)
    table[...] = jnp.concatenate([high, middle, low, jnp.zeros_like(low)], -1)


def class_table(control):
    return pl.pallas_call(
        classes_kernel,
        out_shape=jax.ShapeDtypeStruct((control.shape[0], LANES), BF16),
        compiler_params=pltpu.CompilerParams(vmem_limit_bytes=VMEM),
        name="class_table",
    )(control)


def norm_kernel(place, hidden, other, keypoints, table, mod, normed, mixed):
    half, size = hidden.shape[-2:]
    points = keypoints[pl.ds(pl.program_id(0), 1), :]
    lane = lax.broadcasted_iota(jnp.int32, (LANES, size), 0)
    picks = ((lane % 32 == points) & (lane < 96) & (place[0] == 0)).astype(F32).astype(BF16)
    total = jnp.zeros((1, size), F32)
    for side, values in enumerate((hidden[0, 0], other[0])):
        start = place[0] * half if side == 0 else (1 - place[0]) * half
        rows = pl.ds(pl.multiple_of(start, 64), half)
        control = jnp.dot(table[rows, :], picks, preferred_element_type=F32)
        rounded = (values.astype(F32) + control).astype(BF16)
        mixed[0, rows] = rounded
        total = total + jnp.sum(rounded.astype(F32), 0, keepdims=True)
    centre = total * (1.0 / (2 * half))
    spread = jnp.zeros((1, size), F32)
    for side in range(2):
        part = mixed[0, side * half : (side + 1) * half].astype(F32) - centre
        spread = spread + jnp.sum(part * part, 0, keepdims=True)
    factor = lax.rsqrt(spread * (1.0 / (2 * half)) + EPSILON)
    for tile in range(2 * half // LANES):
        cols = slice(tile * LANES, (tile + 1) * LANES)
        part = ((mixed[0, cols].astype(F32) - centre) * factor).T
        normed[0, :, cols] = (part * (1.0 + mod[1:2, cols]) + mod[0:1, cols]).astype(BF16)


def adaptive_norm(place, hidden, other, keypoints, table, mod, chunk):
    frames, _, half, places = hidden.shape
    size = places // CHUNKS
    width = 2 * half
    grid_spec = pltpu.PrefetchScalarGridSpec(
        num_scalar_prefetch=1,
        grid=(frames,),
        in_specs=[
            pl.BlockSpec((1, 1, half, size), lambda f, s: (f, s[0], 0, chunk)),
            pl.BlockSpec((1, half, size), lambda f, s: (f, 0, 0)),
            pl.BlockSpec((frames, size), lambda f, s: (0, chunk)),
            pl.BlockSpec((width, LANES), lambda f, s: (0, 0)),
            pl.BlockSpec((3, width), lambda f, s: (0, 0)),
        ],
        out_specs=[
            pl.BlockSpec((1, size, width), lambda f, s: (f + s[1] * (3 - 2 * f), 0, 0)),
            pl.BlockSpec((1, width, size), lambda f, s: (f + s[1] * (3 - 2 * f), 0, 0)),
        ],
    )
    return pl.pallas_call(
        norm_kernel,
        grid_spec=grid_spec,
        out_shape=[
            jax.ShapeDtypeStruct((frames, size, width), BF16),
            jax.ShapeDtypeStruct((frames, width, size), BF16),
        ],
        compiler_params=pltpu.CompilerParams(vmem_limit_bytes=SMALL_VMEM),
        cost_estimate=cost(4000 * frames * size * width),
        name="adaptive_norm",
    )(place, hidden, other, keypoints, table, mod)


def piece_kernel(place, w_qkv, w_out, mover, piece):
    def write(weight):
        piece[...] = jnp.dot(mover[...], weight, preferred_element_type=F32).astype(BF16)

    @pl.when(place[3] < 3)
    def _():
        write(w_qkv[0])

    @pl.when(place[3] == 3)
    def _():
        write(w_out[...])


def order_kernel(w_qkv, w_out, mover, ordered):
    def write(weight):
        ordered[0] = jnp.dot(mover[...], weight, preferred_element_type=F32).astype(BF16)

    @pl.when(pl.program_id(0) < 3)
    def _():
        write(w_qkv[0])

    @pl.when(pl.program_id(0) == 3)
    def _():
        write(w_out[...])


def order_heads(w_qkv, w_out, mover):
    half, width = w_out.shape
    return pl.pallas_call(
        order_kernel,
        grid=(4,),
        in_specs=[
            pl.BlockSpec((1, half, width), lambda i: ((i + 1) % 3, 0, 0)),
            pl.BlockSpec((half, width), lambda i: (0, 0)),
            pl.BlockSpec((half, half), lambda i: (0, 0)),
        ],
        out_specs=pl.BlockSpec((1, half, width), lambda i: (i, 0, 0)),
        out_shape=jax.ShapeDtypeStruct((4, half, width), BF16),
        compiler_params=pltpu.CompilerParams(vmem_limit_bytes=60 << 20),
        cost_estimate=cost(8 * half * half * width),
        name="order_heads",
    )(w_qkv, w_out, mover)


def piece_of_heads(place, w_qkv, w_out, mover):
    half, width = w_out.shape
    grid_spec = pltpu.PrefetchScalarGridSpec(
        num_scalar_prefetch=1,
        grid=(1,),
        in_specs=[
            pl.BlockSpec((1, half, width), lambda i, s: ((s[3] + 1) % 3, 0, 0)),
            pl.BlockSpec((half, width), lambda i, s: (0, 0)),
            pl.BlockSpec((half // 2, half), lambda i, s: (s[1], 0)),
        ],
        out_specs=pl.BlockSpec((half // 2, width), lambda i, s: (0, 0)),
    )
    return pl.pallas_call(
        piece_kernel,
        grid_spec=grid_spec,
        out_shape=jax.ShapeDtypeStruct((half // 2, width), BF16),
        compiler_params=pltpu.CompilerParams(vmem_limit_bytes=60 << 20),
        cost_estimate=cost(half * half * width),
        name="piece_of_heads",
    )(place, w_qkv, w_out, mover)


def dot_rows(values, weight):
    return lax.dot_general(values, weight, (((1,), (1,)), ((), ())), preferred_element_type=F32)


def head_norm(values, gain, ones2, head_dim):
    tiles = values.shape[-1] // LANES
    total = None
    for tile in range(tiles):
        part = values[:, tile * LANES : (tile + 1) * LANES]
        total = part * part if total is None else total + part * part
    factor = lax.rsqrt(split_dot(total, ones2) * (1.0 / head_dim) + EPSILON)
    return [
        (values[:, tile * LANES : (tile + 1) * LANES] * factor
         * gain[:, tile * LANES : (tile + 1) * LANES]).astype(BF16)
        for tile in range(tiles)
    ]


def merge_kernel(place, mine, others, weights, sems):
    copies = []
    for kind in range(4):
        for at, source in enumerate((mine, others)):
            copies.append(
                pltpu.make_async_copy(
                    source.at[kind],
                    weights.at[kind, :, at * 32 : at * 32 + 32],
                    sems.at[kind, at],
                )
            )
            copies[-1].start()
    for copy in copies:
        copy.wait()


def merge_heads(place, mine, others):
    _, half, width = mine.shape
    grid_spec = pltpu.PrefetchScalarGridSpec(
        num_scalar_prefetch=1,
        grid=(1,),
        in_specs=[pl.BlockSpec(memory_space=pl.ANY)] * 2,
        out_specs=pl.BlockSpec(memory_space=pltpu.VMEM),
        scratch_shapes=[pltpu.SemaphoreType.DMA((4, 2))],
    )
    return pl.pallas_call(
        merge_kernel,
        grid_spec=grid_spec,
        out_shape=pltpu.VMEM((4, half // 32, 64, width), BF16),
        compiler_params=pltpu.CompilerParams(vmem_limit_bytes=VMEM),
        cost_estimate=cost(8 * half * half * width),
        name="merge_heads",
    )(place, mine.reshape(4, -1, 32, width), others.reshape(4, -1, 32, width))


def block_kernel(
    head_dim, place, own, halo, core, mixed, mod, gains, ones2, weights, carry,
    out, send, rows_in, query, kv, scores, attended, final,
):
    frames, size, width = own.shape
    tiles = width // LANES
    offsets = 2 * WIN + 1
    half = width // 2
    step = pl.program_id(0)
    ones = ones2[...]

    for frame in range(frames):
        rows_in[frame] = halo[frames - 1 - frame]
        rows_in[frames + frame] = own[frame]
        rows_in[2 * frames + frame] = core[frames - 1 - frame]
    reach = 3 * frames * size

    all_rows = rows_in[...].reshape(reach, width)
    edge = width + LANES
    key_value = weights[KEY : VALUE + 1].reshape(2 * width, width)
    keys = dot_rows(all_rows, key_value[0:edge])
    for tile, part in enumerate(head_norm(keys[:, :width], gains[1:2], ones, head_dim)):
        kv[0, :, :, tile * LANES : (tile + 1) * LANES] = part.reshape(3 * frames, size, LANES)
    kv[1, :, :, :LANES] = keys[:, width:].astype(BF16).reshape(3 * frames, size, LANES)
    own_rows = rows_in[frames : 2 * frames].reshape(frames * size, width)
    queries = dot_rows(own_rows, weights[QUERY].reshape(width, width))
    for tile, part in enumerate(head_norm(queries, gains[0:1], ones, head_dim)):
        query[:, :, tile * LANES : (tile + 1) * LANES] = part.reshape(frames, size, LANES)

    def window(kind, frame, rows, cols):
        return kv[kind, frame, rows, cols].astype(F32)

    def score(start, first):
        rows = slice(start, start + 16)
        pair = (first, first + 1)
        sums = {}
        for tile in range(tiles):
            cols = slice(tile * LANES, (tile + 1) * LANES)
            asked = [query[frame, rows, cols].astype(F32) for frame in pair]
            for reached in range(first, first + 1 + offsets):
                key = window(0, reached, rows, cols)
                for frame, one in zip(pair, asked):
                    offset = reached - frame
                    if 0 <= offset < offsets:
                        at = frame * offsets + offset
                        sums[at] = one * key if tile == 0 else sums[at] + one * key
        for at, value in sums.items():
            scores[at, rows] = value

    scale = 1.0 / math.sqrt(head_dim)
    halo_there = place[2] > 0

    def soften(start, frame, sub=32):
        rows = slice(start, start + sub)
        raw = scores[frame * offsets : (frame + 1) * offsets, rows]
        full = split_dot(raw.reshape(offsets * sub, LANES), ones).reshape(
            offsets, sub, LANES
        ) * scale
        parts = [
            jnp.where(halo_there, full[offset], -1e30) if frame + offset < frames else full[offset]
            for offset in range(offsets)
        ]
        highest = functools.reduce(jnp.maximum, parts)
        parts = [jnp.exp(part - highest) for part in parts]
        inverse = 1.0 / functools.reduce(jnp.add, parts)
        for offset, part in enumerate(parts):
            scores[frame * offsets + offset, rows] = (part * inverse).astype(BF16).astype(F32)

    steps = [functools.partial(score, start, first)
             for start in range(0, size, 16) for first in range(0, frames, 2)]
    steps += [functools.partial(soften, start, frame)
              for start in range(0, size, 32) for frame in range(frames)]
    starts = list(range(LANES, width, COLUMNS))
    done = 0
    for at, start in enumerate(starts):
        high = min(start + COLUMNS, width)
        kv[1, :, :, start:high] = dot_rows(
            all_rows, key_value[width + start : width + high]
        ).astype(BF16).reshape(3 * frames, size, high - start)
        until = len(steps) * (at + 1) // len(starts)
        for unit in steps[done:until]:
            unit()
        done = until

    @pl.loop(0, size // 16)
    def _(at):
        rows = pl.ds(pl.multiple_of(at * 16, 16), 16)
        for first in range(0, frames, 2):
            pair = (first, first + 1)
            shares = {
                frame: [scores[frame * offsets + offset, rows] for offset in range(offsets)]
                for frame in pair
            }
            for tile in range(tiles):
                cols = slice(tile * LANES, (tile + 1) * LANES)
                sums = {}
                for reached in range(first, first + 1 + offsets):
                    value = window(1, reached, rows, cols)
                    for frame in pair:
                        offset = reached - frame
                        if 0 <= offset < offsets:
                            term = shares[frame][offset] * value
                            sums[frame] = term if offset == 0 else sums[frame] + term
                for frame in pair:
                    attended[frame, pl.ds(pl.multiple_of(step * size + at * 16, 16), 16), cols] = (
                        sums[frame].astype(BF16)
                    )

    @pl.when(step == pl.num_programs(0) - 1)
    def _():
        places = attended.shape[1]
        own_half = pl.ds(pl.multiple_of(place[0] * half, 64), half)
        send_half = pl.ds(pl.multiple_of((1 - place[0]) * half, 64), half)
        flat = attended[...].reshape(frames * places, width)
        result = jnp.dot(flat, weights[OUT].reshape(width, width), preferred_element_type=F32)
        result = result * mod[2:3, :]
        for frame in range(frames):
            target = frame + place[1] * (3 - 2 * frame)
            for tile in range(tiles):
                cols = slice(tile * LANES, (tile + 1) * LANES)
                turned = result[frame * places : (frame + 1) * places, cols].T
                final[cols] = (mixed[frame, cols].astype(F32) + turned).astype(BF16)
            out[target, 0] = final[own_half]
            send[target] = final[send_half]


def whole_block(place, own, halo, core, mixed, mod, gains, ones2, weights, carry, head_dim,
                chunk, places):
    frames, size, width = own.shape
    half = width // 2
    block = BLOCK
    once = pl.Buffered(1)
    rows = pl.BlockSpec((frames, block, width), lambda p, s: (0, p, 0))
    in_specs = [
        rows, rows, rows,
        pl.BlockSpec((frames, width, size), lambda p, s: (0, 0, 0), pipeline_mode=once),
        pl.BlockSpec((3, width), lambda p, s: (0, 0)),
        pl.BlockSpec((2, width), lambda p, s: (0, 0)),
        pl.BlockSpec((2 * LANES, LANES), lambda p, s: (0, 0)),
    ]
    in_specs.append(pl.BlockSpec(memory_space=pltpu.VMEM))
    weights = pltpu.with_memory_space_constraint(weights, pltpu.VMEM)
    args = [place, own, halo, core, mixed, mod, gains, ones2, weights]
    aliases = {}
    if carry is not None:
        in_specs.append(pl.BlockSpec(memory_space=pl.ANY))
        aliases = {len(args): 0}
        args.append(carry)

    def kernel(*refs):
        block_kernel(head_dim, *refs[:9], None, *refs[9 + len(aliases) :])

    grid_spec = pltpu.PrefetchScalarGridSpec(
        num_scalar_prefetch=1,
        grid=(size // block,),
        in_specs=in_specs,
        out_specs=[
            pl.BlockSpec((frames, 1, half, size), lambda p, s: (0, s[0], 0, chunk)),
            pl.BlockSpec((frames, half, size), lambda p, s: (0, 0, 0)),
        ],
        scratch_shapes=[
            pltpu.VMEM((3 * frames, block, width), BF16),
            pltpu.VMEM((frames, block, width), BF16),
            pltpu.VMEM((2, 3 * frames, block, width), BF16),
            pltpu.VMEM((frames * (2 * WIN + 1), block, LANES), F32),
            pltpu.VMEM((frames, size, width), BF16),
            pltpu.VMEM((width, size), BF16),
        ],
    )
    return pl.pallas_call(
        kernel,
        grid_spec=grid_spec,
        out_shape=[
            jax.ShapeDtypeStruct((frames, 2, half, places), BF16),
            jax.ShapeDtypeStruct((frames, half, size), BF16),
        ],
        input_output_aliases=aliases,
        compiler_params=pltpu.CompilerParams(vmem_limit_bytes=VMEM),
        cost_estimate=cost(36 * frames * size * width * width),
        name="whole_block",
    )(*args)


def on_device(
    mesh_sizes, hidden, keypoints, tsteps, mod_table, ctrl_table, ctrl_proj, w_qkv, q_gain, k_gain,
    w_out,
):
    queue_size, head_size = mesh_sizes
    frames, _, places, half = hidden.shape
    width = 2 * half
    heads, head_dim = q_gain.shape
    classes = ctrl_table.shape[0]
    size = places // CHUNKS
    head = lax.axis_index("head")
    queue = lax.axis_index("queue")
    core = queue % 2
    swap = [(0, 1), (1, 0)]
    across = [
        (2 * q + h, 2 * ((q + queue_size // 2) % queue_size) + 1 - h)
        for q in range(queue_size)
        for h in range(2)
    ]
    cores = [(q, q ^ 1) for q in range(queue_size)]
    halos = [(q, q + 1) for q in range(1, queue_size - 1, 2)]
    halos += [(b, a) for a, b in halos]

    halo_there = ((queue > 0) & (queue < queue_size - 1)).astype(jnp.int32)
    place = jnp.stack([head, core, halo_there, queue // 8 % 4]).astype(jnp.int32)
    hidden = hidden.transpose(0, 1, 3, 2)
    w_qkv = w_qkv.transpose(1, 2, 0)

    def after(value, *others):
        return lax.optimization_barrier((value, others))[0]

    source = jnp.arange(half)
    mover = (
        source[None, :] == ((source % heads) * head_dim + source // heads)[:, None]
    ).astype(BF16)
    piece = piece_of_heads(place, w_qkv, w_out, mover)
    eighth = lax.ppermute(piece, ("queue", "head"), across)
    sharers = [
        [((top * 4 + x) * 4 + y) * 2 + c for x in range(4) for c in range(2)]
        for top in range(queue_size // 32)
        for y in range(4)
    ]

    cut = after(hidden, piece)
    parts = [
        lax.dynamic_slice(
            cut, (0, 1 - head, 0, chunk * size), (frames, 1, half, size)
        ).reshape(frames, half, size)
        for chunk in range(CHUNKS)
    ]
    arrived = [lax.ppermute(part, "head", swap) for part in parts[:2]]
    for part in after(parts[2:], arrived[0]):
        arrived.append(lax.ppermute(part, "head", swap))
    w_qkv, w_out = after((w_qkv, w_out), parts)
    mine = order_heads(w_qkv, w_out, mover)

    control = jnp.dot(ctrl_table, ctrl_proj, preferred_element_type=F32)
    small = jnp.concatenate(
        [control, q_gain.T.reshape(1, half), k_gain.T.reshape(1, half)], 0
    )
    small_other = lax.ppermute(small, "head", swap)
    both = jnp.stack([small, small_other])
    gains = both[:, classes:].reshape(2, 2, half // 32, 32).transpose(1, 2, 0, 3).reshape(2, width)
    natural = jnp.where(head == 0, both, both[::-1])[:, :classes]
    natural = natural.transpose(0, 2, 1).reshape(width, classes)
    table = class_table(after(jnp.pad(natural, ((0, 0), (0, 32 - classes))), mine))
    eighth = after(eighth, arrived[0], table)
    others = lax.all_gather(eighth, "queue", axis=0, tiled=True, axis_index_groups=sharers)
    mod = lax.dynamic_index_in_dim(mod_table, tsteps[0], 0, keepdims=False)
    lane = jnp.arange(LANES)
    row = jnp.arange(2 * LANES)
    ones2 = (
        ((row // 32 % 2)[:, None] == (lane // 32 % 2)[None, :])
        & ((row % 8)[:, None] == (lane % 8)[None, :])
    ).astype(BF16)

    normed, mixed, halo, beside = [], [], [], []

    def prepare(chunk, other):
        one, two = adaptive_norm(place, hidden, other, keypoints, table, mod, chunk)
        normed.append(one)
        mixed.append(two)
        halo.append(lax.ppermute(one, "queue", halos))
        beside.append(lax.ppermute(one, "queue", cores))

    ahead = 2
    prepare(0, arrived[0])
    prepare(1, arrived[1])
    others, mine = after((others, mine), normed[1])
    weights = merge_heads(place, mine, others)
    carry = None
    back = []
    for chunk in range(CHUNKS):
        carry, send = whole_block(
            place, normed[chunk], halo[chunk], beside[chunk], mixed[chunk], mod, gains, ones2, weights,
            carry, head_dim, chunk, places,
        )
        if chunk + ahead < CHUNKS:
            other, send = lax.optimization_barrier((arrived[chunk + ahead], send))
            prepare(chunk + ahead, other)
        back.append(lax.ppermute(send, "head", swap))
    for chunk in range(CHUNKS):
        carry = lax.dynamic_update_slice(
            carry, back[chunk][:, None], (0, 1 - head, 0, chunk * size)
        )
    return carry.transpose(0, 1, 3, 2)


def solution(mesh):
    placed = (
        P("queue", None, None, "head"),
        P("queue", None),
        P("queue"),
        P(),
        P(),
        P(None, "head"),
        P(None, None, "head"),
        P("head", None),
        P("head", None),
        P("head", None),
    )
    return jax.shard_map(
        functools.partial(on_device, (mesh.shape["queue"], mesh.shape["head"])),
        mesh=mesh,
        in_specs=placed,
        out_specs=P("queue", None, None, "head"),
        check_vma=False,
    )
```

```python
import functools
import math

import jax
import jax.numpy as jnp
from jax import lax
from jax.experimental import pallas as pl
from jax.experimental.pallas import tpu as pltpu
from jax.sharding import PartitionSpec as P

WIN = 4
EPSILON = 1e-06
CHUNKS = 4
LANES = 128
VMEM = 46 << 20
SMALL_VMEM = 32 << 20
BLOCK = 64
COLUMNS = 256
COST = 0.05
KEY, VALUE, QUERY, OUT = range(4)
F32, BF16 = jnp.float32, jnp.bfloat16


def split_dot(values, ones2):
    high = values.astype(BF16)
    low = (values - high.astype(F32)).astype(BF16)
    return jnp.dot(
        jnp.concatenate([high, low], -1), ones2, preferred_element_type=F32
    )


def cost(flops):
    return pl.CostEstimate(flops=int(flops * COST), bytes_accessed=0, transcendentals=0)


def classes_kernel(control, table):
    values = control[...]
    high = values.astype(BF16)
    rest = values - high.astype(F32)
    middle = rest.astype(BF16)
    low = (rest - middle.astype(F32)).astype(BF16)
    table[...] = jnp.concatenate([high, middle, low, jnp.zeros_like(low)], -1)


def class_table(control):
    return pl.pallas_call(
        classes_kernel,
        out_shape=jax.ShapeDtypeStruct((control.shape[0], LANES), BF16),
        compiler_params=pltpu.CompilerParams(vmem_limit_bytes=VMEM),
        name="class_table",
    )(control)


def norm_kernel(place, hidden, other, keypoints, table, mod, normed, mixed):
    half, size = hidden.shape[-2:]
    points = keypoints[pl.ds(pl.program_id(0), 1), :]
    lane = lax.broadcasted_iota(jnp.int32, (LANES, size), 0)
    picks = ((lane % 32 == points) & (lane < 96) & (place[0] == 0)).astype(F32).astype(BF16)
    total = jnp.zeros((1, size), F32)
    for side, values in enumerate((hidden[0, 0], other[0])):
        start = place[0] * half if side == 0 else (1 - place[0]) * half
        rows = pl.ds(pl.multiple_of(start, 64), half)
        control = jnp.dot(table[rows, :], picks, preferred_element_type=F32)
        rounded = (values.astype(F32) + control).astype(BF16)
        mixed[0, rows] = rounded
        total = total + jnp.sum(rounded.astype(F32), 0, keepdims=True)
    centre = total * (1.0 / (2 * half))
    spread = jnp.zeros((1, size), F32)
    for side in range(2):
        part = mixed[0, side * half : (side + 1) * half].astype(F32) - centre
        spread = spread + jnp.sum(part * part, 0, keepdims=True)
    factor = lax.rsqrt(spread * (1.0 / (2 * half)) + EPSILON)
    for tile in range(2 * half // LANES):
        cols = slice(tile * LANES, (tile + 1) * LANES)
        part = ((mixed[0, cols].astype(F32) - centre) * factor).T
        normed[0, :, cols] = (part * (1.0 + mod[1:2, cols]) + mod[0:1, cols]).astype(BF16)


def adaptive_norm(place, hidden, other, keypoints, table, mod, chunk):
    frames, _, half, places = hidden.shape
    size = places // CHUNKS
    width = 2 * half
    grid_spec = pltpu.PrefetchScalarGridSpec(
        num_scalar_prefetch=1,
        grid=(frames,),
        in_specs=[
            pl.BlockSpec((1, 1, half, size), lambda f, s: (f, s[0], 0, chunk)),
            pl.BlockSpec((1, half, size), lambda f, s: (f, 0, 0)),
            pl.BlockSpec((frames, size), lambda f, s: (0, chunk)),
            pl.BlockSpec((width, LANES), lambda f, s: (0, 0)),
            pl.BlockSpec((3, width), lambda f, s: (0, 0)),
        ],
        out_specs=[
            pl.BlockSpec((1, size, width), lambda f, s: (f + s[1] * (3 - 2 * f), 0, 0)),
            pl.BlockSpec((1, width, size), lambda f, s: (f + s[1] * (3 - 2 * f), 0, 0)),
        ],
    )
    return pl.pallas_call(
        norm_kernel,
        grid_spec=grid_spec,
        out_shape=[
            jax.ShapeDtypeStruct((frames, size, width), BF16),
            jax.ShapeDtypeStruct((frames, width, size), BF16),
        ],
        compiler_params=pltpu.CompilerParams(vmem_limit_bytes=SMALL_VMEM),
        cost_estimate=cost(4000 * frames * size * width),
        name="adaptive_norm",
    )(place, hidden, other, keypoints, table, mod)


def piece_kernel(place, w_qkv, w_out, mover, first, second):
    step = pl.program_id(0)
    kind = place[3] * 2 + step

    def write(weight):
        rows = jnp.dot(mover[...], weight, preferred_element_type=F32).astype(BF16)

        @pl.when(step == 0)
        def _():
            first[...] = rows

        @pl.when(step == 1)
        def _():
            second[...] = rows

    @pl.when(kind < 3)
    def _():
        write(w_qkv[0])

    @pl.when(kind == 3)
    def _():
        write(w_out[...])


def order_kernel(w_qkv, w_out, mover, ordered):
    def write(weight):
        ordered[0] = jnp.dot(mover[...], weight, preferred_element_type=F32).astype(BF16)

    @pl.when(pl.program_id(0) < 3)
    def _():
        write(w_qkv[0])

    @pl.when(pl.program_id(0) == 3)
    def _():
        write(w_out[...])


def order_heads(w_qkv, w_out, mover):
    half, width = w_out.shape
    return pl.pallas_call(
        order_kernel,
        grid=(4,),
        in_specs=[
            pl.BlockSpec((1, half, width), lambda i: ((i + 1) % 3, 0, 0)),
            pl.BlockSpec((half, width), lambda i: (0, 0)),
            pl.BlockSpec((half, half), lambda i: (0, 0)),
        ],
        out_specs=pl.BlockSpec((1, half, width), lambda i: (i, 0, 0)),
        out_shape=jax.ShapeDtypeStruct((4, half, width), BF16),
        compiler_params=pltpu.CompilerParams(vmem_limit_bytes=60 << 20),
        cost_estimate=cost(8 * half * half * width),
        name="order_heads",
    )(w_qkv, w_out, mover)


def pieces_of_heads(place, w_qkv, w_out, mover):
    half, width = w_out.shape
    piece = pl.BlockSpec((half // 2, width), lambda i, s: (0, 0))
    grid_spec = pltpu.PrefetchScalarGridSpec(
        num_scalar_prefetch=1,
        grid=(2,),
        in_specs=[
            pl.BlockSpec((1, half, width), lambda i, s: ((s[3] * 2 + i + 1) % 3, 0, 0)),
            pl.BlockSpec((half, width), lambda i, s: (0, 0)),
            pl.BlockSpec((half // 2, half), lambda i, s: (s[1], 0)),
        ],
        out_specs=[piece, piece],
    )
    return pl.pallas_call(
        piece_kernel,
        grid_spec=grid_spec,
        out_shape=[jax.ShapeDtypeStruct((half // 2, width), BF16)] * 2,
        compiler_params=pltpu.CompilerParams(vmem_limit_bytes=60 << 20),
        cost_estimate=cost(half * half * width),
        name="pieces_of_heads",
    )(place, w_qkv, w_out, mover)


def dot_rows(values, weight):
    return lax.dot_general(values, weight, (((1,), (1,)), ((), ())), preferred_element_type=F32)


def head_norm(values, gain, ones2, head_dim):
    tiles = values.shape[-1] // LANES
    total = None
    for tile in range(tiles):
        part = values[:, tile * LANES : (tile + 1) * LANES]
        total = part * part if total is None else total + part * part
    factor = lax.rsqrt(split_dot(total, ones2) * (1.0 / head_dim) + EPSILON)
    return [
        (values[:, tile * LANES : (tile + 1) * LANES] * factor
         * gain[:, tile * LANES : (tile + 1) * LANES]).astype(BF16)
        for tile in range(tiles)
    ]


def merge_kernel(place, *refs):
    mine, fetched, (weights, sems) = refs[0], refs[1:9], refs[9:]
    part = weights.shape[1] // 2
    copies = []

    def copy(source, to):
        copies.append(pltpu.make_async_copy(source, to, sems.at[len(copies)]))
        copies[-1].start()

    for kind in range(4):
        copy(mine.at[kind], weights.at[kind, :, 0:32])
    for at, source in enumerate(fetched):
        group = place[3] if at % 4 < 2 else 1 - place[3]
        core = place[1] if at < 4 else 1 - place[1]
        copy(source, weights.at[group * 2 + at % 2, pl.ds(core * part, part), 32:64])
    for one in copies:
        one.wait()


def merge_heads(place, mine, fetched):
    _, half, width = mine.shape
    grid_spec = pltpu.PrefetchScalarGridSpec(
        num_scalar_prefetch=1,
        grid=(1,),
        in_specs=[pl.BlockSpec(memory_space=pl.ANY)] * 9,
        out_specs=pl.BlockSpec(memory_space=pltpu.VMEM),
        scratch_shapes=[pltpu.SemaphoreType.DMA((12,))],
    )
    return pl.pallas_call(
        merge_kernel,
        grid_spec=grid_spec,
        out_shape=pltpu.VMEM((4, half // 32, 64, width), BF16),
        compiler_params=pltpu.CompilerParams(vmem_limit_bytes=VMEM),
        cost_estimate=cost(8 * half * half * width),
        name="merge_heads",
    )(place, mine.reshape(4, -1, 32, width), *[one.reshape(-1, 32, width) for one in fetched])


def block_kernel(
    head_dim, place, own, halo, core, mixed, mod, gains, ones2, weights, carry,
    out, send, rows_in, query, kv, scores, attended, final,
):
    frames, size, width = own.shape
    tiles = width // LANES
    offsets = 2 * WIN + 1
    half = width // 2
    step = pl.program_id(0)
    ones = ones2[...]

    for frame in range(frames):
        rows_in[frame] = halo[frames - 1 - frame]
        rows_in[frames + frame] = own[frame]
        rows_in[2 * frames + frame] = core[frames - 1 - frame]
    reach = 3 * frames * size

    all_rows = rows_in[...].reshape(reach, width)
    edge = width + LANES
    key_value = weights[KEY : VALUE + 1].reshape(2 * width, width)
    keys = dot_rows(all_rows, key_value[0:edge])
    for tile, part in enumerate(head_norm(keys[:, :width], gains[1:2], ones, head_dim)):
        kv[0, :, :, tile * LANES : (tile + 1) * LANES] = part.reshape(3 * frames, size, LANES)
    kv[1, :, :, :LANES] = keys[:, width:].astype(BF16).reshape(3 * frames, size, LANES)
    own_rows = rows_in[frames : 2 * frames].reshape(frames * size, width)
    queries = dot_rows(own_rows, weights[QUERY].reshape(width, width))
    for tile, part in enumerate(head_norm(queries, gains[0:1], ones, head_dim)):
        query[:, :, tile * LANES : (tile + 1) * LANES] = part.reshape(frames, size, LANES)

    def window(kind, frame, rows, cols):
        return kv[kind, frame, rows, cols].astype(F32)

    def score(start, first):
        rows = slice(start, start + 16)
        pair = (first, first + 1)
        sums = {}
        for tile in range(tiles):
            cols = slice(tile * LANES, (tile + 1) * LANES)
            asked = [query[frame, rows, cols].astype(F32) for frame in pair]
            for reached in range(first, first + 1 + offsets):
                key = window(0, reached, rows, cols)
                for frame, one in zip(pair, asked):
                    offset = reached - frame
                    if 0 <= offset < offsets:
                        at = frame * offsets + offset
                        sums[at] = one * key if tile == 0 else sums[at] + one * key
        for at, value in sums.items():
            scores[at, rows] = value

    scale = 1.0 / math.sqrt(head_dim)
    halo_there = place[2] > 0

    def soften(start, frame, sub=32):
        rows = slice(start, start + sub)
        raw = scores[frame * offsets : (frame + 1) * offsets, rows]
        full = split_dot(raw.reshape(offsets * sub, LANES), ones).reshape(
            offsets, sub, LANES
        ) * scale
        parts = [
            jnp.where(halo_there, full[offset], -1e30) if frame + offset < frames else full[offset]
            for offset in range(offsets)
        ]
        highest = functools.reduce(jnp.maximum, parts)
        parts = [jnp.exp(part - highest) for part in parts]
        inverse = 1.0 / functools.reduce(jnp.add, parts)
        for offset, part in enumerate(parts):
            scores[frame * offsets + offset, rows] = (part * inverse).astype(BF16).astype(F32)

    steps = [functools.partial(score, start, first)
             for start in range(0, size, 16) for first in range(0, frames, 2)]
    steps += [functools.partial(soften, start, frame)
              for start in range(0, size, 32) for frame in range(frames)]
    starts = list(range(LANES, width, COLUMNS))
    done = 0
    for at, start in enumerate(starts):
        high = min(start + COLUMNS, width)
        kv[1, :, :, start:high] = dot_rows(
            all_rows, key_value[width + start : width + high]
        ).astype(BF16).reshape(3 * frames, size, high - start)
        until = len(steps) * (at + 1) // len(starts)
        for unit in steps[done:until]:
            unit()
        done = until

    @pl.loop(0, size // 16)
    def _(at):
        rows = pl.ds(pl.multiple_of(at * 16, 16), 16)
        for first in range(0, frames, 2):
            pair = (first, first + 1)
            shares = {
                frame: [scores[frame * offsets + offset, rows] for offset in range(offsets)]
                for frame in pair
            }
            for tile in range(tiles):
                cols = slice(tile * LANES, (tile + 1) * LANES)
                sums = {}
                for reached in range(first, first + 1 + offsets):
                    value = window(1, reached, rows, cols)
                    for frame in pair:
                        offset = reached - frame
                        if 0 <= offset < offsets:
                            term = shares[frame][offset] * value
                            sums[frame] = term if offset == 0 else sums[frame] + term
                for frame in pair:
                    attended[frame, pl.ds(pl.multiple_of(step * size + at * 16, 16), 16), cols] = (
                        sums[frame].astype(BF16)
                    )

    @pl.when(step == pl.num_programs(0) - 1)
    def _():
        places = attended.shape[1]
        own_half = pl.ds(pl.multiple_of(place[0] * half, 64), half)
        send_half = pl.ds(pl.multiple_of((1 - place[0]) * half, 64), half)
        flat = attended[...].reshape(frames * places, width)
        result = jnp.dot(flat, weights[OUT].reshape(width, width), preferred_element_type=F32)
        result = result * mod[2:3, :]
        for frame in range(frames):
            target = frame + place[1] * (3 - 2 * frame)
            for tile in range(tiles):
                cols = slice(tile * LANES, (tile + 1) * LANES)
                turned = result[frame * places : (frame + 1) * places, cols].T
                final[cols] = (mixed[frame, cols].astype(F32) + turned).astype(BF16)
            out[target, 0] = final[own_half]
            send[target] = final[send_half]


def whole_block(place, own, halo, core, mixed, mod, gains, ones2, weights, carry, head_dim,
                chunk, places):
    frames, size, width = own.shape
    half = width // 2
    block = BLOCK
    once = pl.Buffered(1)
    rows = pl.BlockSpec((frames, block, width), lambda p, s: (0, p, 0))
    in_specs = [
        rows, rows, rows,
        pl.BlockSpec((frames, width, size), lambda p, s: (0, 0, 0), pipeline_mode=once),
        pl.BlockSpec((3, width), lambda p, s: (0, 0)),
        pl.BlockSpec((2, width), lambda p, s: (0, 0)),
        pl.BlockSpec((2 * LANES, LANES), lambda p, s: (0, 0)),
    ]
    in_specs.append(pl.BlockSpec(memory_space=pltpu.VMEM))
    weights = pltpu.with_memory_space_constraint(weights, pltpu.VMEM)
    args = [place, own, halo, core, mixed, mod, gains, ones2, weights]
    aliases = {}
    if carry is not None:
        in_specs.append(pl.BlockSpec(memory_space=pl.ANY))
        aliases = {len(args): 0}
        args.append(carry)

    def kernel(*refs):
        block_kernel(head_dim, *refs[:9], None, *refs[9 + len(aliases) :])

    grid_spec = pltpu.PrefetchScalarGridSpec(
        num_scalar_prefetch=1,
        grid=(size // block,),
        in_specs=in_specs,
        out_specs=[
            pl.BlockSpec((frames, 1, half, size), lambda p, s: (0, s[0], 0, chunk)),
            pl.BlockSpec((frames, half, size), lambda p, s: (0, 0, 0)),
        ],
        scratch_shapes=[
            pltpu.VMEM((3 * frames, block, width), BF16),
            pltpu.VMEM((frames, block, width), BF16),
            pltpu.VMEM((2, 3 * frames, block, width), BF16),
            pltpu.VMEM((frames * (2 * WIN + 1), block, LANES), F32),
            pltpu.VMEM((frames, size, width), BF16),
            pltpu.VMEM((width, size), BF16),
        ],
    )
    return pl.pallas_call(
        kernel,
        grid_spec=grid_spec,
        out_shape=[
            jax.ShapeDtypeStruct((frames, 2, half, places), BF16),
            jax.ShapeDtypeStruct((frames, half, size), BF16),
        ],
        input_output_aliases=aliases,
        compiler_params=pltpu.CompilerParams(vmem_limit_bytes=VMEM),
        cost_estimate=cost(36 * frames * size * width * width),
        name="whole_block",
    )(*args)


def on_device(
    mesh_sizes, hidden, keypoints, tsteps, mod_table, ctrl_table, ctrl_proj, w_qkv, q_gain, k_gain,
    w_out,
):
    queue_size, head_size = mesh_sizes
    frames, _, places, half = hidden.shape
    width = 2 * half
    heads, head_dim = q_gain.shape
    classes = ctrl_table.shape[0]
    size = places // CHUNKS
    head = lax.axis_index("head")
    queue = lax.axis_index("queue")
    core = queue % 2
    swap = [(0, 1), (1, 0)]
    across = [
        (2 * q + h, 2 * ((q + queue_size // 2) % queue_size) + 1 - h)
        for q in range(queue_size)
        for h in range(2)
    ]
    cores = [(q, q ^ 1) for q in range(queue_size)]
    halos = [(q, q + 1) for q in range(1, queue_size - 1, 2)]
    halos += [(b, a) for a, b in halos]

    halo_there = ((queue > 0) & (queue < queue_size - 1)).astype(jnp.int32)
    place = jnp.stack([head, core, halo_there, queue // 8 % 2]).astype(jnp.int32)
    hidden = hidden.transpose(0, 1, 3, 2)
    w_qkv = w_qkv.transpose(1, 2, 0)

    def after(value, *others):
        return lax.optimization_barrier((value, others))[0]

    source = jnp.arange(half)
    mover = (
        source[None, :] == ((source % heads) * head_dim + source // heads)[:, None]
    ).astype(BF16)
    pieces = pieces_of_heads(place, w_qkv, w_out, mover)
    fetched = [lax.ppermute(piece, ("queue", "head"), across) for piece in pieces]
    sides = [
        [(q, q ^ 8) for q in range(queue_size)],
        [(q, q // 32 * 32 + (q + (8 if q // 8 % 2 else 24)) % 32) for q in range(queue_size)],
    ]

    cut = after(hidden, pieces)
    parts = [
        lax.dynamic_slice(
            cut, (0, 1 - head, 0, chunk * size), (frames, 1, half, size)
        ).reshape(frames, half, size)
        for chunk in range(CHUNKS)
    ]
    arrived = [lax.ppermute(part, "head", swap) for part in parts[:2]]
    for part in after(parts[2:], arrived[0]):
        arrived.append(lax.ppermute(part, "head", swap))
    w_qkv, w_out = after((w_qkv, w_out), parts)
    mine = order_heads(w_qkv, w_out, mover)

    control = jnp.dot(ctrl_table, ctrl_proj, preferred_element_type=F32)
    small = jnp.concatenate(
        [control, q_gain.T.reshape(1, half), k_gain.T.reshape(1, half)], 0
    )
    small_other = lax.ppermute(small, "head", swap)
    both = jnp.stack([small, small_other])
    gains = both[:, classes:].reshape(2, 2, half // 32, 32).transpose(1, 2, 0, 3).reshape(2, width)
    natural = jnp.where(head == 0, both, both[::-1])[:, :classes]
    natural = natural.transpose(0, 2, 1).reshape(width, classes)
    table = class_table(after(jnp.pad(natural, ((0, 0), (0, 32 - classes))), mine))
    mod = lax.dynamic_index_in_dim(mod_table, tsteps[0], 0, keepdims=False)
    lane = jnp.arange(LANES)
    row = jnp.arange(2 * LANES)
    ones2 = (
        ((row // 32 % 2)[:, None] == (lane // 32 % 2)[None, :])
        & ((row % 8)[:, None] == (lane % 8)[None, :])
    ).astype(BF16)

    normed, mixed, halo, beside = [], [], [], []

    def prepare(chunk, other):
        one, two = adaptive_norm(place, hidden, other, keypoints, table, mod, chunk)
        normed.append(one)
        mixed.append(two)
        halo.append(lax.ppermute(one, "queue", halos))
        beside.append(lax.ppermute(one, "queue", cores))

    ahead = 2
    prepare(0, arrived[0])
    fetched = [after(piece, normed[0]) for piece in fetched]
    fetched += [lax.ppermute(piece, "queue", side) for piece, side in zip(fetched, sides)]
    prepare(1, after(arrived[1], halo[0]))
    fetched = fetched[:2] + [after(piece, normed[1]) for piece in fetched[2:]]
    fetched += [lax.ppermute(piece, "queue", cores) for piece in fetched]
    weights = merge_heads(place, mine, fetched)
    carry = None
    back = []
    for chunk in range(CHUNKS):
        carry, send = whole_block(
            place, normed[chunk], halo[chunk], beside[chunk], mixed[chunk], mod, gains, ones2, weights,
            carry, head_dim, chunk, places,
        )
        if chunk + ahead < CHUNKS:
            other, send = lax.optimization_barrier((arrived[chunk + ahead], send))
            prepare(chunk + ahead, other)
        back.append(lax.ppermute(send, "head", swap))
    for chunk in range(CHUNKS):
        carry = lax.dynamic_update_slice(
            carry, back[chunk][:, None], (0, 1 - head, 0, chunk * size)
        )
    return carry.transpose(0, 1, 3, 2)


def solution(mesh):
    placed = (
        P("queue", None, None, "head"),
        P("queue", None),
        P("queue"),
        P(),
        P(),
        P(None, "head"),
        P(None, None, "head"),
        P("head", None),
        P("head", None),
        P("head", None),
    )
    return jax.shard_map(
        functools.partial(on_device, (mesh.shape["queue"], mesh.shape["head"])),
        mesh=mesh,
        in_specs=placed,
        out_specs=P("queue", None, None, "head"),
        check_vma=False,
    )
```

```python
import functools
import math

import jax
import jax.numpy as jnp
from jax import lax
from jax.experimental import pallas as pl
from jax.experimental.pallas import tpu as pltpu
from jax.sharding import PartitionSpec as P

WIN = 4
EPSILON = 1e-06
CHUNKS = 4
LANES = 128
VMEM = 46 << 20
SMALL_VMEM = 32 << 20
BLOCK = 64
COLUMNS = 256
COST = 0.05
KEY, VALUE, QUERY, OUT = range(4)
F32, BF16 = jnp.float32, jnp.bfloat16


def split_dot(values, ones2):
    high = values.astype(BF16)
    low = (values - high.astype(F32)).astype(BF16)
    return jnp.dot(
        jnp.concatenate([high, low], -1), ones2, preferred_element_type=F32
    )


def cost(flops):
    return pl.CostEstimate(flops=int(flops * COST), bytes_accessed=0, transcendentals=0)


def classes_kernel(control, table):
    values = control[...]
    high = values.astype(BF16)
    rest = values - high.astype(F32)
    middle = rest.astype(BF16)
    low = (rest - middle.astype(F32)).astype(BF16)
    table[...] = jnp.concatenate([high, middle, low, jnp.zeros_like(low)], -1)


def class_table(control):
    return pl.pallas_call(
        classes_kernel,
        out_shape=jax.ShapeDtypeStruct((control.shape[0], LANES), BF16),
        compiler_params=pltpu.CompilerParams(vmem_limit_bytes=VMEM),
        name="class_table",
    )(control)


def norm_kernel(place, hidden, other, keypoints, table, mod, normed, mixed):
    half, size = hidden.shape[-2:]
    points = keypoints[pl.ds(pl.program_id(0), 1), :]
    lane = lax.broadcasted_iota(jnp.int32, (LANES, size), 0)
    picks = ((lane % 32 == points) & (lane < 96) & (place[0] == 0)).astype(F32).astype(BF16)
    total = jnp.zeros((1, size), F32)
    for side, values in enumerate((hidden[0, 0], other[0])):
        start = place[0] * half if side == 0 else (1 - place[0]) * half
        rows = pl.ds(pl.multiple_of(start, 64), half)
        control = jnp.dot(table[rows, :], picks, preferred_element_type=F32)
        rounded = (values.astype(F32) + control).astype(BF16)
        mixed[0, rows] = rounded
        total = total + jnp.sum(rounded.astype(F32), 0, keepdims=True)
    centre = total * (1.0 / (2 * half))
    spread = jnp.zeros((1, size), F32)
    for side in range(2):
        part = mixed[0, side * half : (side + 1) * half].astype(F32) - centre
        spread = spread + jnp.sum(part * part, 0, keepdims=True)
    factor = lax.rsqrt(spread * (1.0 / (2 * half)) + EPSILON)
    for tile in range(2 * half // LANES):
        cols = slice(tile * LANES, (tile + 1) * LANES)
        part = ((mixed[0, cols].astype(F32) - centre) * factor).T
        normed[0, :, cols] = (part * (1.0 + mod[1:2, cols]) + mod[0:1, cols]).astype(BF16)


def adaptive_norm(place, hidden, other, keypoints, table, mod, chunk):
    frames, _, half, places = hidden.shape
    size = places // CHUNKS
    width = 2 * half
    grid_spec = pltpu.PrefetchScalarGridSpec(
        num_scalar_prefetch=1,
        grid=(frames,),
        in_specs=[
            pl.BlockSpec((1, 1, half, size), lambda f, s: (f, s[0], 0, chunk)),
            pl.BlockSpec((1, half, size), lambda f, s: (f, 0, 0)),
            pl.BlockSpec((frames, size), lambda f, s: (0, chunk)),
            pl.BlockSpec((width, LANES), lambda f, s: (0, 0)),
            pl.BlockSpec((3, width), lambda f, s: (0, 0)),
        ],
        out_specs=[
            pl.BlockSpec((1, size, width), lambda f, s: (f + s[1] * (3 - 2 * f), 0, 0)),
            pl.BlockSpec((1, width, size), lambda f, s: (f + s[1] * (3 - 2 * f), 0, 0)),
        ],
    )
    return pl.pallas_call(
        norm_kernel,
        grid_spec=grid_spec,
        out_shape=[
            jax.ShapeDtypeStruct((frames, size, width), BF16),
            jax.ShapeDtypeStruct((frames, width, size), BF16),
        ],
        compiler_params=pltpu.CompilerParams(vmem_limit_bytes=SMALL_VMEM),
        cost_estimate=cost(4000 * frames * size * width),
        name="adaptive_norm",
    )(place, hidden, other, keypoints, table, mod)


def piece_kernel(place, w_qkv, w_out, mover, piece):
    def write(weight):
        piece[...] = jnp.dot(mover[...], weight, preferred_element_type=F32).astype(BF16)

    @pl.when(place[3] < 3)
    def _():
        write(w_qkv[0])

    @pl.when(place[3] == 3)
    def _():
        write(w_out[...])


def order_kernel(w_qkv, w_out, mover, ordered):
    def write(weight):
        ordered[0] = jnp.dot(mover[...], weight, preferred_element_type=F32).astype(BF16)

    @pl.when(pl.program_id(0) < 3)
    def _():
        write(w_qkv[0])

    @pl.when(pl.program_id(0) == 3)
    def _():
        write(w_out[...])


def order_heads(w_qkv, w_out, mover):
    half, width = w_out.shape
    return pl.pallas_call(
        order_kernel,
        grid=(4,),
        in_specs=[
            pl.BlockSpec((1, half, width), lambda i: ((i + 1) % 3, 0, 0)),
            pl.BlockSpec((half, width), lambda i: (0, 0)),
            pl.BlockSpec((half, half), lambda i: (0, 0)),
        ],
        out_specs=pl.BlockSpec((1, half, width), lambda i: (i, 0, 0)),
        out_shape=jax.ShapeDtypeStruct((4, half, width), BF16),
        compiler_params=pltpu.CompilerParams(vmem_limit_bytes=60 << 20),
        cost_estimate=cost(8 * half * half * width),
        name="order_heads",
    )(w_qkv, w_out, mover)


def piece_of_heads(place, w_qkv, w_out, mover):
    half, width = w_out.shape
    grid_spec = pltpu.PrefetchScalarGridSpec(
        num_scalar_prefetch=1,
        grid=(1,),
        in_specs=[
            pl.BlockSpec((1, half, width), lambda i, s: ((s[3] + 1) % 3, 0, 0)),
            pl.BlockSpec((half, width), lambda i, s: (0, 0)),
            pl.BlockSpec((half // 2, half), lambda i, s: (s[1], 0)),
        ],
        out_specs=pl.BlockSpec((half // 2, width), lambda i, s: (0, 0)),
    )
    return pl.pallas_call(
        piece_kernel,
        grid_spec=grid_spec,
        out_shape=jax.ShapeDtypeStruct((half // 2, width), BF16),
        compiler_params=pltpu.CompilerParams(vmem_limit_bytes=60 << 20),
        cost_estimate=cost(half * half * width),
        name="piece_of_heads",
    )(place, w_qkv, w_out, mover)


def dot_rows(values, weight):
    return lax.dot_general(values, weight, (((1,), (1,)), ((), ())), preferred_element_type=F32)


def head_norm(values, gain, ones2, head_dim):
    tiles = values.shape[-1] // LANES
    total = None
    for tile in range(tiles):
        part = values[:, tile * LANES : (tile + 1) * LANES]
        total = part * part if total is None else total + part * part
    factor = lax.rsqrt(split_dot(total, ones2) * (1.0 / head_dim) + EPSILON)
    return [
        (values[:, tile * LANES : (tile + 1) * LANES] * factor
         * gain[:, tile * LANES : (tile + 1) * LANES]).astype(BF16)
        for tile in range(tiles)
    ]


def merge_kernel(place, mine, others, weights, sems):
    copies = []
    for kind in range(4):
        for at, source in enumerate((mine, others)):
            copies.append(
                pltpu.make_async_copy(
                    source.at[kind],
                    weights.at[kind, :, at * 32 : at * 32 + 32],
                    sems.at[kind, at],
                )
            )
            copies[-1].start()
    for copy in copies:
        copy.wait()


def merge_heads(place, mine, others):
    _, half, width = mine.shape
    grid_spec = pltpu.PrefetchScalarGridSpec(
        num_scalar_prefetch=1,
        grid=(1,),
        in_specs=[pl.BlockSpec(memory_space=pl.ANY)] * 2,
        out_specs=pl.BlockSpec(memory_space=pltpu.VMEM),
        scratch_shapes=[pltpu.SemaphoreType.DMA((4, 2))],
    )
    return pl.pallas_call(
        merge_kernel,
        grid_spec=grid_spec,
        out_shape=pltpu.VMEM((4, half // 32, 64, width), BF16),
        compiler_params=pltpu.CompilerParams(vmem_limit_bytes=VMEM),
        cost_estimate=cost(8 * half * half * width),
        name="merge_heads",
    )(place, mine.reshape(4, -1, 32, width), others.reshape(4, -1, 32, width))


def block_kernel(
    head_dim, place, own, halo, core, mixed, mod, gains, ones2, weights, carry,
    out, send, rows_in, query, kv, scores, attended, final,
):
    frames, size, width = own.shape
    tiles = width // LANES
    offsets = 2 * WIN + 1
    half = width // 2
    step = pl.program_id(0)
    ones = ones2[...]

    for frame in range(frames):
        rows_in[frame] = halo[frames - 1 - frame]
        rows_in[frames + frame] = own[frame]
        rows_in[2 * frames + frame] = core[frames - 1 - frame]
    reach = 3 * frames * size

    all_rows = rows_in[...].reshape(reach, width)
    edge = width + LANES
    key_value = weights[KEY : VALUE + 1].reshape(2 * width, width)
    keys = dot_rows(all_rows, key_value[0:edge])
    for tile, part in enumerate(head_norm(keys[:, :width], gains[1:2], ones, head_dim)):
        kv[0, :, :, tile * LANES : (tile + 1) * LANES] = part.reshape(3 * frames, size, LANES)
    kv[1, :, :, :LANES] = keys[:, width:].astype(BF16).reshape(3 * frames, size, LANES)
    own_rows = rows_in[frames : 2 * frames].reshape(frames * size, width)
    queries = dot_rows(own_rows, weights[QUERY].reshape(width, width))
    for tile, part in enumerate(head_norm(queries, gains[0:1], ones, head_dim)):
        query[:, :, tile * LANES : (tile + 1) * LANES] = part.reshape(frames, size, LANES)

    def window(kind, frame, rows, cols):
        return kv[kind, frame, rows, cols].astype(F32)

    def score(start, first):
        rows = slice(start, start + 16)
        pair = (first, first + 1)
        sums = {}
        for tile in range(tiles):
            cols = slice(tile * LANES, (tile + 1) * LANES)
            asked = [query[frame, rows, cols].astype(F32) for frame in pair]
            for reached in range(first, first + 1 + offsets):
                key = window(0, reached, rows, cols)
                for frame, one in zip(pair, asked):
                    offset = reached - frame
                    if 0 <= offset < offsets:
                        at = frame * offsets + offset
                        sums[at] = one * key if tile == 0 else sums[at] + one * key
        for at, value in sums.items():
            scores[at, rows] = value

    scale = 1.0 / math.sqrt(head_dim)
    halo_there = place[2] > 0

    def soften(start, frame, sub=32):
        rows = slice(start, start + sub)
        raw = scores[frame * offsets : (frame + 1) * offsets, rows]
        full = split_dot(raw.reshape(offsets * sub, LANES), ones).reshape(
            offsets, sub, LANES
        ) * scale
        parts = [
            jnp.where(halo_there, full[offset], -1e30) if frame + offset < frames else full[offset]
            for offset in range(offsets)
        ]
        highest = functools.reduce(jnp.maximum, parts)
        parts = [jnp.exp(part - highest) for part in parts]
        inverse = 1.0 / functools.reduce(jnp.add, parts)
        for offset, part in enumerate(parts):
            scores[frame * offsets + offset, rows] = (part * inverse).astype(BF16).astype(F32)

    steps = [functools.partial(score, start, first)
             for start in range(0, size, 16) for first in range(0, frames, 2)]
    steps += [functools.partial(soften, start, frame)
              for start in range(0, size, 32) for frame in range(frames)]
    starts = list(range(LANES, width, COLUMNS))
    done = 0
    for at, start in enumerate(starts):
        high = min(start + COLUMNS, width)
        kv[1, :, :, start:high] = dot_rows(
            all_rows, key_value[width + start : width + high]
        ).astype(BF16).reshape(3 * frames, size, high - start)
        until = len(steps) * (at + 1) // len(starts)
        for unit in steps[done:until]:
            unit()
        done = until

    @pl.loop(0, size // 16)
    def _(at):
        rows = pl.ds(pl.multiple_of(at * 16, 16), 16)
        for first in range(0, frames, 2):
            pair = (first, first + 1)
            shares = {
                frame: [scores[frame * offsets + offset, rows] for offset in range(offsets)]
                for frame in pair
            }
            for tile in range(tiles):
                cols = slice(tile * LANES, (tile + 1) * LANES)
                sums = {}
                for reached in range(first, first + 1 + offsets):
                    value = window(1, reached, rows, cols)
                    for frame in pair:
                        offset = reached - frame
                        if 0 <= offset < offsets:
                            term = shares[frame][offset] * value
                            sums[frame] = term if offset == 0 else sums[frame] + term
                for frame in pair:
                    attended[frame, pl.ds(pl.multiple_of(step * size + at * 16, 16), 16), cols] = (
                        sums[frame].astype(BF16)
                    )

    @pl.when(step == pl.num_programs(0) - 1)
    def _():
        places = attended.shape[1]
        own_half = pl.ds(pl.multiple_of(place[0] * half, 64), half)
        send_half = pl.ds(pl.multiple_of((1 - place[0]) * half, 64), half)
        flat = attended[...].reshape(frames * places, width)
        result = jnp.dot(flat, weights[OUT].reshape(width, width), preferred_element_type=F32)
        result = result * mod[2:3, :]
        for frame in range(frames):
            target = frame + place[1] * (3 - 2 * frame)
            for tile in range(tiles):
                cols = slice(tile * LANES, (tile + 1) * LANES)
                turned = result[frame * places : (frame + 1) * places, cols].T
                final[cols] = (mixed[frame, cols].astype(F32) + turned).astype(BF16)
            out[target, 0] = final[own_half]
            send[target] = final[send_half]


def whole_block(place, own, halo, core, mixed, mod, gains, ones2, weights, carry, head_dim,
                chunk, places):
    frames, size, width = own.shape
    half = width // 2
    block = BLOCK
    once = pl.Buffered(1)
    rows = pl.BlockSpec((frames, block, width), lambda p, s: (0, p, 0))
    in_specs = [
        rows, rows, rows,
        pl.BlockSpec((frames, width, size), lambda p, s: (0, 0, 0), pipeline_mode=once),
        pl.BlockSpec((3, width), lambda p, s: (0, 0)),
        pl.BlockSpec((2, width), lambda p, s: (0, 0)),
        pl.BlockSpec((2 * LANES, LANES), lambda p, s: (0, 0)),
    ]
    in_specs.append(pl.BlockSpec(memory_space=pltpu.VMEM))
    weights = pltpu.with_memory_space_constraint(weights, pltpu.VMEM)
    args = [place, own, halo, core, mixed, mod, gains, ones2, weights]
    aliases = {}
    if carry is not None:
        in_specs.append(pl.BlockSpec(memory_space=pl.ANY))
        aliases = {len(args): 0}
        args.append(carry)

    def kernel(*refs):
        block_kernel(head_dim, *refs[:9], None, *refs[9 + len(aliases) :])

    grid_spec = pltpu.PrefetchScalarGridSpec(
        num_scalar_prefetch=1,
        grid=(size // block,),
        in_specs=in_specs,
        out_specs=[
            pl.BlockSpec((frames, 1, half, size), lambda p, s: (0, s[0], 0, chunk)),
            pl.BlockSpec((frames, half, size), lambda p, s: (0, 0, 0)),
        ],
        scratch_shapes=[
            pltpu.VMEM((3 * frames, block, width), BF16),
            pltpu.VMEM((frames, block, width), BF16),
            pltpu.VMEM((2, 3 * frames, block, width), BF16),
            pltpu.VMEM((frames * (2 * WIN + 1), block, LANES), F32),
            pltpu.VMEM((frames, size, width), BF16),
            pltpu.VMEM((width, size), BF16),
        ],
    )
    return pl.pallas_call(
        kernel,
        grid_spec=grid_spec,
        out_shape=[
            jax.ShapeDtypeStruct((frames, 2, half, places), BF16),
            jax.ShapeDtypeStruct((frames, half, size), BF16),
        ],
        input_output_aliases=aliases,
        compiler_params=pltpu.CompilerParams(vmem_limit_bytes=VMEM),
        cost_estimate=cost(36 * frames * size * width * width),
        name="whole_block",
    )(*args)


def on_device(
    mesh_sizes, hidden, keypoints, tsteps, mod_table, ctrl_table, ctrl_proj, w_qkv, q_gain, k_gain,
    w_out,
):
    queue_size, head_size = mesh_sizes
    frames, _, places, half = hidden.shape
    width = 2 * half
    heads, head_dim = q_gain.shape
    classes = ctrl_table.shape[0]
    size = places // CHUNKS
    head = lax.axis_index("head")
    queue = lax.axis_index("queue")
    core = queue % 2
    swap = [(0, 1), (1, 0)]
    across = [
        (2 * q + h, 2 * ((q + queue_size // 2) % queue_size) + 1 - h)
        for q in range(queue_size)
        for h in range(2)
    ]
    cores = [(q, q ^ 1) for q in range(queue_size)]
    halos = [(q, q + 1) for q in range(1, queue_size - 1, 2)]
    halos += [(b, a) for a, b in halos]

    halo_there = ((queue > 0) & (queue < queue_size - 1)).astype(jnp.int32)
    place = jnp.stack([head, core, halo_there, queue // 8 % 4]).astype(jnp.int32)
    hidden = hidden.transpose(0, 1, 3, 2)
    w_qkv = w_qkv.transpose(1, 2, 0)

    def after(value, *others):
        return lax.optimization_barrier((value, others))[0]

    source = jnp.arange(half)
    mover = (
        source[None, :] == ((source % heads) * head_dim + source // heads)[:, None]
    ).astype(BF16)
    piece = piece_of_heads(place, w_qkv, w_out, mover)
    eighth = lax.ppermute(piece, ("queue", "head"), across)
    sharers = [
        [((top * 4 + x) * 4 + y) * 2 + c for x in range(4) for c in range(2)]
        for top in range(queue_size // 32)
        for y in range(4)
    ]

    cut = after(hidden, piece)
    parts = [
        lax.dynamic_slice(
            cut, (0, 1 - head, 0, chunk * size), (frames, 1, half, size)
        ).reshape(frames, half, size)
        for chunk in range(CHUNKS)
    ]
    arrived = [lax.ppermute(part, "head", swap) for part in parts[:3]]
    for part in after(parts[3:], arrived[0]):
        arrived.append(lax.ppermute(part, "head", swap))
    w_qkv, w_out = after((w_qkv, w_out), parts)
    mine = order_heads(w_qkv, w_out, mover)

    control = jnp.dot(ctrl_table, ctrl_proj, preferred_element_type=F32)
    small = jnp.concatenate(
        [control, q_gain.T.reshape(1, half), k_gain.T.reshape(1, half)], 0
    )
    small_other = lax.ppermute(small, "head", swap)
    both = jnp.stack([small, small_other])
    gains = both[:, classes:].reshape(2, 2, half // 32, 32).transpose(1, 2, 0, 3).reshape(2, width)
    natural = jnp.where(head == 0, both, both[::-1])[:, :classes]
    natural = natural.transpose(0, 2, 1).reshape(width, classes)
    table = class_table(after(jnp.pad(natural, ((0, 0), (0, 32 - classes))), mine))
    eighth = after(eighth, arrived[0], table)
    others = lax.all_gather(eighth, "queue", axis=0, tiled=True, axis_index_groups=sharers)
    mod = lax.dynamic_index_in_dim(mod_table, tsteps[0], 0, keepdims=False)
    lane = jnp.arange(LANES)
    row = jnp.arange(2 * LANES)
    ones2 = (
        ((row // 32 % 2)[:, None] == (lane // 32 % 2)[None, :])
        & ((row % 8)[:, None] == (lane % 8)[None, :])
    ).astype(BF16)

    normed, mixed, halo, beside = [], [], [], []

    def prepare(chunk, other):
        one, two = adaptive_norm(place, hidden, other, keypoints, table, mod, chunk)
        normed.append(one)
        mixed.append(two)
        halo.append(lax.ppermute(one, "queue", halos))
        beside.append(lax.ppermute(one, "queue", cores))

    ahead = 3
    prepare(0, arrived[0])
    prepare(1, arrived[1])
    prepare(2, after(arrived[2], normed[1], halo[0]))
    others, mine = after((others, mine), normed[2])
    weights = merge_heads(place, mine, others)
    carry = None
    back = []
    for chunk in range(CHUNKS):
        carry, send = whole_block(
            place, normed[chunk], halo[chunk], beside[chunk], mixed[chunk], mod, gains, ones2, weights,
            carry, head_dim, chunk, places,
        )
        if chunk + ahead < CHUNKS:
            other, send = lax.optimization_barrier((arrived[chunk + ahead], send))
            prepare(chunk + ahead, other)
        back.append(lax.ppermute(send, "head", swap))
    for chunk in range(CHUNKS):
        carry = lax.dynamic_update_slice(
            carry, back[chunk][:, None], (0, 1 - head, 0, chunk * size)
        )
    return carry.transpose(0, 1, 3, 2)


def solution(mesh):
    placed = (
        P("queue", None, None, "head"),
        P("queue", None),
        P("queue"),
        P(),
        P(),
        P(None, "head"),
        P(None, None, "head"),
        P("head", None),
        P("head", None),
        P("head", None),
    )
    return jax.shard_map(
        functools.partial(on_device, (mesh.shape["queue"], mesh.shape["head"])),
        mesh=mesh,
        in_specs=placed,
        out_specs=P("queue", None, None, "head"),
        check_vma=False,
    )
```

```python
import functools
import math

import jax
import jax.numpy as jnp
from jax import lax
from jax.experimental import pallas as pl
from jax.experimental.pallas import tpu as pltpu
from jax.sharding import PartitionSpec as P

WIN = 4
EPSILON = 1e-06
CHUNKS = 4
LANES = 128
VMEM = 46 << 20
SMALL_VMEM = 32 << 20
BLOCK = 64
COLUMNS = 256
COST = 0.05
KEY, VALUE, QUERY, OUT = range(4)
F32, BF16 = jnp.float32, jnp.bfloat16


def split_dot(values, ones2):
    high = values.astype(BF16)
    low = (values - high.astype(F32)).astype(BF16)
    return jnp.dot(
        jnp.concatenate([high, low], -1), ones2, preferred_element_type=F32
    )


def cost(flops):
    return pl.CostEstimate(flops=int(flops * COST), bytes_accessed=0, transcendentals=0)


def classes_kernel(control, table):
    values = control[...]
    high = values.astype(BF16)
    rest = values - high.astype(F32)
    middle = rest.astype(BF16)
    low = (rest - middle.astype(F32)).astype(BF16)
    table[...] = jnp.concatenate([high, middle, low, jnp.zeros_like(low)], -1)


def class_table(control):
    return pl.pallas_call(
        classes_kernel,
        out_shape=jax.ShapeDtypeStruct((control.shape[0], LANES), BF16),
        compiler_params=pltpu.CompilerParams(vmem_limit_bytes=VMEM),
        name="class_table",
    )(control)


def norm_kernel(place, hidden, other, keypoints, table, mod, normed, mixed):
    half, size = hidden.shape[-2:]
    points = keypoints[pl.ds(pl.program_id(0), 1), :]
    lane = lax.broadcasted_iota(jnp.int32, (LANES, size), 0)
    picks = ((lane % 32 == points) & (lane < 96) & (place[0] == 0)).astype(F32).astype(BF16)
    total = jnp.zeros((1, size), F32)
    for side, values in enumerate((hidden[0, 0], other[0])):
        start = place[0] * half if side == 0 else (1 - place[0]) * half
        rows = pl.ds(pl.multiple_of(start, 64), half)
        control = jnp.dot(table[rows, :], picks, preferred_element_type=F32)
        rounded = (values.astype(F32) + control).astype(BF16)
        mixed[0, rows] = rounded
        total = total + jnp.sum(rounded.astype(F32), 0, keepdims=True)
    centre = total * (1.0 / (2 * half))
    spread = jnp.zeros((1, size), F32)
    for side in range(2):
        part = mixed[0, side * half : (side + 1) * half].astype(F32) - centre
        spread = spread + jnp.sum(part * part, 0, keepdims=True)
    factor = lax.rsqrt(spread * (1.0 / (2 * half)) + EPSILON)
    for tile in range(2 * half // LANES):
        cols = slice(tile * LANES, (tile + 1) * LANES)
        part = ((mixed[0, cols].astype(F32) - centre) * factor).T
        normed[0, :, cols] = (part * (1.0 + mod[1:2, cols]) + mod[0:1, cols]).astype(BF16)


def adaptive_norm(place, hidden, other, keypoints, table, mod, chunk):
    frames, _, half, places = hidden.shape
    size = places // CHUNKS
    width = 2 * half
    grid_spec = pltpu.PrefetchScalarGridSpec(
        num_scalar_prefetch=1,
        grid=(frames,),
        in_specs=[
            pl.BlockSpec((1, 1, half, size), lambda f, s: (f, s[0], 0, chunk)),
            pl.BlockSpec((1, half, size), lambda f, s: (f, 0, 0)),
            pl.BlockSpec((frames, size), lambda f, s: (0, chunk)),
            pl.BlockSpec((width, LANES), lambda f, s: (0, 0)),
            pl.BlockSpec((3, width), lambda f, s: (0, 0)),
        ],
        out_specs=[
            pl.BlockSpec((1, size, width), lambda f, s: (f + s[1] * (3 - 2 * f), 0, 0)),
            pl.BlockSpec((1, width, size), lambda f, s: (f + s[1] * (3 - 2 * f), 0, 0)),
        ],
    )
    return pl.pallas_call(
        norm_kernel,
        grid_spec=grid_spec,
        out_shape=[
            jax.ShapeDtypeStruct((frames, size, width), BF16),
            jax.ShapeDtypeStruct((frames, width, size), BF16),
        ],
        compiler_params=pltpu.CompilerParams(vmem_limit_bytes=SMALL_VMEM),
        cost_estimate=cost(4000 * frames * size * width),
        name="adaptive_norm",
    )(place, hidden, other, keypoints, table, mod)


def piece_kernel(place, w_qkv, w_out, mover, piece):
    def write(weight):
        piece[...] = jnp.dot(mover[...], weight, preferred_element_type=F32).astype(BF16)

    @pl.when(place[3] < 3)
    def _():
        write(w_qkv[0])

    @pl.when(place[3] == 3)
    def _():
        write(w_out[...])


def order_kernel(w_qkv, w_out, mover, ordered):
    def write(weight):
        ordered[0] = jnp.dot(mover[...], weight, preferred_element_type=F32).astype(BF16)

    @pl.when(pl.program_id(0) < 3)
    def _():
        write(w_qkv[0])

    @pl.when(pl.program_id(0) == 3)
    def _():
        write(w_out[...])


def order_heads(w_qkv, w_out, mover):
    half, width = w_out.shape
    return pl.pallas_call(
        order_kernel,
        grid=(4,),
        in_specs=[
            pl.BlockSpec((1, half, width), lambda i: ((i + 1) % 3, 0, 0)),
            pl.BlockSpec((half, width), lambda i: (0, 0)),
            pl.BlockSpec((half, half), lambda i: (0, 0)),
        ],
        out_specs=pl.BlockSpec((1, half, width), lambda i: (i, 0, 0)),
        out_shape=jax.ShapeDtypeStruct((4, half, width), BF16),
        compiler_params=pltpu.CompilerParams(vmem_limit_bytes=60 << 20),
        cost_estimate=cost(8 * half * half * width),
        name="order_heads",
    )(w_qkv, w_out, mover)


def piece_of_heads(place, w_qkv, w_out, mover):
    half, width = w_out.shape
    grid_spec = pltpu.PrefetchScalarGridSpec(
        num_scalar_prefetch=1,
        grid=(1,),
        in_specs=[
            pl.BlockSpec((1, half, width), lambda i, s: ((s[3] + 1) % 3, 0, 0)),
            pl.BlockSpec((half, width), lambda i, s: (0, 0)),
            pl.BlockSpec((half // 2, half), lambda i, s: (s[1], 0)),
        ],
        out_specs=pl.BlockSpec((half // 2, width), lambda i, s: (0, 0)),
    )
    return pl.pallas_call(
        piece_kernel,
        grid_spec=grid_spec,
        out_shape=jax.ShapeDtypeStruct((half // 2, width), BF16),
        compiler_params=pltpu.CompilerParams(vmem_limit_bytes=60 << 20),
        cost_estimate=cost(half * half * width),
        name="piece_of_heads",
    )(place, w_qkv, w_out, mover)


def dot_rows(values, weight):
    return lax.dot_general(values, weight, (((1,), (1,)), ((), ())), preferred_element_type=F32)


def head_norm(values, gain, ones2, head_dim):
    tiles = values.shape[-1] // LANES
    total = None
    for tile in range(tiles):
        part = values[:, tile * LANES : (tile + 1) * LANES]
        total = part * part if total is None else total + part * part
    factor = lax.rsqrt(split_dot(total, ones2) * (1.0 / head_dim) + EPSILON)
    return [
        (values[:, tile * LANES : (tile + 1) * LANES] * factor
         * gain[:, tile * LANES : (tile + 1) * LANES]).astype(BF16)
        for tile in range(tiles)
    ]


def merge_kernel(place, mine, others, weights, sems):
    copies = []
    for kind in range(4):
        for at, source in enumerate((mine, others)):
            copies.append(
                pltpu.make_async_copy(
                    source.at[kind],
                    weights.at[kind, :, at * 32 : at * 32 + 32],
                    sems.at[kind, at],
                )
            )
            copies[-1].start()
    for copy in copies:
        copy.wait()


def merge_heads(place, mine, others):
    _, half, width = mine.shape
    grid_spec = pltpu.PrefetchScalarGridSpec(
        num_scalar_prefetch=1,
        grid=(1,),
        in_specs=[pl.BlockSpec(memory_space=pl.ANY)] * 2,
        out_specs=pl.BlockSpec(memory_space=pltpu.VMEM),
        scratch_shapes=[pltpu.SemaphoreType.DMA((4, 2))],
    )
    return pl.pallas_call(
        merge_kernel,
        grid_spec=grid_spec,
        out_shape=pltpu.VMEM((4, half // 32, 64, width), BF16),
        compiler_params=pltpu.CompilerParams(vmem_limit_bytes=VMEM),
        cost_estimate=cost(8 * half * half * width),
        name="merge_heads",
    )(place, mine.reshape(4, -1, 32, width), others.reshape(4, -1, 32, width))


def block_kernel(
    head_dim, place, own, halo, core, mixed, mod, gains, ones2, weights, carry,
    out, send, rows_in, query, kv, scores, attended, final,
):
    frames, size, width = own.shape
    tiles = width // LANES
    offsets = 2 * WIN + 1
    half = width // 2
    step = pl.program_id(0)
    ones = ones2[...]

    for frame in range(frames):
        rows_in[frame] = halo[frames - 1 - frame]
        rows_in[frames + frame] = own[frame]
        rows_in[2 * frames + frame] = core[frames - 1 - frame]
    reach = 3 * frames * size

    all_rows = rows_in[...].reshape(reach, width)
    edge = width + LANES
    key_value = weights[KEY : VALUE + 1].reshape(2 * width, width)
    keys = dot_rows(all_rows, key_value[0:edge])
    for tile, part in enumerate(head_norm(keys[:, :width], gains[1:2], ones, head_dim)):
        kv[0, :, :, tile * LANES : (tile + 1) * LANES] = part.reshape(3 * frames, size, LANES)
    kv[1, :, :, :LANES] = keys[:, width:].astype(BF16).reshape(3 * frames, size, LANES)
    own_rows = rows_in[frames : 2 * frames].reshape(frames * size, width)
    queries = dot_rows(own_rows, weights[QUERY].reshape(width, width))
    for tile, part in enumerate(head_norm(queries, gains[0:1], ones, head_dim)):
        query[:, :, tile * LANES : (tile + 1) * LANES] = part.reshape(frames, size, LANES)

    def window(kind, frame, rows, cols):
        return kv[kind, frame, rows, cols].astype(F32)

    def score(start, first):
        rows = slice(start, start + 16)
        pair = (first, first + 1)
        sums = {}
        for tile in range(tiles):
            cols = slice(tile * LANES, (tile + 1) * LANES)
            asked = [query[frame, rows, cols].astype(F32) for frame in pair]
            for reached in range(first, first + 1 + offsets):
                key = window(0, reached, rows, cols)
                for frame, one in zip(pair, asked):
                    offset = reached - frame
                    if 0 <= offset < offsets:
                        at = frame * offsets + offset
                        sums[at] = one * key if tile == 0 else sums[at] + one * key
        for at, value in sums.items():
            scores[at, rows] = value

    scale = 1.0 / math.sqrt(head_dim)
    halo_there = place[2] > 0

    def soften(start, frame, sub=32):
        rows = slice(start, start + sub)
        raw = scores[frame * offsets : (frame + 1) * offsets, rows]
        full = split_dot(raw.reshape(offsets * sub, LANES), ones).reshape(
            offsets, sub, LANES
        ) * scale
        parts = [
            jnp.where(halo_there, full[offset], -1e30) if frame + offset < frames else full[offset]
            for offset in range(offsets)
        ]
        highest = functools.reduce(jnp.maximum, parts)
        parts = [jnp.exp(part - highest) for part in parts]
        inverse = 1.0 / functools.reduce(jnp.add, parts)
        for offset, part in enumerate(parts):
            scores[frame * offsets + offset, rows] = (part * inverse).astype(BF16).astype(F32)

    steps = [functools.partial(score, start, first)
             for start in range(0, size, 16) for first in range(0, frames, 2)]
    steps += [functools.partial(soften, start, frame)
              for start in range(0, size, 32) for frame in range(frames)]
    starts = list(range(LANES, width, COLUMNS))
    done = 0
    for at, start in enumerate(starts):
        high = min(start + COLUMNS, width)
        kv[1, :, :, start:high] = dot_rows(
            all_rows, key_value[width + start : width + high]
        ).astype(BF16).reshape(3 * frames, size, high - start)
        until = len(steps) * (at + 1) // len(starts)
        for unit in steps[done:until]:
            unit()
        done = until

    @pl.loop(0, size // 16)
    def _(at):
        rows = pl.ds(pl.multiple_of(at * 16, 16), 16)
        for first in range(0, frames, 2):
            pair = (first, first + 1)
            shares = {
                frame: [scores[frame * offsets + offset, rows] for offset in range(offsets)]
                for frame in pair
            }
            for tile in range(tiles):
                cols = slice(tile * LANES, (tile + 1) * LANES)
                sums = {}
                for reached in range(first, first + 1 + offsets):
                    value = window(1, reached, rows, cols)
                    for frame in pair:
                        offset = reached - frame
                        if 0 <= offset < offsets:
                            term = shares[frame][offset] * value
                            sums[frame] = term if offset == 0 else sums[frame] + term
                for frame in pair:
                    attended[frame, pl.ds(pl.multiple_of(step * size + at * 16, 16), 16), cols] = (
                        sums[frame].astype(BF16)
                    )

    @pl.when(step == pl.num_programs(0) - 1)
    def _():
        places = attended.shape[1]
        own_half = pl.ds(pl.multiple_of(place[0] * half, 64), half)
        send_half = pl.ds(pl.multiple_of((1 - place[0]) * half, 64), half)
        flat = attended[...].reshape(frames * places, width)
        result = jnp.dot(flat, weights[OUT].reshape(width, width), preferred_element_type=F32)
        result = result * mod[2:3, :]
        for frame in range(frames):
            target = frame + place[1] * (3 - 2 * frame)
            for tile in range(tiles):
                cols = slice(tile * LANES, (tile + 1) * LANES)
                turned = result[frame * places : (frame + 1) * places, cols].T
                final[cols] = (mixed[frame, cols].astype(F32) + turned).astype(BF16)
            out[target, 0] = final[own_half]
            send[target] = final[send_half]


def whole_block(place, own, halo, core, mixed, mod, gains, ones2, weights, carry, head_dim,
                chunk, places):
    frames, size, width = own.shape
    half = width // 2
    block = BLOCK
    once = pl.Buffered(1)
    rows = pl.BlockSpec((frames, block, width), lambda p, s: (0, p, 0))
    in_specs = [
        rows, rows, rows,
        pl.BlockSpec((frames, width, size), lambda p, s: (0, 0, 0), pipeline_mode=once),
        pl.BlockSpec((3, width), lambda p, s: (0, 0)),
        pl.BlockSpec((2, width), lambda p, s: (0, 0)),
        pl.BlockSpec((2 * LANES, LANES), lambda p, s: (0, 0)),
    ]
    in_specs.append(pl.BlockSpec(memory_space=pltpu.VMEM))
    weights = pltpu.with_memory_space_constraint(weights, pltpu.VMEM)
    args = [place, own, halo, core, mixed, mod, gains, ones2, weights]
    aliases = {}
    if carry is not None:
        in_specs.append(pl.BlockSpec(memory_space=pl.ANY))
        aliases = {len(args): 0}
        args.append(carry)

    def kernel(*refs):
        block_kernel(head_dim, *refs[:9], None, *refs[9 + len(aliases) :])

    grid_spec = pltpu.PrefetchScalarGridSpec(
        num_scalar_prefetch=1,
        grid=(size // block,),
        in_specs=in_specs,
        out_specs=[
            pl.BlockSpec((frames, 1, half, size), lambda p, s: (0, s[0], 0, chunk)),
            pl.BlockSpec((frames, half, size), lambda p, s: (0, 0, 0)),
        ],
        scratch_shapes=[
            pltpu.VMEM((3 * frames, block, width), BF16),
            pltpu.VMEM((frames, block, width), BF16),
            pltpu.VMEM((2, 3 * frames, block, width), BF16),
            pltpu.VMEM((frames * (2 * WIN + 1), block, LANES), F32),
            pltpu.VMEM((frames, size, width), BF16),
            pltpu.VMEM((width, size), BF16),
        ],
    )
    return pl.pallas_call(
        kernel,
        grid_spec=grid_spec,
        out_shape=[
            jax.ShapeDtypeStruct((frames, 2, half, places), BF16),
            jax.ShapeDtypeStruct((frames, half, size), BF16),
        ],
        input_output_aliases=aliases,
        compiler_params=pltpu.CompilerParams(vmem_limit_bytes=VMEM),
        cost_estimate=cost(36 * frames * size * width * width),
        name="whole_block",
    )(*args)


def on_device(
    mesh_sizes, hidden, keypoints, tsteps, mod_table, ctrl_table, ctrl_proj, w_qkv, q_gain, k_gain,
    w_out,
):
    queue_size, head_size = mesh_sizes
    frames, _, places, half = hidden.shape
    width = 2 * half
    heads, head_dim = q_gain.shape
    classes = ctrl_table.shape[0]
    size = places // CHUNKS
    head = lax.axis_index("head")
    queue = lax.axis_index("queue")
    core = queue % 2
    swap = [(0, 1), (1, 0)]
    across = [
        (2 * q + h, 2 * ((q + queue_size // 2) % queue_size) + 1 - h)
        for q in range(queue_size)
        for h in range(2)
    ]
    cores = [(q, q ^ 1) for q in range(queue_size)]
    halos = [(q, q + 1) for q in range(1, queue_size - 1, 2)]
    halos += [(b, a) for a, b in halos]

    halo_there = ((queue > 0) & (queue < queue_size - 1)).astype(jnp.int32)
    place = jnp.stack([head, core, halo_there, queue // 8 % 4]).astype(jnp.int32)
    hidden = hidden.transpose(0, 1, 3, 2)
    w_qkv = w_qkv.transpose(1, 2, 0)

    def after(value, *others):
        return lax.optimization_barrier((value, others))[0]

    source = jnp.arange(half)
    mover = (
        source[None, :] == ((source % heads) * head_dim + source // heads)[:, None]
    ).astype(BF16)
    piece = piece_of_heads(place, w_qkv, w_out, mover)
    eighth = lax.ppermute(piece, ("queue", "head"), across)
    sharers = [
        [((top * 4 + x) * 4 + y) * 2 + c for x in range(4) for c in range(2)]
        for top in range(queue_size // 32)
        for y in range(4)
    ]

    cut = after(hidden, piece)
    parts = [
        lax.dynamic_slice(
            cut, (0, 1 - head, 0, chunk * size), (frames, 1, half, size)
        ).reshape(frames, half, size)
        for chunk in range(CHUNKS)
    ]
    arrived = [lax.ppermute(part, "head", swap) for part in parts[:3]]
    for part in after(parts[3:], arrived[0]):
        arrived.append(lax.ppermute(part, "head", swap))
    w_qkv, w_out = after((w_qkv, w_out), parts)
    mine = order_heads(w_qkv, w_out, mover)

    control = jnp.dot(ctrl_table, ctrl_proj, preferred_element_type=F32)
    small = jnp.concatenate(
        [control, q_gain.T.reshape(1, half), k_gain.T.reshape(1, half)], 0
    )
    small_other = lax.ppermute(small, "head", swap)
    both = jnp.stack([small, small_other])
    gains = both[:, classes:].reshape(2, 2, half // 32, 32).transpose(1, 2, 0, 3).reshape(2, width)
    natural = jnp.where(head == 0, both, both[::-1])[:, :classes]
    natural = natural.transpose(0, 2, 1).reshape(width, classes)
    table = class_table(after(jnp.pad(natural, ((0, 0), (0, 32 - classes))), mine))
    eighth = after(eighth, arrived[0], table)
    others = lax.all_gather(eighth, "queue", axis=0, tiled=True, axis_index_groups=sharers)
    mod = lax.dynamic_index_in_dim(mod_table, tsteps[0], 0, keepdims=False)
    lane = jnp.arange(LANES)
    row = jnp.arange(2 * LANES)
    ones2 = (
        ((row // 32 % 2)[:, None] == (lane // 32 % 2)[None, :])
        & ((row % 8)[:, None] == (lane % 8)[None, :])
    ).astype(BF16)

    normed, mixed, halo, beside = [], [], [], []

    def prepare(chunk, other):
        one, two = adaptive_norm(place, hidden, other, keypoints, table, mod, chunk)
        normed.append(one)
        mixed.append(two)
        halo.append(lax.ppermute(one, "queue", halos))
        beside.append(lax.ppermute(one, "queue", cores))

    ahead = 3
    prepare(0, arrived[0])
    prepare(1, arrived[1])
    prepare(2, after(arrived[2], normed[1]))
    others, mine = after((others, mine), normed[2])
    weights = merge_heads(place, mine, others)
    carry = None
    back = []
    for chunk in range(CHUNKS):
        carry, send = whole_block(
            place, normed[chunk], halo[chunk], beside[chunk], mixed[chunk], mod, gains, ones2, weights,
            carry, head_dim, chunk, places,
        )
        if chunk + ahead < CHUNKS:
            other, send = lax.optimization_barrier((arrived[chunk + ahead], send))
            prepare(chunk + ahead, other)
        back.append(lax.ppermute(send, "head", swap))
    for chunk in range(CHUNKS):
        carry = lax.dynamic_update_slice(
            carry, back[chunk][:, None], (0, 1 - head, 0, chunk * size)
        )
    return carry.transpose(0, 1, 3, 2)


def solution(mesh):
    placed = (
        P("queue", None, None, "head"),
        P("queue", None),
        P("queue"),
        P(),
        P(),
        P(None, "head"),
        P(None, None, "head"),
        P("head", None),
        P("head", None),
        P("head", None),
    )
    return jax.shard_map(
        functools.partial(on_device, (mesh.shape["queue"], mesh.shape["head"])),
        mesh=mesh,
        in_specs=placed,
        out_specs=P("queue", None, None, "head"),
        check_vma=False,
    )
```

```python
import functools
import math

import jax
import jax.numpy as jnp
from jax import lax
from jax.experimental import pallas as pl
from jax.experimental.pallas import tpu as pltpu
from jax.sharding import PartitionSpec as P

WIN = 4
EPSILON = 1e-06
CHUNKS = 4
LANES = 128
VMEM = 46 << 20
SMALL_VMEM = 32 << 20
BLOCK = 64
COLUMNS = 256
COST = 0.05
KEY, VALUE, QUERY, OUT = range(4)
F32, BF16 = jnp.float32, jnp.bfloat16


def split_dot(values, ones2):
    high = values.astype(BF16)
    low = (values - high.astype(F32)).astype(BF16)
    return jnp.dot(
        jnp.concatenate([high, low], -1), ones2, preferred_element_type=F32
    )


def cost(flops):
    return pl.CostEstimate(flops=int(flops * COST), bytes_accessed=0, transcendentals=0)


def classes_kernel(control, table):
    values = control[...]
    high = values.astype(BF16)
    rest = values - high.astype(F32)
    middle = rest.astype(BF16)
    low = (rest - middle.astype(F32)).astype(BF16)
    table[...] = jnp.concatenate([high, middle, low, jnp.zeros_like(low)], -1)


def class_table(control):
    return pl.pallas_call(
        classes_kernel,
        out_shape=jax.ShapeDtypeStruct((control.shape[0], LANES), BF16),
        compiler_params=pltpu.CompilerParams(vmem_limit_bytes=VMEM),
        name="class_table",
    )(control)


def norm_kernel(place, hidden, other, keypoints, table, mod, normed, mixed):
    half, size = hidden.shape[-2:]
    points = keypoints[pl.ds(pl.program_id(0), 1), :]
    lane = lax.broadcasted_iota(jnp.int32, (LANES, size), 0)
    picks = ((lane % 32 == points) & (lane < 96) & (place[0] == 0)).astype(F32).astype(BF16)
    total = jnp.zeros((1, size), F32)
    for side, values in enumerate((hidden[0, 0], other[0])):
        start = place[0] * half if side == 0 else (1 - place[0]) * half
        rows = pl.ds(pl.multiple_of(start, 64), half)
        control = jnp.dot(table[rows, :], picks, preferred_element_type=F32)
        rounded = (values.astype(F32) + control).astype(BF16)
        mixed[0, rows] = rounded
        total = total + jnp.sum(rounded.astype(F32), 0, keepdims=True)
    centre = total * (1.0 / (2 * half))
    spread = jnp.zeros((1, size), F32)
    for side in range(2):
        part = mixed[0, side * half : (side + 1) * half].astype(F32) - centre
        spread = spread + jnp.sum(part * part, 0, keepdims=True)
    factor = lax.rsqrt(spread * (1.0 / (2 * half)) + EPSILON)
    for tile in range(2 * half // LANES):
        cols = slice(tile * LANES, (tile + 1) * LANES)
        part = ((mixed[0, cols].astype(F32) - centre) * factor).T
        normed[0, :, cols] = (part * (1.0 + mod[1:2, cols]) + mod[0:1, cols]).astype(BF16)


def adaptive_norm(place, hidden, other, keypoints, table, mod, chunk):
    frames, _, half, places = hidden.shape
    size = places // CHUNKS
    width = 2 * half
    grid_spec = pltpu.PrefetchScalarGridSpec(
        num_scalar_prefetch=1,
        grid=(frames,),
        in_specs=[
            pl.BlockSpec((1, 1, half, size), lambda f, s: (f, s[0], 0, chunk)),
            pl.BlockSpec((1, half, size), lambda f, s: (f, 0, 0)),
            pl.BlockSpec((frames, size), lambda f, s: (0, chunk)),
            pl.BlockSpec((width, LANES), lambda f, s: (0, 0)),
            pl.BlockSpec((3, width), lambda f, s: (0, 0)),
        ],
        out_specs=[
            pl.BlockSpec((1, size, width), lambda f, s: (f + s[1] * (3 - 2 * f), 0, 0)),
            pl.BlockSpec((1, width, size), lambda f, s: (f + s[1] * (3 - 2 * f), 0, 0)),
        ],
    )
    return pl.pallas_call(
        norm_kernel,
        grid_spec=grid_spec,
        out_shape=[
            jax.ShapeDtypeStruct((frames, size, width), BF16),
            jax.ShapeDtypeStruct((frames, width, size), BF16),
        ],
        compiler_params=pltpu.CompilerParams(vmem_limit_bytes=SMALL_VMEM),
        cost_estimate=cost(4000 * frames * size * width),
        name="adaptive_norm",
    )(place, hidden, other, keypoints, table, mod)


def piece_kernel(place, w_qkv, w_out, mover, piece):
    def write(weight):
        piece[...] = jnp.dot(mover[...], weight, preferred_element_type=F32).astype(BF16)

    @pl.when(place[3] < 3)
    def _():
        write(w_qkv[0])

    @pl.when(place[3] == 3)
    def _():
        write(w_out[...])


def order_kernel(w_qkv, w_out, mover, ordered):
    def write(weight):
        ordered[0] = jnp.dot(mover[...], weight, preferred_element_type=F32).astype(BF16)

    @pl.when(pl.program_id(0) < 3)
    def _():
        write(w_qkv[0])

    @pl.when(pl.program_id(0) == 3)
    def _():
        write(w_out[...])


def order_heads(w_qkv, w_out, mover):
    half, width = w_out.shape
    return pl.pallas_call(
        order_kernel,
        grid=(4,),
        in_specs=[
            pl.BlockSpec((1, half, width), lambda i: ((i + 1) % 3, 0, 0)),
            pl.BlockSpec((half, width), lambda i: (0, 0)),
            pl.BlockSpec((half, half), lambda i: (0, 0)),
        ],
        out_specs=pl.BlockSpec((1, half, width), lambda i: (i, 0, 0)),
        out_shape=jax.ShapeDtypeStruct((4, half, width), BF16),
        compiler_params=pltpu.CompilerParams(vmem_limit_bytes=60 << 20),
        cost_estimate=cost(8 * half * half * width),
        name="order_heads",
    )(w_qkv, w_out, mover)


def piece_of_heads(place, w_qkv, w_out, mover):
    half, width = w_out.shape
    grid_spec = pltpu.PrefetchScalarGridSpec(
        num_scalar_prefetch=1,
        grid=(1,),
        in_specs=[
            pl.BlockSpec((1, half, width), lambda i, s: ((s[3] + 1) % 3, 0, 0)),
            pl.BlockSpec((half, width), lambda i, s: (0, 0)),
            pl.BlockSpec((half // 2, half), lambda i, s: (s[1], 0)),
        ],
        out_specs=pl.BlockSpec((half // 2, width), lambda i, s: (0, 0)),
    )
    return pl.pallas_call(
        piece_kernel,
        grid_spec=grid_spec,
        out_shape=jax.ShapeDtypeStruct((half // 2, width), BF16),
        compiler_params=pltpu.CompilerParams(vmem_limit_bytes=60 << 20),
        cost_estimate=cost(half * half * width),
        name="piece_of_heads",
    )(place, w_qkv, w_out, mover)


def dot_rows(values, weight):
    return lax.dot_general(values, weight, (((1,), (1,)), ((), ())), preferred_element_type=F32)


def head_norm(values, gain, ones2, head_dim):
    tiles = values.shape[-1] // LANES
    total = None
    for tile in range(tiles):
        part = values[:, tile * LANES : (tile + 1) * LANES]
        total = part * part if total is None else total + part * part
    factor = lax.rsqrt(split_dot(total, ones2) * (1.0 / head_dim) + EPSILON)
    return [
        (values[:, tile * LANES : (tile + 1) * LANES] * factor
         * gain[:, tile * LANES : (tile + 1) * LANES]).astype(BF16)
        for tile in range(tiles)
    ]


def merge_kernel(place, mine, others, weights, sems):
    copies = []
    for kind in range(4):
        for at, source in enumerate((mine, others)):
            copies.append(
                pltpu.make_async_copy(
                    source.at[kind],
                    weights.at[kind, :, at * 32 : at * 32 + 32],
                    sems.at[kind, at],
                )
            )
            copies[-1].start()
    for copy in copies:
        copy.wait()


def merge_heads(place, mine, others):
    _, half, width = mine.shape
    grid_spec = pltpu.PrefetchScalarGridSpec(
        num_scalar_prefetch=1,
        grid=(1,),
        in_specs=[pl.BlockSpec(memory_space=pl.ANY)] * 2,
        out_specs=pl.BlockSpec(memory_space=pltpu.VMEM),
        scratch_shapes=[pltpu.SemaphoreType.DMA((4, 2))],
    )
    return pl.pallas_call(
        merge_kernel,
        grid_spec=grid_spec,
        out_shape=pltpu.VMEM((4, half // 32, 64, width), BF16),
        compiler_params=pltpu.CompilerParams(vmem_limit_bytes=VMEM),
        cost_estimate=cost(8 * half * half * width),
        name="merge_heads",
    )(place, mine.reshape(4, -1, 32, width), others.reshape(4, -1, 32, width))


def block_kernel(
    head_dim, place, own, halo, core, mixed, mod, gains, ones2, weights, carry,
    out, send, rows_in, query, kv, scores, attended, final,
):
    frames, size, width = own.shape
    tiles = width // LANES
    offsets = 2 * WIN + 1
    half = width // 2
    step = pl.program_id(0)
    ones = ones2[...]

    for frame in range(frames):
        rows_in[frame] = halo[frames - 1 - frame]
        rows_in[frames + frame] = own[frame]
        rows_in[2 * frames + frame] = core[frames - 1 - frame]
    reach = 3 * frames * size

    all_rows = rows_in[...].reshape(reach, width)
    edge = width + LANES
    key_value = weights[KEY : VALUE + 1].reshape(2 * width, width)
    keys = dot_rows(all_rows, key_value[0:edge])
    for tile, part in enumerate(head_norm(keys[:, :width], gains[1:2], ones, head_dim)):
        kv[0, :, :, tile * LANES : (tile + 1) * LANES] = part.reshape(3 * frames, size, LANES)
    kv[1, :, :, :LANES] = keys[:, width:].astype(BF16).reshape(3 * frames, size, LANES)
    own_rows = rows_in[frames : 2 * frames].reshape(frames * size, width)
    queries = dot_rows(own_rows, weights[QUERY].reshape(width, width))
    for tile, part in enumerate(head_norm(queries, gains[0:1], ones, head_dim)):
        query[:, :, tile * LANES : (tile + 1) * LANES] = part.reshape(frames, size, LANES)

    def window(kind, frame, rows, cols):
        return kv[kind, frame, rows, cols].astype(F32)

    def score(start, first):
        rows = slice(start, start + 16)
        pair = (first, first + 1)
        sums = {}
        for tile in range(tiles):
            cols = slice(tile * LANES, (tile + 1) * LANES)
            asked = [query[frame, rows, cols].astype(F32) for frame in pair]
            for reached in range(first, first + 1 + offsets):
                key = window(0, reached, rows, cols)
                for frame, one in zip(pair, asked):
                    offset = reached - frame
                    if 0 <= offset < offsets:
                        at = frame * offsets + offset
                        sums[at] = one * key if tile == 0 else sums[at] + one * key
        for at, value in sums.items():
            scores[at, rows] = value

    scale = 1.0 / math.sqrt(head_dim)
    halo_there = place[2] > 0

    def soften(start, frame, sub=32):
        rows = slice(start, start + sub)
        raw = scores[frame * offsets : (frame + 1) * offsets, rows]
        full = split_dot(raw.reshape(offsets * sub, LANES), ones).reshape(
            offsets, sub, LANES
        ) * scale
        parts = [
            jnp.where(halo_there, full[offset], -1e30) if frame + offset < frames else full[offset]
            for offset in range(offsets)
        ]
        highest = functools.reduce(jnp.maximum, parts)
        parts = [jnp.exp(part - highest) for part in parts]
        inverse = 1.0 / functools.reduce(jnp.add, parts)
        for offset, part in enumerate(parts):
            scores[frame * offsets + offset, rows] = (part * inverse).astype(BF16).astype(F32)

    steps = [functools.partial(score, start, first)
             for start in range(0, size, 16) for first in range(0, frames, 2)]
    steps += [functools.partial(soften, start, frame)
              for start in range(0, size, 32) for frame in range(frames)]
    starts = list(range(LANES, width, COLUMNS))
    done = 0
    for at, start in enumerate(starts):
        high = min(start + COLUMNS, width)
        kv[1, :, :, start:high] = dot_rows(
            all_rows, key_value[width + start : width + high]
        ).astype(BF16).reshape(3 * frames, size, high - start)
        until = len(steps) * (at + 1) // len(starts)
        for unit in steps[done:until]:
            unit()
        done = until

    @pl.loop(0, size // 16)
    def _(at):
        rows = pl.ds(pl.multiple_of(at * 16, 16), 16)
        for first in range(0, frames, 2):
            pair = (first, first + 1)
            shares = {
                frame: [scores[frame * offsets + offset, rows] for offset in range(offsets)]
                for frame in pair
            }
            for tile in range(tiles):
                cols = slice(tile * LANES, (tile + 1) * LANES)
                sums = {}
                for reached in range(first, first + 1 + offsets):
                    value = window(1, reached, rows, cols)
                    for frame in pair:
                        offset = reached - frame
                        if 0 <= offset < offsets:
                            term = shares[frame][offset] * value
                            sums[frame] = term if offset == 0 else sums[frame] + term
                for frame in pair:
                    attended[frame, pl.ds(pl.multiple_of(step * size + at * 16, 16), 16), cols] = (
                        sums[frame].astype(BF16)
                    )

    @pl.when(step == pl.num_programs(0) - 1)
    def _():
        places = attended.shape[1]
        own_half = pl.ds(pl.multiple_of(place[0] * half, 64), half)
        send_half = pl.ds(pl.multiple_of((1 - place[0]) * half, 64), half)
        flat = attended[...].reshape(frames * places, width)
        result = jnp.dot(flat, weights[OUT].reshape(width, width), preferred_element_type=F32)
        result = result * mod[2:3, :]
        for frame in range(frames):
            target = frame + place[1] * (3 - 2 * frame)
            for tile in range(tiles):
                cols = slice(tile * LANES, (tile + 1) * LANES)
                turned = result[frame * places : (frame + 1) * places, cols].T
                final[cols] = (mixed[frame, cols].astype(F32) + turned).astype(BF16)
            out[target, 0] = final[own_half]
            send[target] = final[send_half]


def whole_block(place, own, halo, core, mixed, mod, gains, ones2, weights, carry, head_dim,
                chunk, places):
    frames, size, width = own.shape
    half = width // 2
    block = BLOCK
    once = pl.Buffered(1)
    rows = pl.BlockSpec((frames, block, width), lambda p, s: (0, p, 0))
    in_specs = [
        rows, rows, rows,
        pl.BlockSpec((frames, width, size), lambda p, s: (0, 0, 0), pipeline_mode=once),
        pl.BlockSpec((3, width), lambda p, s: (0, 0)),
        pl.BlockSpec((2, width), lambda p, s: (0, 0)),
        pl.BlockSpec((2 * LANES, LANES), lambda p, s: (0, 0)),
    ]
    in_specs.append(pl.BlockSpec(memory_space=pltpu.VMEM))
    weights = pltpu.with_memory_space_constraint(weights, pltpu.VMEM)
    args = [place, own, halo, core, mixed, mod, gains, ones2, weights]
    aliases = {}
    if carry is not None:
        in_specs.append(pl.BlockSpec(memory_space=pl.ANY))
        aliases = {len(args): 0}
        args.append(carry)

    def kernel(*refs):
        block_kernel(head_dim, *refs[:9], None, *refs[9 + len(aliases) :])

    grid_spec = pltpu.PrefetchScalarGridSpec(
        num_scalar_prefetch=1,
        grid=(size // block,),
        in_specs=in_specs,
        out_specs=[
            pl.BlockSpec((frames, 1, half, size), lambda p, s: (0, s[0], 0, chunk)),
            pl.BlockSpec((frames, half, size), lambda p, s: (0, 0, 0)),
        ],
        scratch_shapes=[
            pltpu.VMEM((3 * frames, block, width), BF16),
            pltpu.VMEM((frames, block, width), BF16),
            pltpu.VMEM((2, 3 * frames, block, width), BF16),
            pltpu.VMEM((frames * (2 * WIN + 1), block, LANES), F32),
            pltpu.VMEM((frames, size, width), BF16),
            pltpu.VMEM((width, size), BF16),
        ],
    )
    return pl.pallas_call(
        kernel,
        grid_spec=grid_spec,
        out_shape=[
            jax.ShapeDtypeStruct((frames, 2, half, places), BF16),
            jax.ShapeDtypeStruct((frames, half, size), BF16),
        ],
        input_output_aliases=aliases,
        compiler_params=pltpu.CompilerParams(vmem_limit_bytes=VMEM),
        cost_estimate=cost(36 * frames * size * width * width),
        name="whole_block",
    )(*args)


def on_device(
    mesh_sizes, hidden, keypoints, tsteps, mod_table, ctrl_table, ctrl_proj, w_qkv, q_gain, k_gain,
    w_out,
):
    queue_size, head_size = mesh_sizes
    frames, _, places, half = hidden.shape
    width = 2 * half
    heads, head_dim = q_gain.shape
    classes = ctrl_table.shape[0]
    size = places // CHUNKS
    head = lax.axis_index("head")
    queue = lax.axis_index("queue")
    core = queue % 2
    swap = [(0, 1), (1, 0)]
    across = [
        (2 * q + h, 2 * ((q + queue_size // 2) % queue_size) + 1 - h)
        for q in range(queue_size)
        for h in range(2)
    ]
    cores = [(q, q ^ 1) for q in range(queue_size)]
    halos = [(q, q + 1) for q in range(1, queue_size - 1, 2)]
    halos += [(b, a) for a, b in halos]

    halo_there = ((queue > 0) & (queue < queue_size - 1)).astype(jnp.int32)
    place = jnp.stack([head, core, halo_there, queue // 8 % 4]).astype(jnp.int32)
    hidden = hidden.transpose(0, 1, 3, 2)
    w_qkv = w_qkv.transpose(1, 2, 0)

    def after(value, *others):
        return lax.optimization_barrier((value, others))[0]

    source = jnp.arange(half)
    mover = (
        source[None, :] == ((source % heads) * head_dim + source // heads)[:, None]
    ).astype(BF16)
    piece = piece_of_heads(place, w_qkv, w_out, mover)
    eighth = lax.ppermute(piece, ("queue", "head"), across)
    sharers = [
        [((top * 4 + x) * 4 + y) * 2 + c for x in range(4) for c in range(2)]
        for top in range(queue_size // 32)
        for y in range(4)
    ]

    def cut(source, chunk):
        return lax.dynamic_slice(
            source, (0, 1 - head, 0, chunk * size), (frames, 1, half, size)
        ).reshape(frames, half, size)

    part = cut(after(hidden, piece), 0)
    arrived = [lax.ppermute(part, "head", swap)]
    w_qkv, w_out = after((w_qkv, w_out), part)
    mine = order_heads(w_qkv, w_out, mover)
    later = after(hidden, mine)
    arrived.append(lax.ppermute(cut(later, 1), "head", swap))
    for part in after([cut(later, chunk) for chunk in range(2, CHUNKS)], arrived[0]):
        arrived.append(lax.ppermute(part, "head", swap))

    control = jnp.dot(ctrl_table, ctrl_proj, preferred_element_type=F32)
    small = jnp.concatenate(
        [control, q_gain.T.reshape(1, half), k_gain.T.reshape(1, half)], 0
    )
    small_other = lax.ppermute(small, "head", swap)
    both = jnp.stack([small, small_other])
    gains = both[:, classes:].reshape(2, 2, half // 32, 32).transpose(1, 2, 0, 3).reshape(2, width)
    natural = jnp.where(head == 0, both, both[::-1])[:, :classes]
    natural = natural.transpose(0, 2, 1).reshape(width, classes)
    table = class_table(after(jnp.pad(natural, ((0, 0), (0, 32 - classes))), mine))
    eighth = after(eighth, arrived[0], table)
    others = lax.all_gather(eighth, "queue", axis=0, tiled=True, axis_index_groups=sharers)
    mod = lax.dynamic_index_in_dim(mod_table, tsteps[0], 0, keepdims=False)
    lane = jnp.arange(LANES)
    row = jnp.arange(2 * LANES)
    ones2 = (
        ((row // 32 % 2)[:, None] == (lane // 32 % 2)[None, :])
        & ((row % 8)[:, None] == (lane % 8)[None, :])
    ).astype(BF16)

    normed, mixed, halo, beside = [], [], [], []

    def prepare(chunk, other):
        one, two = adaptive_norm(place, hidden, other, keypoints, table, mod, chunk)
        normed.append(one)
        mixed.append(two)
        halo.append(lax.ppermute(one, "queue", halos))
        beside.append(lax.ppermute(one, "queue", cores))

    ahead = 2
    prepare(0, arrived[0])
    prepare(1, arrived[1])
    others, mine = after((others, mine), normed[1])
    weights = merge_heads(place, mine, others)
    carry = None
    back = []
    for chunk in range(CHUNKS):
        carry, send = whole_block(
            place, normed[chunk], halo[chunk], beside[chunk], mixed[chunk], mod, gains, ones2, weights,
            carry, head_dim, chunk, places,
        )
        if chunk + ahead < CHUNKS:
            other, send = lax.optimization_barrier((arrived[chunk + ahead], send))
            prepare(chunk + ahead, other)
        back.append(lax.ppermute(send, "head", swap))
    for chunk in range(CHUNKS):
        carry = lax.dynamic_update_slice(
            carry, back[chunk][:, None], (0, 1 - head, 0, chunk * size)
        )
    return carry.transpose(0, 1, 3, 2)


def solution(mesh):
    placed = (
        P("queue", None, None, "head"),
        P("queue", None),
        P("queue"),
        P(),
        P(),
        P(None, "head"),
        P(None, None, "head"),
        P("head", None),
        P("head", None),
        P("head", None),
    )
    return jax.shard_map(
        functools.partial(on_device, (mesh.shape["queue"], mesh.shape["head"])),
        mesh=mesh,
        in_specs=placed,
        out_specs=P("queue", None, None, "head"),
        check_vma=False,
    )
```
